512 devices in a mesh: band: 32 (over z, x_lo), dom: 16 (over x_hi, y, core).
Axes of the slice: x: 4 (x_hi: 2, x_lo: 2; x = x_hi * 2 + x_lo), y: 4, z: 16, core: 2. Of those that a mesh axis runs over, the one named last changes fastest.
Arguments:
- targets: bfloat16 [1024, 262144], P('band', 'dom'), as said below
- sources: bfloat16 [2, 128, 262144], P(None, 'band', 'dom'), as said below
- pair_tgt: int32 [2, 64], P(None, 'band'), may hold values from 0 to 31
- pair_src: int32 [2, 64], replicated, may hold values from 0 to 127, as said below
Outputs:
- target_exchange: bfloat16 [1024, 262144], P('band', 'dom')
- source_exchange: bfloat16 [2, 128, 262144], P(None, 'band', 'dom')
The draws below stay inside these ranges and needn't reach their ends.
Inputs may be any that keep to these rules, and one draw needn't show every extreme that they name: `pair_src`: for each block, the 2 entries of one band group (entries g * 2 to g * 2 + 1) are distinct. `targets`: orbital values of order one. `sources`: orbital values of order one.
All inputs are finite; a program needn't handle non-finite values.
Results may differ from the reference program's by a relative error of at most 0.0039.
Values may be sent and summed in bfloat16 or wider, within the bound.
No kernel may reach another device: no remote copies, remote signals or barrier semaphores. Data moves between devices by JAX's collectives and lax.ppermute only.
A program may use at most 128 MiB of HBM per device.

```python
import math
import jax
import jax.numpy as jnp
from jax import lax

NY = 64
NZ = 64
SRC = 128
ORB_DEV = 32
PAIRS = 2
NBLK = 2
SWEEPS = 8
CELLS = 262144
NORB = 1024
NPAIR = 64


def grid_axes():
    planes_total = CELLS // (NY * NZ)
    along_x = (jnp.arange(planes_total, dtype=jnp.float32) + 0.5) / planes_total
    along_y = (jnp.arange(NY, dtype=jnp.float32) + 0.5) / NY
    along_z = (jnp.arange(NZ, dtype=jnp.float32) + 0.5) / NZ
    return (along_x, along_y, along_z)


def smooth_waves(key, row_count):
    along_x, along_y, along_z = grid_axes()
    summed = jnp.zeros((row_count, along_x.shape[0], NY, NZ), jnp.float32)
    for wave_index in range(2):
        wave_key = jax.random.fold_in(key, 100 + wave_index)
        cycle_key, phase_key = jax.random.split(wave_key)
        cycles = jax.random.randint(cycle_key, (row_count, 3), 1, 3).astype(jnp.float32)
        phases = jax.random.uniform(phase_key, (row_count, 3), jnp.float32, -math.pi, math.pi)
        factor_x = jnp.cos(2.0 * math.pi * cycles[:, 0:1] * along_x[None, :] + phases[:, 0:1])
        factor_y = jnp.cos(2.0 * math.pi * cycles[:, 1:2] * along_y[None, :] + phases[:, 1:2])
        factor_z = jnp.cos(2.0 * math.pi * cycles[:, 2:3] * along_z[None, :] + phases[:, 2:3])
        summed = summed + factor_x[:, :, None, None] * factor_y[:, None, :, None] * factor_z[:, None, None, :]
    return 0.7 * summed.reshape(row_count, CELLS)


def mixed_rows(key, row_count, rough):
    smooth_key, amp_key, rough_key = jax.random.split(key, 3)
    smooth_amp = jnp.exp(jax.random.uniform(amp_key, (row_count, 1), jnp.float32, math.log(0.1), math.log(1.5)))
    rough_amp = jax.random.uniform(rough_key, (row_count, 1), jnp.float32, 0.25, 1.0)
    return smooth_amp * smooth_waves(smooth_key, row_count) + rough_amp * rough


def draw_targets(key, part):
    key = jax.random.fold_in(key, 11)
    noise_key, mix_key = jax.random.split(key, 2)
    cell_index = jnp.arange(CELLS, dtype=jnp.int32)
    plane_index = (cell_index // (NY * NZ)).astype(jnp.float32)
    envelope = 0.6 + plane_index / (CELLS // (NY * NZ))
    rough = jax.random.normal(noise_key, (NORB, CELLS), jnp.float32)
    values = mixed_rows(mix_key, NORB, rough)
    values = values * envelope[None, :]
    return jnp.clip(values, -6.0, 6.0).astype(jnp.bfloat16)


def draw_sources(key, part):
    key = jax.random.fold_in(key, 13)
    noise_key, mix_key = jax.random.split(key, 2)
    row_count = NBLK * SRC
    rough = jax.random.normal(noise_key, (row_count, CELLS), jnp.float32)
    values = mixed_rows(mix_key, row_count, rough)
    values = jnp.clip(values, -6.0, 6.0)
    return values.reshape(NBLK, SRC, CELLS).astype(jnp.bfloat16)


def choose_sources(row_key):
    return jax.random.permutation(row_key, SRC)[:PAIRS]


def draw_pair_src(key, part):
    key = jax.random.fold_in(key, 17)
    groups = NBLK * (NPAIR // PAIRS)
    row_keys = jax.random.split(key, groups)
    chosen = jax.vmap(choose_sources)(row_keys)
    return chosen.reshape(NBLK, NPAIR).astype(jnp.int32)


def with_ends(entries, stream_key, least, largest):
    longest = entries.shape.index(max(entries.shape))
    spots = []
    for shift in (0, 1):
        where = [jax.random.randint(jax.random.fold_in(stream_key, axis), (), 0, length) for axis, length in enumerate(entries.shape)]
        where[longest] = (where[longest] + shift) % entries.shape[longest]
        spots.append(tuple(where))
    return entries.at[spots[0]].set(least).at[spots[1]].set(largest)


def setup_inputs(seed: int = 0) -> dict:
    key_of = jax.random.split(jax.random.key(seed), 5)
    return {
        "targets": draw_targets(jax.random.fold_in(key_of[4], 71), 0),
        "sources": draw_sources(jax.random.fold_in(key_of[4], 71), 0),
        "pair_tgt": with_ends(jax.random.randint(key_of[2], (NBLK, NPAIR), 0, ORB_DEV), jax.random.fold_in(key_of[2], 1), 0, ORB_DEV - 1).astype(jnp.int32),
        "pair_src": draw_pair_src(jax.random.fold_in(key_of[4], 71), 0),
    }


def apply_operator(padded, field):
    count, planes, depth, length = field.shape

    def offset_view(axis, delta):
        starts = [0, 2, 2, 2]
        starts[axis] = 2 + delta
        return lax.slice(padded, (0, starts[1], starts[2], starts[3]), (count, starts[1] + planes, starts[2] + depth, starts[3] + length))

    total = 90.0 * field
    for axis in (1, 2, 3):
        total = total - 16.0 * (offset_view(axis, 1) + offset_view(axis, -1)) + (offset_view(axis, 2) + offset_view(axis, -2))
    return total / 12.0


def operate(field):
    padded = jnp.pad(field, ((0, 0), (2, 2), (2, 2), (2, 2)))
    return apply_operator(padded, field)


def expand(vector):
    return vector[:, None, None, None]


def local_dot(left, right):
    return jnp.sum(left * right, axis=(1, 2, 3))


def solve(density):
    solution = jnp.zeros_like(density)
    residual = density
    direction = density
    norm_now = local_dot(residual, residual)
    for sweep in range(SWEEPS):
        applied = operate(direction)
        step_size = norm_now / local_dot(direction, applied)
        solution = solution + expand(step_size) * direction
        residual = residual - expand(step_size) * applied
        norm_next = local_dot(residual, residual)
        direction = residual + expand(norm_next / norm_now) * direction
        norm_now = norm_next
    return solution


def reference(targets, sources, pair_tgt, pair_src):
    grid_x = CELLS // (NY * NZ)
    target_sum = jnp.zeros((NORB, CELLS), jnp.float32)
    source_outs = []
    for block in range(NBLK):
        block_sources = sources[block]
        tgt_row = pair_tgt[block]
        src_row = pair_src[block]

        def group_step(carry, group):
            target_acc, source_acc = carry
            start = (group * PAIRS).astype(jnp.int32)
            target_ids = group * ORB_DEV + lax.dynamic_slice(tgt_row, (start,), (PAIRS,))
            source_ids = lax.dynamic_slice(src_row, (start,), (PAIRS,))
            target_vals = targets[target_ids].astype(jnp.float32)
            source_vals = block_sources[source_ids].astype(jnp.float32)
            density = (target_vals * source_vals).reshape(PAIRS, grid_x, NY, NZ)
            potential = solve(density).reshape(PAIRS, CELLS)
            target_acc = target_acc.at[target_ids].add(-potential * source_vals)
            group_term = lax.optimization_barrier((-potential * target_vals).astype(jnp.bfloat16))
            source_acc = source_acc.at[source_ids].add(group_term.astype(jnp.float32))
            return (target_acc, source_acc), None

        start_acc = jnp.zeros((SRC, CELLS), jnp.float32)
        groups = jnp.arange(NPAIR // PAIRS, dtype=jnp.int32)
        (target_sum, source_acc), unused = lax.scan(group_step, (target_sum, start_acc), groups)
        source_outs.append(source_acc.astype(jnp.bfloat16))
    return target_sum.astype(jnp.bfloat16), jnp.stack(source_outs)
```

```python
import numpy as np
import jax
import jax.numpy as jnp
from jax import lax
from jax.experimental import pallas as pl
from jax.experimental.pallas import tpu as pltpu
from jax.sharding import PartitionSpec as P

SIDE = 64
SWEEPS = 8
RING = 16
ROW = 128
HALF = 64
VMEM_LIMIT = 48 * 1024 * 1024
F32 = jnp.float32
BF16 = jnp.bfloat16


def eigen_system():
    line = np.zeros((SIDE, SIDE))
    for delta, weight in ((0, 30.0), (1, -16.0), (2, 1.0)):
        for i in range(SIDE - delta):
            line[i, i + delta] = weight / 12.0
            line[i + delta, i] = weight / 12.0
    values, vectors = np.linalg.eigh(line)
    return values, vectors * np.where(vectors[0] < 0, -1.0, 1.0)[None, :]


def halves(matrix):
    high = np.asarray(matrix, np.float32).astype(jnp.bfloat16)
    low = (np.asarray(matrix, np.float64) - high.astype(np.float64)).astype(jnp.bfloat16)
    return np.stack([high, low])


def tables():
    values, v = eigen_system()
    along_z = np.kron(np.eye(2), v)
    even, odd = v[0::2], v[1::2]
    fwd = np.zeros((2, 32, 4, 2, 4, 32))
    bwd = np.zeros((2, 4, 32, 2, 32, 4))
    for x in range(4):
        fwd[0, :, x, 0, x, :] = even[:, 0::2].T
        fwd[0, :, x, 1, x, :] = odd[:, 0::2].T
        fwd[1, :, x, 0, x, :] = odd[:, 1::2].T
        fwd[1, :, x, 1, x, :] = even[:, 1::2].T
        bwd[0, x, :, 0, :, x] = even[:, 0::2]
        bwd[0, x, :, 1, :, x] = even[:, 1::2]
        bwd[1, x, :, 0, :, x] = odd[:, 1::2]
        bwd[1, x, :, 1, :, x] = odd[:, 0::2]
    along_x = np.zeros((2, SIDE, RING, 2, 4))
    for pick in range(2):
        along_x[pick, :, :, pick, :] = v.T.reshape(SIDE, RING, 4)
    rows = np.arange(SIDE).reshape(RING, 2, 1, 2, 1)
    spectrum = values[rows] + values.reshape(1, 1, SIDE, 1, 1) + values.reshape(1, 1, 1, 1, SIDE)
    return dict(
        z_fwd=halves(along_z),
        z_bwd=halves(along_z.T),
        y_fwd=halves(fwd.reshape(256, 256)),
        y_bwd=halves(bwd.reshape(256, 256)),
        x_fwd=halves(along_x.reshape(ROW, ROW)),
        x_bwd=halves(along_x.reshape(ROW, ROW).T),
        spectrum=spectrum.reshape(RING, ROW, ROW).astype(np.float32),
    )


def split(value):
    high = value.astype(BF16)
    return high, (value - high.astype(F32)).astype(BF16)


def mm(left, right):
    return jnp.dot(left, right, preferred_element_type=F32)


def left_mul(table, value):
    high, low = split(value)
    return mm(table[0], high) + mm(table[0], low) + mm(table[1], high)


def right_mul(value, table):
    high, low = split(value)
    return mm(high, table[0]) + mm(low, table[0]) + mm(high, table[1])


def mix_rows(table, value):
    swapped = jnp.concatenate([value[:, HALF:], value[:, :HALF]], axis=1)
    both = left_mul(table, jnp.concatenate([value, swapped], axis=0))
    lane = lax.broadcasted_iota(jnp.int32, (ROW, ROW), 1)
    return jnp.where(lane < HALF, both[:ROW], both[ROW:])


def vmem_call(kernel, outs, operands, scalars=0, scratch=()):
    whole = pl.BlockSpec(memory_space=pltpu.VMEM)
    smem = pl.BlockSpec(memory_space=pltpu.SMEM)
    return pl.pallas_call(
        kernel,
        out_shape=outs,
        in_specs=[smem] * scalars + [whole] * (len(operands) - scalars),
        out_specs=[whole] * len(outs),
        scratch_shapes=list(scratch),
        compiler_params=pltpu.CompilerParams(vmem_limit_bytes=VMEM_LIMIT),
    )(*operands)


def struct(shape, dtype):
    return jax.ShapeDtypeStruct(shape, dtype)


def owner_of(source):
    owner = lax.shift_right_logical(source, 2)
    return lax.shift_right_logical(owner, 1), lax.bitwise_and(owner, 1), lax.bitwise_and(source, 3)


def ring(value):
    return lax.bitwise_and(value, RING - 1)


def pick_kernel(place, pair_src, near0, near1, near2, near3, *outs):
    z, x, core = place[0], place[1], place[2]
    held = (
        (near0, 0),
        (near1, 1),
        (near2, RING - 1),
        (near3, jnp.where(core == 0, 2, RING - 2)),
    )
    for out, offset in zip(outs, (0, 4, -4, 8)):
        band = 2 * ring(z + offset) + x
        for slot in range(4):
            block, k = slot // 2, slot % 2
            z_own, x_own, row = owner_of(pair_src[block, 2 * band + k])
            index = 8 * lax.bitwise_xor(x_own, x) + 4 * block + row
            behind = ring(z - z_own)
            out[slot] = jnp.zeros((ROW, ROW), BF16)
            for rows, delta in held:

                @pl.when(behind == delta)
                def _():
                    out[slot] = rows[index]


def density_kernel(r0, r1, r2, r3, wanted, z_fwd, y_fwd, source_rows, spectra):
    for p in range(4):
        row = r0[p].astype(F32) + r1[p].astype(F32) + r2[p].astype(F32) + r3[p].astype(F32)
        source_rows[p] = row.astype(BF16)
        density = row * wanted[p].astype(F32)
        mixed = mix_rows(y_fwd, right_mul(density, z_fwd)).astype(spectra.dtype)
        for copy in range(4):
            spectra[4 * copy + p] = mixed


def solve_kernel(quarter, slabs, spectrum, x_fwd, x_bwd, out, residual, direction, total):
    def dot_of(value):
        return jnp.sum(value.reshape(RING, 8, ROW), axis=0)

    zero = jnp.zeros((8, ROW), F32)

    def start(j, carry):
        norm, power = carry
        rows = pl.ds(pl.multiple_of(8 * j, 8), 8)
        part = slabs[:, rows, :].astype(F32).reshape(ROW, ROW)
        value = left_mul(x_fwd, part)
        residual[j] = value
        direction[j] = value
        total[j] = jnp.zeros((ROW, ROW), F32)
        square = value * value
        return norm + dot_of(square), power + dot_of(square * spectrum[j])

    norm, power = lax.fori_loop(0, RING, start, (zero, zero))
    norm, power = jnp.sum(norm), jnp.sum(power)
    for sweep in range(SWEEPS):
        step = norm / power

        def advance(j, acc):
            d = direction[j]
            r = residual[j] - step * (spectrum[j] * d)
            total[j] = total[j] + step * d
            residual[j] = r
            return acc + dot_of(r * r)

        new = jnp.sum(lax.fori_loop(0, RING, advance, zero))
        if sweep < SWEEPS - 1:
            ratio = new / norm

            def turn(j, acc):
                d = residual[j] + ratio * direction[j]
                direction[j] = d
                return acc + dot_of(d * (spectrum[j] * d))

            power = jnp.sum(lax.fori_loop(0, RING, turn, zero))
            norm = new
    for jj in range(4):
        part = left_mul(x_bwd, total[4 * quarter[0] + jj])
        out[:, 8 * jj : 8 * jj + 8, :] = part.reshape(RING, 8, ROW).astype(out.dtype)


def term_kernel(pair_tgt, spectra, source_rows, wanted, z_bwd, y_bwd, target_rows, terms, held):
    for p in range(4):
        rows = jnp.concatenate([spectra[4 * q + p].astype(F32) for q in range(4)], axis=0)
        potential = right_mul(mix_rows(y_bwd, rows), z_bwd)
        terms[p] = (-potential * wanted[p].astype(F32)).astype(BF16)
        held[p] = -potential * source_rows[p].astype(F32)
    for p in range(4):
        same = jnp.zeros((ROW, ROW), F32)
        for other in range(4):
            hit = pair_tgt[p // 2, p % 2] == pair_tgt[other // 2, other % 2]
            same = same + jnp.where(hit, held[other], 0.0)
        target_rows[p] = same.astype(BF16)


def owner_kernel(place, pair_src, near0, near1, near2, near3, mine, partner, total):
    z, x, core = place[0], place[1], place[2]
    total[...] = jnp.zeros((16, ROW, ROW), F32)
    centres = (z, z - 1, z + 1, jnp.where(core == 0, z - 2, z + 2))
    for rows, centre in zip((near0, near1, near2, near3), centres):
        for m, offset in enumerate((0, -4, 4, 8)):
            band = 2 * ring(centre + offset) + x
            for slot in range(4):
                z_own, x_own, row = owner_of(pair_src[slot // 2, 2 * band + slot % 2])

                @pl.when(z_own == z)
                def _():
                    index = 8 * lax.bitwise_xor(x_own, x) + 4 * (slot // 2) + row
                    total[index] = total[index] + rows[4 * m + slot].astype(F32)

    mine[...] = total[0:8]
    partner[...] = total[8:16].astype(BF16)


AXES = ("band", "dom")


def shift(value, steps, mirror=False):
    pairs = []
    for z in range(RING):
        for x in range(2):
            for dom in range(16):
                go = -steps if mirror and dom % 2 else steps
                there = 2 * ((z + go) % RING) + x
                pairs.append(((2 * z + x) * 16 + dom, there * 16 + dom))
    return lax.ppermute(value, AXES, pairs)


def across(value):
    return lax.ppermute(value, "band", [(i, i ^ 1) for i in range(32)])


def neighbours(value):
    return value, shift(value, 1), shift(value, -1), shift(value, 2, True)


def per_device(targets, sources, pair_tgt, pair_src):
    table = {name: jnp.asarray(value) for name, value in tables().items()}
    band, dom = lax.axis_index("band"), lax.axis_index("dom")
    place = jnp.stack([band // 2, band % 2, dom % 2]).astype(jnp.int32)
    quarter = (dom // 4).astype(jnp.int32).reshape(1)

    own = sources.reshape(8, ROW, ROW)
    rows = jnp.concatenate([own, across(own)], axis=0)
    near = neighbours(rows)
    four = struct((4, ROW, ROW), BF16)
    picked = vmem_call(pick_kernel, [four] * 4, (place, pair_src) + near, scalars=2)
    reached = (picked[0], shift(picked[1], 4), shift(picked[2], -4), shift(picked[3], 8))

    ids = pair_tgt.reshape(4)
    wanted = targets[ids].reshape(4, ROW, ROW)
    source_rows, spectra = vmem_call(
        density_kernel,
        [four, struct((16, ROW, ROW), BF16)],
        reached + (wanted, table["z_fwd"], table["y_fwd"]),
    )
    slabs = lax.all_to_all(spectra, "dom", 0, 0, tiled=True)
    state = pltpu.VMEM((RING, ROW, ROW), F32)
    (solved,) = vmem_call(
        solve_kernel,
        [struct((16, 32, ROW), F32)],
        (quarter, slabs, table["spectrum"], table["x_fwd"], table["x_bwd"]),
        scalars=1,
        scratch=(state, state, state),
    )
    back = lax.all_to_all(solved, "dom", 0, 0, tiled=True)
    target_rows, terms = vmem_call(
        term_kernel,
        [four, four],
        (pair_tgt, back, source_rows, wanted, table["z_bwd"], table["y_bwd"]),
        scalars=1,
        scratch=(pltpu.VMEM((4, ROW, ROW), F32),),
    )

    gathered = jnp.concatenate([terms, shift(terms, 4), shift(terms, -4), shift(terms, 8)], axis=0)
    near = neighbours(gathered)
    mine, partner = vmem_call(
        owner_kernel,
        [struct((8, ROW, ROW), F32), struct((8, ROW, ROW), BF16)],
        (place, pair_src) + near,
        scalars=2,
        scratch=(pltpu.VMEM((16, ROW, ROW), F32),),
    )
    owned = (mine + across(partner).astype(F32)).astype(BF16).reshape(sources.shape)

    flat = target_rows.reshape(4, targets.shape[1])
    slots = jnp.arange(targets.shape[0], dtype=jnp.int32)[:, None]
    summed = jnp.zeros(targets.shape, BF16)
    for p in range(4):
        summed = jnp.where(slots == ids[p], flat[p][None, :], summed)
    return summed, owned


def solution(mesh):
    return jax.shard_map(
        per_device,
        mesh=mesh,
        in_specs=(P("band", "dom"), P(None, "band", "dom"), P(None, "band"), P()),
        out_specs=(P("band", "dom"), P(None, "band", "dom")),
        check_vma=False,
    )
```

```python
import numpy as np
import jax
import jax.numpy as jnp
from jax import lax
from jax.experimental import pallas as pl
from jax.experimental.pallas import tpu as pltpu
from jax.sharding import PartitionSpec as P

SIDE = 64
SWEEPS = 8
RING = 16
CAP = 6
ROW = 128
HALF = 64
VMEM_LIMIT = 48 * 1024 * 1024
F32 = jnp.float32
BF16 = jnp.bfloat16


def eigen_system():
    line = np.zeros((SIDE, SIDE))
    for delta, weight in ((0, 30.0), (1, -16.0), (2, 1.0)):
        for i in range(SIDE - delta):
            line[i, i + delta] = weight / 12.0
            line[i + delta, i] = weight / 12.0
    values, vectors = np.linalg.eigh(line)
    return values, vectors * np.where(vectors[0] < 0, -1.0, 1.0)[None, :]


def halves(matrix):
    high = np.asarray(matrix, np.float32).astype(jnp.bfloat16)
    low = (np.asarray(matrix, np.float64) - high.astype(np.float64)).astype(jnp.bfloat16)
    return np.stack([high, low])


def tables():
    values, v = eigen_system()
    along_z = np.kron(np.eye(2), v)
    even, odd = v[0::2], v[1::2]
    fwd = np.zeros((2, 32, 4, 2, 4, 32))
    bwd = np.zeros((2, 4, 32, 2, 32, 4))
    for x in range(4):
        fwd[0, :, x, 0, x, :] = even[:, 0::2].T
        fwd[0, :, x, 1, x, :] = odd[:, 0::2].T
        fwd[1, :, x, 0, x, :] = odd[:, 1::2].T
        fwd[1, :, x, 1, x, :] = even[:, 1::2].T
        bwd[0, x, :, 0, :, x] = even[:, 0::2]
        bwd[0, x, :, 1, :, x] = even[:, 1::2]
        bwd[1, x, :, 0, :, x] = odd[:, 1::2]
        bwd[1, x, :, 1, :, x] = odd[:, 0::2]
    along_x = np.zeros((2, SIDE, RING, 2, 4))
    for pick in range(2):
        along_x[pick, :, :, pick, :] = v.T.reshape(SIDE, RING, 4)
    rows = np.arange(SIDE).reshape(RING, 2, 1, 2, 1)
    spectrum = values[rows] + values.reshape(1, 1, SIDE, 1, 1) + values.reshape(1, 1, 1, 1, SIDE)
    return dict(
        z_fwd=halves(along_z),
        z_bwd=halves(along_z.T),
        y_fwd=halves(fwd.reshape(256, 256)),
        y_bwd=halves(bwd.reshape(256, 256)),
        x_fwd=halves(along_x.reshape(ROW, ROW)),
        x_bwd=halves(along_x.reshape(ROW, ROW).T),
        spectrum=spectrum.reshape(RING, ROW, ROW).astype(np.float32),
    )


def split(value):
    high = value.astype(BF16)
    return high, (value - high.astype(F32)).astype(BF16)


def mm(left, right):
    return jnp.dot(left, right, preferred_element_type=F32)


def left_mul(table, value):
    high, low = split(value)
    return mm(table[0], high) + mm(table[0], low) + mm(table[1], high)


def right_mul(value, table):
    high, low = split(value)
    return mm(high, table[0]) + mm(low, table[0]) + mm(high, table[1])


def mix_rows(table, value):
    swapped = jnp.concatenate([value[:, HALF:], value[:, :HALF]], axis=1)
    both = left_mul(table, jnp.concatenate([value, swapped], axis=0))
    lane = lax.broadcasted_iota(jnp.int32, (ROW, ROW), 1)
    return jnp.where(lane < HALF, both[:ROW], both[ROW:])


def vmem_call(kernel, outs, operands, scalars=0, scratch=(), alias=None):
    whole = pl.BlockSpec(memory_space=pltpu.VMEM)
    smem = pl.BlockSpec(memory_space=pltpu.SMEM)
    return pl.pallas_call(
        kernel,
        out_shape=outs,
        in_specs=[smem] * scalars + [whole] * (len(operands) - scalars),
        out_specs=[whole] * len(outs),
        scratch_shapes=list(scratch),
        input_output_aliases=alias or {},
        compiler_params=pltpu.CompilerParams(vmem_limit_bytes=VMEM_LIMIT),
    )(*operands)


def struct(shape, dtype):
    return jax.ShapeDtypeStruct(shape, dtype)


def owner_of(source):
    owner = lax.shift_right_logical(source, 2)
    return lax.shift_right_logical(owner, 1), lax.bitwise_and(owner, 1), lax.bitwise_and(source, 3)


def ring(value):
    return lax.bitwise_and(value, RING - 1)


def each_want(pair_src, residue, x):
    for turn in range(4):
        band = 2 * (4 * turn + residue) + x
        for slot in range(4):
            block, k = slot // 2, slot % 2
            z_own, x_own, row = owner_of(pair_src[block, 2 * band + k])
            yield 4 * turn + slot, z_own, lax.bitwise_xor(x_own, x), 4 * block + row


def steps_of(core):
    return 1, -1, jnp.where(core == 0, 2, -2)


def pack_wanted_kernel(place, pair_src, own, other, *outs):
    z, x, core, first = place[0], place[1], place[2], place[3]
    for out, step in zip(outs, steps_of(core)):
        count = -first
        for _, z_own, side, row in each_want(pair_src, lax.bitwise_and(z + step, 3), x):
            mine = z_own == z
            fits = jnp.logical_and(mine, jnp.logical_and(count >= 0, count < CAP))
            for rows, where in ((own, 0), (other, 1)):

                @pl.when(jnp.logical_and(fits, side == where))
                def _():
                    out[count] = rows[row]

            count = count + mine.astype(jnp.int32)


def place_wanted_kernel(place, pair_src, own, other, near1, near2, near3, before, out):
    z, x, core, first = place[0], place[1], place[2], place[3]
    del before
    steps = steps_of(core)
    counts = [-first] * 3
    for index, z_own, side, row in each_want(pair_src, lax.bitwise_and(z, 3), x):
        for rows, where in ((own, 0), (other, 1)):

            @pl.when(jnp.logical_and(z_own == z, side == where))
            def _():
                out[index] = rows[row]

        for n, rows in enumerate((near1, near2, near3)):
            theirs = z_own == ring(z - steps[n])
            count = counts[n]

            @pl.when(jnp.logical_and(theirs, jnp.logical_and(count >= 0, count < CAP)))
            def _():
                out[index] = rows[count]

            counts[n] = count + theirs.astype(jnp.int32)


def density_kernel(reached, wanted, z_fwd, y_fwd, source_rows, spectra):
    for p in range(4):
        row = reached[p].astype(F32)
        for turn in range(1, 4):
            row = row + reached[4 * turn + p].astype(F32)
        source_rows[p] = row.astype(BF16)
        density = row * wanted[p].astype(F32)
        mixed = mix_rows(y_fwd, right_mul(density, z_fwd)).astype(spectra.dtype)
        for copy in range(4):
            spectra[4 * copy + p] = mixed


def solve_kernel(quarter, slabs, spectrum, x_fwd, x_bwd, out, first, residual, direction):
    def dot_of(value):
        return jnp.sum(value.reshape(RING, 8, ROW), axis=0)

    zero = jnp.zeros((8, ROW), F32)

    def start(j, carry):
        norm, power = carry
        part = slabs[:, pl.ds(pl.multiple_of(8 * j, 8), 8), :].reshape(ROW, ROW)
        value = mm(x_fwd[0], part) + mm(x_fwd[1], part)
        first[j] = value
        square = value * value
        return norm + dot_of(square), power + dot_of(square * spectrum[j])

    norm, power = lax.fori_loop(0, RING, start, (zero, zero), unroll=2)
    norm, power = jnp.sum(norm), jnp.sum(power)
    steps, ratios = [norm / power], [jnp.float32(0.0)]
    for sweep in range(SWEEPS - 1):
        step, ratio = steps[-1], ratios[-1]

        def advance(j, carry, sweep=sweep, step=step, ratio=ratio):
            new, power = carry
            lam = spectrum[j]
            if sweep == 0:
                d = first[j]
                r = d - step * (lam * d)
            else:
                d = residual[j] + ratio * (first[j] if sweep == 1 else direction[j])
                r = residual[j] - step * (lam * d)
            if sweep > 0:
                direction[j] = d
            residual[j] = r
            square = r * r
            return new + dot_of(square), power + dot_of(square * lam)

        new, power = lax.fori_loop(0, RING, advance, (zero, zero), unroll=2)
        new, power = jnp.sum(new), jnp.sum(power)
        ratio = new / norm
        steps.append(new / (power - ratio * new / step))
        ratios.append(ratio)
        norm = new

    for jj in range(4):
        j = 4 * quarter[0] + jj
        lam, r = spectrum[j], first[j]
        d, total = r, steps[0] * r
        for sweep in range(1, SWEEPS):
            r = r - steps[sweep - 1] * (lam * d)
            d = r + ratios[sweep] * d
            total = total + steps[sweep] * d
        part = left_mul(x_bwd, total)
        out[:, 8 * jj : 8 * jj + 8, :] = part.reshape(RING, 8, ROW).astype(out.dtype)


def term_kernel(pair_tgt, spectra, source_rows, wanted, z_bwd, y_bwd, target_rows, terms, held):
    for p in range(4):
        rows = jnp.concatenate([spectra[4 * q + p].astype(F32) for q in range(4)], axis=0)
        potential = right_mul(mix_rows(y_bwd, rows), z_bwd)
        term = (-potential * wanted[p].astype(F32)).astype(BF16)
        for turn in range(4):
            terms[4 * turn + p] = term
        held[p] = -potential * source_rows[p].astype(F32)
    for p in range(4):
        same = jnp.zeros((ROW, ROW), F32)
        for other in range(4):
            hit = pair_tgt[p // 2, p % 2] == pair_tgt[other // 2, other % 2]
            same = same + jnp.where(hit, held[other], 0.0)
        target_rows[p] = same.astype(BF16)


def pack_terms_kernel(place, pair_src, terms, *outs):
    z, x, core, first = place[0], place[1], place[2], place[3]
    for out, step in zip(outs, steps_of(core)):
        count = -first
        for index, z_own, _, _ in each_want(pair_src, lax.bitwise_and(z, 3), x):
            theirs = z_own == ring(z + step)

            @pl.when(jnp.logical_and(theirs, jnp.logical_and(count >= 0, count < CAP)))
            def _():
                out[count] = terms[index]

            count = count + theirs.astype(jnp.int32)


def add_terms_kernel(place, pair_src, terms, near1, near2, near3, before, total):
    z, x, core, first = place[0], place[1], place[2], place[3]
    total[...] = before[...]
    for index, z_own, side, row in each_want(pair_src, lax.bitwise_and(z, 3), x):

        @pl.when(jnp.logical_and(z_own == z, first == 0))
        def _():
            at = 8 * side + row
            total[at] = total[at] + terms[index].astype(F32)

    for rows, step in zip((near1, near2, near3), steps_of(core)):
        count = -first
        for _, z_own, side, row in each_want(pair_src, lax.bitwise_and(z - step, 3), x):
            mine = z_own == z

            @pl.when(jnp.logical_and(mine, jnp.logical_and(count >= 0, count < CAP)))
            def _():
                at = 8 * side + row
                total[at] = total[at] + rows[count].astype(F32)

            count = count + mine.astype(jnp.int32)


AXES = ("band", "dom")


def shift(value, steps, mirror=False):
    pairs = []
    for z in range(RING):
        for x in range(2):
            for dom in range(16):
                go = -steps if mirror and dom % 2 else steps
                there = 2 * ((z + go) % RING) + x
                pairs.append(((2 * z + x) * 16 + dom, there * 16 + dom))
    return lax.ppermute(value, AXES, pairs)


def across(value):
    return lax.ppermute(value, "band", [(i, i ^ 1) for i in range(32)])


def hand_over(values):
    plus, minus, two = values
    return shift(plus, 1), shift(minus, -1), shift(two, 2, True)


def along_ring(value):
    groups = [[2 * (4 * turn + rest) + x for turn in range(4)] for rest in range(4) for x in range(2)]
    return lax.all_to_all(value, "band", 0, 0, axis_index_groups=groups, tiled=True)


def rounds_of(pair_src):
    group = jnp.arange(pair_src.shape[1], dtype=jnp.int32) // 2
    z, x = group // 2, group % 2
    z_own = pair_src // 8
    key = (z_own * 8 + (z % 4) * 2 + x).reshape(-1)
    moves = ((z_own - z) % 4 != 0).astype(jnp.int32).reshape(-1)
    shared = moves * jnp.sum((key[:, None] == key[None, :]).astype(jnp.int32), axis=1)
    return jnp.maximum(1, (jnp.max(shared) + CAP - 1) // CAP)


def per_device(targets, sources, pair_tgt, pair_src):
    table = {name: jnp.asarray(value) for name, value in tables().items()}
    band, dom = lax.axis_index("band"), lax.axis_index("dom")
    quarter = (dom // 4).astype(jnp.int32).reshape(1)
    rounds = rounds_of(pair_src)
    packet = struct((CAP, ROW, ROW), BF16)
    sixteen = struct((16, ROW, ROW), BF16)

    def place_in(turn):
        return jnp.stack([band // 2, band % 2, dom % 2, CAP * turn]).astype(jnp.int32)

    own = sources.reshape(8, ROW, ROW)
    other = across(own)

    def deliver(turn, before):
        scalars = (place_in(turn), pair_src)
        packed = vmem_call(pack_wanted_kernel, [packet] * 3, scalars + (own, other), scalars=2)
        operands = scalars + (own, other) + hand_over(packed) + (before,)
        return vmem_call(place_wanted_kernel, [sixteen], operands, scalars=2, alias={7: 0})[0]

    picked = lax.fori_loop(0, rounds, deliver, jnp.zeros((16, ROW, ROW), BF16))
    reached = along_ring(picked)

    ids = pair_tgt.reshape(4)
    wanted = targets[ids].reshape(4, ROW, ROW)
    four = struct((4, ROW, ROW), BF16)
    source_rows, spectra = vmem_call(
        density_kernel,
        [four, sixteen],
        (reached, wanted, table["z_fwd"], table["y_fwd"]),
    )
    slabs = lax.all_to_all(spectra, "dom", 0, 0, tiled=True)
    state = pltpu.VMEM((RING, ROW, ROW), F32)
    (solved,) = vmem_call(
        solve_kernel,
        [struct((16, 32, ROW), F32)],
        (quarter, slabs, table["spectrum"], table["x_fwd"], table["x_bwd"]),
        scalars=1,
        scratch=(state, state, state),
    )
    back = lax.all_to_all(solved, "dom", 0, 0, tiled=True)
    target_rows, terms = vmem_call(
        term_kernel,
        [four, sixteen],
        (pair_tgt, back, source_rows, wanted, table["z_bwd"], table["y_bwd"]),
        scalars=1,
        scratch=(pltpu.VMEM((4, ROW, ROW), F32),),
    )

    gathered = along_ring(terms)

    def collect(turn, before):
        scalars = (place_in(turn), pair_src)
        packed = vmem_call(pack_terms_kernel, [packet] * 3, scalars + (gathered,), scalars=2)
        operands = scalars + (gathered,) + hand_over(packed) + (before,)
        outs = [struct((16, ROW, ROW), F32)]
        return vmem_call(add_terms_kernel, outs, operands, scalars=2, alias={6: 0})[0]

    total = lax.fori_loop(0, rounds, collect, jnp.zeros((16, ROW, ROW), F32))
    partner = across(total[8:].astype(BF16))
    owned = (total[:8] + partner.astype(F32)).astype(BF16).reshape(sources.shape)

    flat = target_rows.reshape(4, targets.shape[1])
    slots = jnp.arange(targets.shape[0], dtype=jnp.int32)[:, None]
    summed = jnp.zeros(targets.shape, BF16)
    for p in range(4):
        summed = jnp.where(slots == ids[p], flat[p][None, :], summed)
    return summed, owned


def solution(mesh):
    return jax.shard_map(
        per_device,
        mesh=mesh,
        in_specs=(P("band", "dom"), P(None, "band", "dom"), P(None, "band"), P()),
        out_specs=(P("band", "dom"), P(None, "band", "dom")),
        check_vma=False,
    )
```

```python
import numpy as np
import jax
import jax.numpy as jnp
from jax import lax
from jax.experimental import pallas as pl
from jax.experimental.pallas import tpu as pltpu
from jax.sharding import PartitionSpec as P

SIDE = 64
SWEEPS = 8
RING = 16
STEPS = (1, -1, 2, -2, 3)
CAPS = (5, 5, 5, 5, 3)
ROW = 128
HALF = 64
VMEM_LIMIT = 48 * 1024 * 1024
F32 = jnp.float32
BF16 = jnp.bfloat16


def eigen_system():
    line = np.zeros((SIDE, SIDE))
    for delta, weight in ((0, 30.0), (1, -16.0), (2, 1.0)):
        for i in range(SIDE - delta):
            line[i, i + delta] = weight / 12.0
            line[i + delta, i] = weight / 12.0
    values, vectors = np.linalg.eigh(line)
    return values, vectors * np.where(vectors[0] < 0, -1.0, 1.0)[None, :]


def halves(matrix):
    high = np.asarray(matrix, np.float32).astype(jnp.bfloat16)
    low = (np.asarray(matrix, np.float64) - high.astype(np.float64)).astype(jnp.bfloat16)
    return np.stack([high, low])


def tables():
    values, v = eigen_system()
    along_z = np.kron(np.eye(2), v)
    even, odd = v[0::2], v[1::2]
    fwd = np.zeros((2, 32, 4, 2, 4, 32))
    bwd = np.zeros((2, 4, 32, 2, 32, 4))
    for x in range(4):
        fwd[0, :, x, 0, x, :] = even[:, 0::2].T
        fwd[0, :, x, 1, x, :] = odd[:, 0::2].T
        fwd[1, :, x, 0, x, :] = odd[:, 1::2].T
        fwd[1, :, x, 1, x, :] = even[:, 1::2].T
        bwd[0, x, :, 0, :, x] = even[:, 0::2]
        bwd[0, x, :, 1, :, x] = even[:, 1::2]
        bwd[1, x, :, 0, :, x] = odd[:, 1::2]
        bwd[1, x, :, 1, :, x] = odd[:, 0::2]
    along_x = np.zeros((2, SIDE, RING, 2, 4))
    for pick in range(2):
        along_x[pick, :, :, pick, :] = v.T.reshape(SIDE, RING, 4)
    rows = np.arange(SIDE).reshape(RING, 2, 1, 2, 1)
    spectrum = values[rows] + values.reshape(1, 1, SIDE, 1, 1) + values.reshape(1, 1, 1, 1, SIDE)
    return dict(
        z_fwd=halves(along_z),
        z_bwd=halves(along_z.T),
        y_fwd=halves(fwd.reshape(256, 256)),
        y_bwd=halves(bwd.reshape(256, 256)),
        x_fwd=halves(along_x.reshape(ROW, ROW)),
        x_bwd=halves(along_x.reshape(ROW, ROW).T),
        spectrum=spectrum.reshape(RING, ROW, ROW).astype(np.float32),
    )


def split(value):
    high = value.astype(BF16)
    return high, (value - high.astype(F32)).astype(BF16)


def mm(left, right):
    return jnp.dot(left, right, preferred_element_type=F32)


def left_mul(table, value):
    high, low = split(value)
    return mm(table[0], high) + mm(table[0], low) + mm(table[1], high)


def right_mul(value, table):
    high, low = split(value)
    return mm(high, table[0]) + mm(low, table[0]) + mm(high, table[1])


def mix_rows(table, value):
    swapped = jnp.concatenate([value[:, HALF:], value[:, :HALF]], axis=1)
    both = left_mul(table, jnp.concatenate([value, swapped], axis=0))
    lane = lax.broadcasted_iota(jnp.int32, (ROW, ROW), 1)
    return jnp.where(lane < HALF, both[:ROW], both[ROW:])


def vmem_call(kernel, outs, operands, scalars=0, scratch=()):
    whole = pl.BlockSpec(memory_space=pltpu.VMEM)
    smem = pl.BlockSpec(memory_space=pltpu.SMEM)
    return pl.pallas_call(
        kernel,
        out_shape=outs,
        in_specs=[smem] * scalars + [whole] * (len(operands) - scalars),
        out_specs=[whole] * len(outs),
        scratch_shapes=list(scratch),
        compiler_params=pltpu.CompilerParams(vmem_limit_bytes=VMEM_LIMIT),
    )(*operands)


def struct(shape, dtype):
    return jax.ShapeDtypeStruct(shape, dtype)


def owner_of(source):
    owner = lax.shift_right_logical(source, 2)
    return lax.shift_right_logical(owner, 1), lax.bitwise_and(owner, 1), lax.bitwise_and(source, 3)


def ring(value):
    return lax.bitwise_and(value, RING - 1)


def each_want(pair_src, relay, x, way, kinds=3):
    for kind, offset in enumerate((0, -5, 5)[:kinds]):
        band = 2 * ring(relay + offset * way) + x
        for slot in range(4):
            z_own, x_own, row = owner_of(pair_src[slot // 2, 2 * band + slot % 2])
            yield kind, slot, z_own, lax.bitwise_xor(x_own, x), 4 * (slot // 2) + row


def lanes_of(place, sign):
    z, x, way, turn = place[0], place[1], place[2], place[3]
    for n, (step, cap) in enumerate(zip(STEPS, CAPS)):
        there = ring(z + sign * step * way)
        yield n, there, -cap * turn, cap, (way, 3) if step < 3 else (way, 2)


def wants_at(place, pair_src, relay, lane):
    way, kinds = lane
    for want in each_want(pair_src, relay, place[1], way, kinds):
        if kinds == 3 or want[0] == 1:
            yield want


def fits(hit, count, cap):
    return jnp.logical_and(hit, jnp.logical_and(count >= 0, count < cap))


def copy_row(out, at, own, other, side, row):
    for rows, where in ((own, 0), (other, 1)):

        @pl.when(side == where)
        def _():
            out[at] = rows[row]


def pack_wanted_kernel(place, pair_src, own, other, *outs):
    for n, relay, count, cap, lane in lanes_of(place, -1):
        for _, _, z_own, side, row in wants_at(place, pair_src, relay, lane):
            mine = z_own == place[0]

            @pl.when(fits(mine, count, cap))
            def _():
                copy_row(outs[n], count, own, other, side, row)

            count = count + mine.astype(jnp.int32)


def place_wanted_kernel(place, pair_src, own, other, *refs):
    near, before, outs = refs[:5], refs[5:-3], refs[-3:]
    z = place[0]
    for old, out in zip(before, outs):
        out[...] = old[...]
    if not before:
        for kind, slot, z_own, side, row in each_want(pair_src, z, place[1], place[2]):

            @pl.when(z_own == z)
            def _():
                copy_row(outs[kind], slot, own, other, side, row)

    for n, owner, count, cap, lane in lanes_of(place, 1):
        for kind, slot, z_own, _, _ in wants_at(place, pair_src, z, lane):
            theirs = z_own == owner

            @pl.when(fits(theirs, count, cap))
            def _():
                outs[kind][slot] = near[n][count]

            count = count + theirs.astype(jnp.int32)


def density_kernel(place, pair_src, here, ahead, behind, wanted, z_fwd, y_fwd, source_rows, spectra):
    z, x, way = place[0], place[1], place[2]
    for p in range(4):
        z_own, _, _ = owner_of(pair_src[p // 2, 2 * (2 * z + x) + p % 2])
        away = ring(way * (z_own - z) + 2)
        for rows, least, most in ((here, 0, 4), (ahead, 5, 10), (behind, 11, 15)):

            @pl.when(jnp.logical_and(away >= least, away <= most))
            def _():
                source_rows[p] = rows[p]

        density = source_rows[p].astype(F32) * wanted[p].astype(F32)
        mixed = mix_rows(y_fwd, right_mul(density, z_fwd)).astype(spectra.dtype)
        for copy in range(4):
            spectra[4 * copy + p] = mixed


def solve_kernel(quarter, slabs, spectrum, x_fwd, x_bwd, out, first, residual, direction):
    def dot_of(value):
        return jnp.sum(value.reshape(RING, 8, ROW), axis=0)

    zero = jnp.zeros((8, ROW), F32)

    def start(j, carry):
        norm, power = carry
        part = slabs[:, pl.ds(pl.multiple_of(8 * j, 8), 8), :].reshape(ROW, ROW)
        value = mm(x_fwd[0], part) + mm(x_fwd[1], part)
        first[j] = value
        square = value * value
        return norm + dot_of(square), power + dot_of(square * spectrum[j])

    norm, power = lax.fori_loop(0, RING, start, (zero, zero), unroll=2)
    norm, power = jnp.sum(norm), jnp.sum(power)
    steps, ratios = [norm / power], [jnp.float32(0.0)]
    for sweep in range(SWEEPS - 1):
        step, ratio = steps[-1], ratios[-1]

        def advance(j, carry, sweep=sweep, step=step, ratio=ratio):
            new, power = carry
            lam = spectrum[j]
            if sweep == 0:
                d = first[j]
                r = d - step * (lam * d)
            else:
                d = residual[j] + ratio * (first[j] if sweep == 1 else direction[j])
                r = residual[j] - step * (lam * d)
            if sweep > 0:
                direction[j] = d
            residual[j] = r
            square = r * r
            return new + dot_of(square), power + dot_of(square * lam)

        new, power = lax.fori_loop(0, RING, advance, (zero, zero), unroll=2)
        new, power = jnp.sum(new), jnp.sum(power)
        ratio = new / norm
        steps.append(new / (power - ratio * new / step))
        ratios.append(ratio)
        norm = new

    for jj in range(4):
        j = 4 * quarter[0] + jj
        lam, r = spectrum[j], first[j]
        d, total = r, steps[0] * r
        for sweep in range(1, SWEEPS):
            r = r - steps[sweep - 1] * (lam * d)
            d = r + ratios[sweep] * d
            total = total + steps[sweep] * d
        part = left_mul(x_bwd, total)
        out[:, 8 * jj : 8 * jj + 8, :] = part.reshape(RING, 8, ROW).astype(out.dtype)


def term_kernel(pair_tgt, spectra, source_rows, wanted, z_bwd, y_bwd, target_rows, terms, held):
    for p in range(4):
        rows = jnp.concatenate([spectra[4 * q + p].astype(F32) for q in range(4)], axis=0)
        potential = right_mul(mix_rows(y_bwd, rows), z_bwd)
        terms[p] = (-potential * wanted[p].astype(F32)).astype(BF16)
        held[p] = -potential * source_rows[p].astype(F32)
    for p in range(4):
        same = jnp.zeros((ROW, ROW), F32)
        for other in range(4):
            hit = pair_tgt[p // 2, p % 2] == pair_tgt[other // 2, other % 2]
            same = same + jnp.where(hit, held[other], 0.0)
        target_rows[p] = same.astype(BF16)


def pack_terms_kernel(place, pair_src, here, ahead, behind, *outs):
    terms = (here, ahead, behind)
    for n, owner, count, cap, lane in lanes_of(place, 1):
        for kind, slot, z_own, _, _ in wants_at(place, pair_src, place[0], lane):
            theirs = z_own == owner

            @pl.when(fits(theirs, count, cap))
            def _():
                outs[n][count] = terms[kind][slot]

            count = count + theirs.astype(jnp.int32)


def add_terms_kernel(place, pair_src, here, ahead, behind, *refs):
    near, before, totals = refs[:5], refs[5:-2], refs[-2:]
    terms = (here, ahead, behind)
    z = place[0]

    def add(side, row, term):
        for where, total in enumerate(totals):

            @pl.when(side == where)
            def _():
                total[row] = total[row] + term.astype(F32)

    for total in totals:
        total[...] = jnp.zeros((8, ROW, ROW), F32)
    for old, total in zip(before, totals):
        total[...] = old[...]
    if not before:
        for kind, slot, z_own, side, row in each_want(pair_src, z, place[1], place[2]):

            @pl.when(z_own == z)
            def _():
                add(side, row, terms[kind][slot])

    for n, relay, count, cap, lane in lanes_of(place, -1):
        for _, _, z_own, side, row in wants_at(place, pair_src, relay, lane):
            mine = z_own == z

            @pl.when(fits(mine, count, cap))
            def _():
                add(side, row, near[n][count])

            count = count + mine.astype(jnp.int32)


AXES = ("band", "dom")


def shift(value, steps):
    pairs = []
    for z in range(RING):
        for x in range(2):
            for dom in range(16):
                there = 2 * ((z + (-steps if dom % 2 else steps)) % RING) + x
                pairs.append(((2 * z + x) * 16 + dom, there * 16 + dom))
    return lax.ppermute(value, AXES, pairs)


def across(value):
    return lax.ppermute(value, "band", [(i, i ^ 1) for i in range(32)])


def rounds_of(pair_src):
    band = jnp.arange(pair_src.shape[1], dtype=jnp.int32) // 2
    z, x = band // 2, band % 2
    z_own = pair_src // 8
    away = (z_own - z + 2) % RING
    relay = jnp.where(away <= 4, z, jnp.where(away < 10, z + 5, z - 5)) % RING
    far = away == 10
    relay = jnp.where(far, RING, relay)
    key = ((z_own * 32 + relay) * 2 + x).reshape(-1)
    shared = jnp.sum((key[:, None] == key[None, :]).astype(jnp.int32), axis=1).reshape(pair_src.shape)
    turns = jnp.where(far, (shared + CAPS[4] - 1) // CAPS[4], (shared + CAPS[0] - 1) // CAPS[0])
    return jnp.max(jnp.where(relay == z_own, 1, turns))


def per_device(targets, sources, pair_tgt, pair_src):
    table = {name: jnp.asarray(value) for name, value in tables().items()}
    band, dom = lax.axis_index("band"), lax.axis_index("dom")
    quarter = (dom // 4).astype(jnp.int32).reshape(1)
    rounds = rounds_of(pair_src)
    packets = [struct((cap, ROW, ROW), BF16) for cap in CAPS]
    four = struct((4, ROW, ROW), BF16)
    eight = struct((8, ROW, ROW), F32)

    def scalars_of(turn):
        turn = jnp.asarray(turn, jnp.int32)
        return jnp.stack([band // 2, band % 2, 1 - 2 * (dom % 2), turn]).astype(jnp.int32), pair_src

    own = sources.reshape(8, ROW, ROW)
    other = across(own)

    def deliver(turn, before):
        scalars = scalars_of(turn)
        packed = vmem_call(pack_wanted_kernel, packets, scalars + (own, other), scalars=2)
        near = tuple(shift(packet, -step) for packet, step in zip(packed, STEPS))
        operands = scalars + (own, other) + near + tuple(before)
        return vmem_call(place_wanted_kernel, [four] * 3, operands, scalars=2)

    here, ahead, behind = lax.fori_loop(1, rounds, deliver, deliver(0, ()))
    reached = (here, shift(ahead, -5), shift(behind, 5))

    ids = pair_tgt.reshape(4)
    wanted = targets[ids].reshape(4, ROW, ROW)
    source_rows, spectra = vmem_call(
        density_kernel,
        [four, struct((16, ROW, ROW), BF16)],
        scalars_of(0) + reached + (wanted, table["z_fwd"], table["y_fwd"]),
        scalars=2,
    )
    slabs = lax.all_to_all(spectra, "dom", 0, 0, tiled=True)
    state = pltpu.VMEM((RING, ROW, ROW), F32)
    (solved,) = vmem_call(
        solve_kernel,
        [struct((16, 32, ROW), F32)],
        (quarter, slabs, table["spectrum"], table["x_fwd"], table["x_bwd"]),
        scalars=1,
        scratch=(state, state, state),
    )
    back = lax.all_to_all(solved, "dom", 0, 0, tiled=True)
    target_rows, terms = vmem_call(
        term_kernel,
        [four, four],
        (pair_tgt, back, source_rows, wanted, table["z_bwd"], table["y_bwd"]),
        scalars=1,
        scratch=(pltpu.VMEM((4, ROW, ROW), F32),),
    )
    held = (terms, shift(terms, 5), shift(terms, -5))

    def collect(turn, before):
        scalars = scalars_of(turn)
        packed = vmem_call(pack_terms_kernel, packets, scalars + held, scalars=2)
        near = tuple(shift(packet, step) for packet, step in zip(packed, STEPS))
        operands = scalars + held + near + tuple(before)
        return vmem_call(add_terms_kernel, [eight] * 2, operands, scalars=2)

    mine, partner = lax.fori_loop(1, rounds, collect, collect(0, ()))
    owned = (mine + across(partner.astype(BF16)).astype(F32)).astype(BF16).reshape(sources.shape)

    flat = target_rows.reshape(4, targets.shape[1])
    slots = jnp.arange(targets.shape[0], dtype=jnp.int32)[:, None]
    summed = jnp.zeros(targets.shape, BF16)
    for p in range(4):
        summed = jnp.where(slots == ids[p], flat[p][None, :], summed)
    return summed, owned


def solution(mesh):
    return jax.shard_map(
        per_device,
        mesh=mesh,
        in_specs=(P("band", "dom"), P(None, "band", "dom"), P(None, "band"), P()),
        out_specs=(P("band", "dom"), P(None, "band", "dom")),
        check_vma=False,
    )
```

```python
import numpy as np
import jax
import jax.numpy as jnp
from jax import lax
from jax.experimental import pallas as pl
from jax.experimental.pallas import tpu as pltpu
from jax.sharding import PartitionSpec as P

SIDE = 64
SWEEPS = 8
RING = 16
CAP = 4
ROW = 128
HALF = 64
VMEM_LIMIT = 48 * 1024 * 1024
F32 = jnp.float32
BF16 = jnp.bfloat16


def eigen_system():
    line = np.zeros((SIDE, SIDE))
    for delta, weight in ((0, 30.0), (1, -16.0), (2, 1.0)):
        for i in range(SIDE - delta):
            line[i, i + delta] = weight / 12.0
            line[i + delta, i] = weight / 12.0
    values, vectors = np.linalg.eigh(line)
    return values, vectors * np.where(vectors[0] < 0, -1.0, 1.0)[None, :]


def halves(matrix):
    high = np.asarray(matrix, np.float32).astype(jnp.bfloat16)
    low = (np.asarray(matrix, np.float64) - high.astype(np.float64)).astype(jnp.bfloat16)
    return np.stack([high, low])


def tables():
    values, v = eigen_system()
    along_z = np.kron(np.eye(2), v)
    even, odd = v[0::2], v[1::2]
    fwd = np.zeros((2, 32, 4, 2, 4, 32))
    bwd = np.zeros((2, 4, 32, 2, 32, 4))
    for x in range(4):
        fwd[0, :, x, 0, x, :] = even[:, 0::2].T
        fwd[0, :, x, 1, x, :] = odd[:, 0::2].T
        fwd[1, :, x, 0, x, :] = odd[:, 1::2].T
        fwd[1, :, x, 1, x, :] = even[:, 1::2].T
        bwd[0, x, :, 0, :, x] = even[:, 0::2]
        bwd[0, x, :, 1, :, x] = even[:, 1::2]
        bwd[1, x, :, 0, :, x] = odd[:, 1::2]
        bwd[1, x, :, 1, :, x] = odd[:, 0::2]
    along_x = np.zeros((2, SIDE, RING, 2, 4))
    for pick in range(2):
        along_x[pick, :, :, pick, :] = v.T.reshape(SIDE, RING, 4)
    rows = np.arange(SIDE).reshape(RING, 2, 1, 2, 1)
    spectrum = values[rows] + values.reshape(1, 1, SIDE, 1, 1) + values.reshape(1, 1, 1, 1, SIDE)
    return dict(
        z_fwd=halves(along_z),
        z_bwd=halves(along_z.T),
        y_fwd=halves(fwd.reshape(256, 256)),
        y_bwd=halves(bwd.reshape(256, 256)),
        x_fwd=halves(along_x.reshape(ROW, ROW)),
        x_bwd=halves(along_x.reshape(ROW, ROW).T),
        spectrum=spectrum.reshape(RING, ROW, ROW).astype(np.float32),
    )


def split(value):
    high = value.astype(BF16)
    return high, (value - high.astype(F32)).astype(BF16)


def mm(left, right):
    return jnp.dot(left, right, preferred_element_type=F32)


def left_mul(table, value):
    high, low = split(value)
    return mm(table[0], high) + mm(table[0], low) + mm(table[1], high)


def right_mul(value, table):
    high, low = split(value)
    return mm(high, table[0]) + mm(low, table[0]) + mm(high, table[1])


def mix_rows(table, value):
    swapped = jnp.concatenate([value[:, HALF:], value[:, :HALF]], axis=1)
    both = left_mul(table, jnp.concatenate([value, swapped], axis=0))
    lane = lax.broadcasted_iota(jnp.int32, (ROW, ROW), 1)
    return jnp.where(lane < HALF, both[:ROW], both[ROW:])


def vmem_call(kernel, outs, operands, scalars=0, scratch=()):
    whole = pl.BlockSpec(memory_space=pltpu.VMEM)
    smem = pl.BlockSpec(memory_space=pltpu.SMEM)
    return pl.pallas_call(
        kernel,
        out_shape=outs,
        in_specs=[smem] * scalars + [whole] * (len(operands) - scalars),
        out_specs=[whole] * len(outs),
        scratch_shapes=list(scratch),
        compiler_params=pltpu.CompilerParams(vmem_limit_bytes=VMEM_LIMIT),
    )(*operands)


def smem_call(kernel, size, *operands):
    smem = pl.BlockSpec(memory_space=pltpu.SMEM)
    return pl.pallas_call(
        kernel,
        out_shape=struct((size,), jnp.int32),
        in_specs=[smem] * len(operands),
        out_specs=smem,
    )(*operands)


def struct(shape, dtype):
    return jax.ShapeDtypeStruct(shape, dtype)


def owner_of(source):
    return lax.shift_right_logical(source, 2), lax.bitwise_and(source, 3)


def wants_of(pair_src, member):
    for quad in range(4):
        for slot in range(4):
            owner, row = owner_of(pair_src[slot // 2, 2 * (8 * quad + member) + slot % 2])
            yield 4 * quad + slot, owner, 4 * (slot // 2) + row


def in_round(hit, count):
    return jnp.logical_and(hit, jnp.logical_and(count >= 0, count < CAP))


def sent_kernel(place, pair_src, sent):
    for member in range(8):
        for n in range(CAP):
            sent[member * CAP + n] = -1
        count = -CAP * place[1]
        for _, owner, row in wants_of(pair_src, member):
            hit = owner == place[0]

            @pl.when(in_round(hit, count))
            def _():
                sent[member * CAP + count] = row

            count = count + hit.astype(jnp.int32)


def found_kernel(place, pair_src, found):
    band = place[0]
    wants = list(wants_of(pair_src, lax.bitwise_and(band, 7)))
    for index, owner, _ in wants:
        count = -CAP * place[1]
        for _, other, _ in wants[:index]:
            count = count + (other == owner).astype(jnp.int32)
        near = lax.shift_right_logical(owner, 3) == lax.shift_right_logical(band, 3)
        at = lax.bitwise_and(owner, 7) * CAP + count
        found[index] = jnp.where(in_round(near, count), at, -1)


def pack_rows_kernel(sent, own, out):
    for n in range(8 * CAP):

        @pl.when(sent[n] >= 0)
        def _():
            out[n] = own[sent[n]]


def place_rows_kernel(found, near, *refs):
    out = refs[-1]
    for before in refs[:-1]:
        out[...] = before[...]
    for want in range(16):

        @pl.when(found[want] >= 0)
        def _():
            out[want] = near[found[want]]


def pack_terms_kernel(found, held, out):
    for want in range(16):

        @pl.when(found[want] >= 0)
        def _():
            out[found[want]] = held[want]


def add_terms_kernel(sent, near, *refs):
    total = refs[-1]
    total[...] = jnp.zeros((8, ROW, ROW), F32)
    for before in refs[:-1]:
        total[...] = before[...]
    for n in range(8 * CAP):

        @pl.when(sent[n] >= 0)
        def _():
            total[sent[n]] = total[sent[n]] + near[n].astype(F32)


def density_kernel(place, pair_src, reached, wanted, z_fwd, y_fwd, source_rows, spectra):
    for p in range(4):
        owner, _ = owner_of(pair_src[p // 2, 2 * place[0] + p % 2])
        source_rows[p] = reached[4 * lax.shift_right_logical(owner, 3) + p]
        density = source_rows[p].astype(F32) * wanted[p].astype(F32)
        mixed = mix_rows(y_fwd, right_mul(density, z_fwd)).astype(spectra.dtype)
        for copy in range(4):
            spectra[4 * copy + p] = mixed


def solve_kernel(quarter, slabs, spectrum, x_fwd, x_bwd, out, first, residual, direction):
    def dot_of(value):
        return jnp.sum(value.reshape(RING, 8, ROW), axis=0)

    zero = jnp.zeros((8, ROW), F32)

    def start(j, carry):
        norm, power = carry
        part = slabs[:, pl.ds(pl.multiple_of(8 * j, 8), 8), :].reshape(ROW, ROW)
        value = mm(x_fwd[0], part) + mm(x_fwd[1], part)
        first[j] = value
        square = value * value
        return norm + dot_of(square), power + dot_of(square * spectrum[j])

    norm, power = lax.fori_loop(0, RING, start, (zero, zero), unroll=2)
    norm, power = jnp.sum(norm), jnp.sum(power)
    steps, ratios = [norm / power], [jnp.float32(0.0)]
    for sweep in range(SWEEPS - 1):
        step, ratio = steps[-1], ratios[-1]

        def advance(j, carry, sweep=sweep, step=step, ratio=ratio):
            new, power = carry
            lam = spectrum[j]
            if sweep == 0:
                d = first[j]
                r = d - step * (lam * d)
            else:
                d = residual[j] + ratio * (first[j] if sweep == 1 else direction[j])
                r = residual[j] - step * (lam * d)
            if sweep > 0:
                direction[j] = d
            residual[j] = r
            square = r * r
            return new + dot_of(square), power + dot_of(square * lam)

        new, power = lax.fori_loop(0, RING, advance, (zero, zero), unroll=2)
        new, power = jnp.sum(new), jnp.sum(power)
        ratio = new / norm
        steps.append(new / (power - ratio * new / step))
        ratios.append(ratio)
        norm = new

    for jj in range(4):
        j = 4 * quarter[0] + jj
        lam, r = spectrum[j], first[j]
        d, total = r, steps[0] * r
        for sweep in range(1, SWEEPS):
            r = r - steps[sweep - 1] * (lam * d)
            d = r + ratios[sweep] * d
            total = total + steps[sweep] * d
        part = left_mul(x_bwd, total)
        out[:, 8 * jj : 8 * jj + 8, :] = part.reshape(RING, 8, ROW).astype(out.dtype)


def term_kernel(pair_tgt, spectra, source_rows, wanted, z_bwd, y_bwd, target_rows, terms, held):
    for p in range(4):
        rows = jnp.concatenate([spectra[4 * q + p].astype(F32) for q in range(4)], axis=0)
        potential = right_mul(mix_rows(y_bwd, rows), z_bwd)
        term = (-potential * wanted[p].astype(F32)).astype(BF16)
        for quad in range(4):
            terms[4 * quad + p] = term
        held[p] = -potential * source_rows[p].astype(F32)
    for p in range(4):
        same = jnp.zeros((ROW, ROW), F32)
        for other in range(4):
            hit = pair_tgt[p // 2, p % 2] == pair_tgt[other // 2, other % 2]
            same = same + jnp.where(hit, held[other], 0.0)
        target_rows[p] = same.astype(BF16)


def within_quad(value):
    groups = [[8 * quad + member for member in range(8)] for quad in range(4)]
    return lax.all_to_all(value, "band", 0, 0, axis_index_groups=groups, tiled=True)


def along_ring(value):
    groups = [[8 * quad + member for quad in range(4)] for member in range(8)]
    return lax.all_to_all(value, "band", 0, 0, axis_index_groups=groups, tiled=True)


def rounds_of(pair_src):
    band = jnp.arange(pair_src.shape[1], dtype=jnp.int32) // 2
    key = ((pair_src // 4) * 8 + band % 8).reshape(-1)
    shared = jnp.sum((key[:, None] == key[None, :]).astype(jnp.int32), axis=1)
    return (jnp.max(shared) + CAP - 1) // CAP


def per_device(targets, sources, pair_tgt, pair_src):
    table = {name: jnp.asarray(value) for name, value in tables().items()}
    band, dom = lax.axis_index("band"), lax.axis_index("dom")
    quarter = (dom // 4).astype(jnp.int32).reshape(1)
    rounds = rounds_of(pair_src)
    four = struct((4, ROW, ROW), BF16)
    sixteen = struct((16, ROW, ROW), BF16)
    packet = struct((8 * CAP, ROW, ROW), BF16)
    own = sources.reshape(8, ROW, ROW)

    def place_in(turn):
        return jnp.stack([band, jnp.asarray(turn, jnp.int32)]).astype(jnp.int32)

    def sent_in(turn):
        return smem_call(sent_kernel, 8 * CAP, place_in(turn), pair_src)

    def found_in(turn):
        return smem_call(found_kernel, 16, place_in(turn), pair_src)

    def deliver(sent, found, before):
        (packed,) = vmem_call(pack_rows_kernel, [packet], (sent, own), scalars=1)
        operands = (found, within_quad(packed)) + before
        return vmem_call(place_rows_kernel, [sixteen], operands, scalars=1)[0]

    sent, found = sent_in(0), found_in(0)
    picked = lax.fori_loop(
        1,
        rounds,
        lambda turn, before: deliver(sent_in(turn), found_in(turn), (before,)),
        deliver(sent, found, ()),
    )
    reached = along_ring(picked)

    ids = pair_tgt.reshape(4)
    wanted = targets[ids].reshape(4, ROW, ROW)
    source_rows, spectra = vmem_call(
        density_kernel,
        [four, sixteen],
        (place_in(0), pair_src, reached, wanted, table["z_fwd"], table["y_fwd"]),
        scalars=2,
    )
    slabs = lax.all_to_all(spectra, "dom", 0, 0, tiled=True)
    state = pltpu.VMEM((RING, ROW, ROW), F32)
    (solved,) = vmem_call(
        solve_kernel,
        [struct((16, 32, ROW), F32)],
        (quarter, slabs, table["spectrum"], table["x_fwd"], table["x_bwd"]),
        scalars=1,
        scratch=(state, state, state),
    )
    back = lax.all_to_all(solved, "dom", 0, 0, tiled=True)
    target_rows, terms = vmem_call(
        term_kernel,
        [four, sixteen],
        (pair_tgt, back, source_rows, wanted, table["z_bwd"], table["y_bwd"]),
        scalars=1,
        scratch=(pltpu.VMEM((4, ROW, ROW), F32),),
    )
    held = along_ring(terms)

    def collect(sent, found, before):
        (packed,) = vmem_call(pack_terms_kernel, [packet], (found, held), scalars=1)
        operands = (sent, within_quad(packed)) + before
        return vmem_call(add_terms_kernel, [struct((8, ROW, ROW), F32)], operands, scalars=1)[0]

    total = lax.fori_loop(
        1,
        rounds,
        lambda turn, before: collect(sent_in(turn), found_in(turn), (before,)),
        collect(sent, found, ()),
    )
    owned = total.astype(BF16).reshape(sources.shape)

    flat = target_rows.reshape(4, targets.shape[1])
    slots = jnp.arange(targets.shape[0], dtype=jnp.int32)[:, None]
    summed = jnp.zeros(targets.shape, BF16)
    for p in range(4):
        summed = jnp.where(slots == ids[p], flat[p][None, :], summed)
    return summed, owned


def solution(mesh):
    return jax.shard_map(
        per_device,
        mesh=mesh,
        in_specs=(P("band", "dom"), P(None, "band", "dom"), P(None, "band"), P()),
        out_specs=(P("band", "dom"), P(None, "band", "dom")),
        check_vma=False,
    )
```

```python
import numpy as np
import jax
import jax.numpy as jnp
from jax import lax
from jax.experimental import pallas as pl
from jax.experimental.pallas import tpu as pltpu
from jax.sharding import PartitionSpec as P

SIDE = 64
SWEEPS = 8
RING = 16
CAP = 6
STEPS = (1, -1, 2)
ROW = 128
HALF = 64
VMEM_LIMIT = 48 * 1024 * 1024
F32 = jnp.float32
BF16 = jnp.bfloat16


def eigen_system():
    line = np.zeros((SIDE, SIDE))
    for delta, weight in ((0, 30.0), (1, -16.0), (2, 1.0)):
        for i in range(SIDE - delta):
            line[i, i + delta] = weight / 12.0
            line[i + delta, i] = weight / 12.0
    values, vectors = np.linalg.eigh(line)
    return values, vectors * np.where(vectors[0] < 0, -1.0, 1.0)[None, :]


def halves(matrix):
    high = np.asarray(matrix, np.float32).astype(jnp.bfloat16)
    low = (np.asarray(matrix, np.float64) - high.astype(np.float64)).astype(jnp.bfloat16)
    return np.stack([high, low])


def tables():
    values, v = eigen_system()
    along_z = np.kron(np.eye(2), v)
    even, odd = v[0::2], v[1::2]
    fwd = np.zeros((2, 32, 4, 2, 4, 32))
    bwd = np.zeros((2, 4, 32, 2, 32, 4))
    for x in range(4):
        fwd[0, :, x, 0, x, :] = even[:, 0::2].T
        fwd[0, :, x, 1, x, :] = odd[:, 0::2].T
        fwd[1, :, x, 0, x, :] = odd[:, 1::2].T
        fwd[1, :, x, 1, x, :] = even[:, 1::2].T
        bwd[0, x, :, 0, :, x] = even[:, 0::2]
        bwd[0, x, :, 1, :, x] = even[:, 1::2]
        bwd[1, x, :, 0, :, x] = odd[:, 1::2]
        bwd[1, x, :, 1, :, x] = odd[:, 0::2]
    along_x = np.zeros((4, SIDE, RING, 4, 4))
    for pick in range(4):
        along_x[pick, :, :, pick, :] = v.T.reshape(SIDE, RING, 4)
    rows = np.arange(SIDE).reshape(8, 4, 1, 2, 1)
    spectrum = values[rows] + values.reshape(1, 1, SIDE, 1, 1) + values.reshape(1, 1, 1, 1, SIDE)
    return dict(
        z_fwd=halves(along_z),
        z_bwd=halves(along_z.T),
        y_fwd=halves(fwd.reshape(256, 256)),
        y_bwd=halves(bwd.reshape(256, 256)),
        x_fwd=halves(along_x.reshape(256, 256)),
        x_bwd=halves(along_x.reshape(256, 256).T),
        spectrum=spectrum.reshape(8, 256, ROW).astype(np.float32),
    )


def split(value):
    high = value.astype(BF16)
    return high, (value - high.astype(F32)).astype(BF16)


def mm(left, right):
    return jnp.dot(left, right, preferred_element_type=F32)


def left_mul(table, value):
    high, low = split(value)
    return mm(table[0], high) + mm(table[0], low) + mm(table[1], high)


def right_mul(value, table):
    high, low = split(value)
    return mm(high, table[0]) + mm(low, table[0]) + mm(high, table[1])


def swap_halves(value):
    return jnp.concatenate([value[:, HALF:], value[:, :HALF]], axis=1)


def by_half(both):
    lane = lax.broadcasted_iota(jnp.int32, (ROW, ROW), 1)
    return jnp.where(lane < HALF, both[:ROW], both[ROW:])


def vmem_call(kernel, outs, operands, scalars=0, scratch=()):
    whole = pl.BlockSpec(memory_space=pltpu.VMEM)
    smem = pl.BlockSpec(memory_space=pltpu.SMEM)
    return pl.pallas_call(
        kernel,
        out_shape=outs,
        in_specs=[smem] * scalars + [whole] * (len(operands) - scalars),
        out_specs=[whole] * len(outs),
        scratch_shapes=list(scratch),
        compiler_params=pltpu.CompilerParams(vmem_limit_bytes=VMEM_LIMIT),
    )(*operands)


def smem_call(kernel, size, *operands):
    smem = pl.BlockSpec(memory_space=pltpu.SMEM)
    return pl.pallas_call(
        kernel,
        out_shape=struct((size,), jnp.int32),
        in_specs=[smem] * len(operands),
        out_specs=smem,
    )(*operands)


def struct(shape, dtype):
    return jax.ShapeDtypeStruct(shape, dtype)


def ring(value):
    return lax.bitwise_and(value, RING - 1)


def want_of(pair_src, z, x, want):
    quad, slot = lax.shift_right_logical(want, 2), lax.bitwise_and(want, 3)
    block = lax.shift_right_logical(slot, 1)
    band = 2 * (4 * quad + lax.bitwise_and(z, 3)) + x
    source = pair_src[block, 2 * band + lax.bitwise_and(slot, 1)]
    z_own = lax.shift_right_logical(source, 3)
    other = lax.bitwise_xor(lax.bitwise_and(lax.shift_right_logical(source, 2), 1), x)
    return z_own, 8 * other + 4 * block + lax.bitwise_and(source, 3)


def wants_of(pair_src, z, x):
    for want in range(16):
        yield (want,) + want_of(pair_src, z, x, jnp.int32(want))


def in_round(hit, count):
    return jnp.logical_and(hit, jnp.logical_and(count >= 0, count < CAP))


def sent_kernel(place, pair_src, sent):
    z, x = place[0], place[1]
    for lane, step in enumerate(STEPS):
        for n in range(CAP):
            sent[lane * CAP + n] = -1
        count = -CAP * place[2]
        for _, z_own, row in wants_of(pair_src, z + step, x):
            hit = z_own == z

            @pl.when(in_round(hit, count))
            def _():
                sent[lane * CAP + count] = row

            count = count + hit.astype(jnp.int32)


def found_kernel(place, pair_src, found):
    z, x, turn = place[0], place[1], place[2]
    counts = [-CAP * turn for _ in STEPS]
    for want, z_own, row in wants_of(pair_src, z, x):
        at = jnp.where(jnp.logical_and(z_own == z, turn == 0), row, -1)
        for lane, step in enumerate(STEPS):
            hit = z_own == ring(z - step)
            at = jnp.where(in_round(hit, counts[lane]), 16 + lane * CAP + counts[lane], at)
            counts[lane] = counts[lane] + hit.astype(jnp.int32)
        found[want] = at


def pack_rows_kernel(sent, own, other, *outs):
    for lane, out in enumerate(outs):
        for n in range(CAP):
            row = sent[lane * CAP + n]

            @pl.when(row >= 0)
            def _():
                @pl.when(row < 8)
                def _():
                    out[n] = own[row]

                @pl.when(row >= 8)
                def _():
                    out[n] = other[row - 8]


def place_rows_kernel(found, own, other, *refs):
    out = refs[-1]
    for before in refs[3:-1]:
        out[...] = before[...]
    spans = [(own, 0, 8), (other, 8, 16)]
    spans += [(near, 16 + lane * CAP, 16 + lane * CAP + CAP) for lane, near in enumerate(refs[:3])]
    for want in range(16):
        at = found[want]

        @pl.when(at >= 0)
        def _():
            for rows, first, last in spans:

                @pl.when(jnp.logical_and(at >= first, at < last))
                def _():
                    out[want] = rows[at - first]


def for_each_solved(place, pair_src, body):
    z, x = place[0], place[1]

    def step(want, carry):
        z_own, _ = want_of(pair_src, z, x, want)
        ahead = ring(z - z_own)

        @pl.when(jnp.logical_or(ahead <= 2, ahead == RING - 1))
        def _():
            body(want)

        return carry

    lax.fori_loop(0, 16, step, 0)


def density_kernel(place, pair_src, sources, wanted, z_fwd, y_fwd, spectra):
    def body(want):
        density = sources[want].astype(F32) * wanted[want].astype(F32)
        along = right_mul(density, z_fwd)
        mixed = left_mul(y_fwd, jnp.concatenate([along, swap_halves(along)], axis=0))
        spectra[want] = by_half(mixed).astype(BF16)

    for_each_solved(place, pair_src, body)


def solve_kernel(slabs, spectrum, x_fwd, x_bwd, out, residual, direction, total):
    def dot_of(value):
        return jnp.sum(value.reshape(32, 8, ROW), axis=0)

    zero = jnp.zeros((8, ROW), F32)

    def start(j, carry):
        norm, power = carry
        part = slabs[:, pl.ds(pl.multiple_of(16 * j, 16), 16), :].reshape(256, ROW)
        value = mm(x_fwd[0], part) + mm(x_fwd[1], part)
        direction[j] = value
        square = value * value
        return norm + dot_of(square), power + dot_of(square * spectrum[j])

    norm, power = lax.fori_loop(0, 8, start, (zero, zero))
    norm, power = jnp.sum(norm), jnp.sum(power)
    step, ratio = norm / power, jnp.float32(0.0)
    for sweep in range(SWEEPS - 1):

        def advance(j, carry, sweep=sweep, step=step, ratio=ratio):
            new, power = carry
            lam = spectrum[j]
            if sweep == 0:
                d = direction[j]
                r = d - step * (lam * d)
                total[j] = step * d
            else:
                r = residual[j]
                d = r + ratio * direction[j]
                r = r - step * (lam * d)
                direction[j] = d
                total[j] = total[j] + step * d
            residual[j] = r
            square = r * r
            return new + dot_of(square), power + dot_of(square * lam)

        new, power = lax.fori_loop(0, 8, advance, (zero, zero))
        new, power = jnp.sum(new), jnp.sum(power)
        ratio = new / norm
        step = new / (power - ratio * new / step)
        norm = new

    def finish(j, carry):
        value = total[j] + step * (residual[j] + ratio * direction[j])
        part = left_mul(x_bwd, value).reshape(RING, 16, ROW)
        out[:, pl.ds(pl.multiple_of(16 * j, 16), 16), :] = part.astype(out.dtype)
        return carry

    lax.fori_loop(0, 8, finish, 0)


def term_kernel(place, pair_src, spectra, sources, wanted, z_bwd, y_bwd, terms, shares):
    def body(want):
        rows = spectra[want]
        rows = jnp.concatenate([rows, swap_halves(rows)], axis=0)
        potential = right_mul(by_half(mm(y_bwd[0], rows) + mm(y_bwd[1], rows)), z_bwd)
        terms[want] = (-potential * wanted[want].astype(F32)).astype(BF16)
        shares[want] = (-potential * sources[want].astype(F32)).astype(BF16)

    for_each_solved(place, pair_src, body)


def pack_terms_kernel(found, terms, *outs):
    for want in range(16):
        at = found[want] - 16

        @pl.when(at >= 0)
        def _():
            for lane, out in enumerate(outs):

                @pl.when(jnp.logical_and(at >= lane * CAP, at < lane * CAP + CAP))
                def _():
                    out[at - lane * CAP] = terms[want]


def add_terms_kernel(sent, found, terms, *refs):
    near, before, (mine, partner, held) = refs[:3], refs[3:-3], refs[-3:]
    mine[...] = before[0][...] if before else jnp.zeros((8, ROW, ROW), F32)
    held[...] = before[1][...].astype(F32) if before else jnp.zeros((8, ROW, ROW), F32)

    def add(row, term):
        @pl.when(row < 8)
        def _():
            mine[row] = mine[row] + term[...].astype(F32)

        @pl.when(row >= 8)
        def _():
            held[row - 8] = held[row - 8] + term[...].astype(F32)

    for want in range(16):
        at = found[want]

        @pl.when(jnp.logical_and(at >= 0, at < 16))
        def _():
            add(at, terms.at[want])

    for lane in range(3):
        for n in range(CAP):
            row = sent[lane * CAP + n]

            @pl.when(row >= 0)
            def _():
                add(row, near[lane].at[n])

    partner[...] = held[...].astype(BF16)


def target_kernel(place, pair_src, pair_tgt, shares, rows, held):
    z, x = place[0], place[1]
    quad = lax.shift_right_logical(z, 2)
    for p in range(4):
        z_own, _ = want_of(pair_src, z, x, 4 * quad + p)
        ahead = lax.bitwise_and(z - z_own, 3)
        relay = ring(z_own + jnp.where(ahead == 3, -1, ahead))
        held[p] = shares[4 * lax.shift_right_logical(relay, 2) + p].astype(F32)
    for p in range(4):
        same = jnp.zeros((ROW, ROW), F32)
        for other in range(4):
            hit = pair_tgt[p // 2, p % 2] == pair_tgt[other // 2, other % 2]
            same = same + jnp.where(hit, held[other], 0.0)
        rows[p] = same.astype(BF16)


def shift(value, steps):
    pairs = [(2 * z + x, 2 * ((z + steps) % RING) + x) for z in range(RING) for x in range(2)]
    return lax.ppermute(value, "band", pairs)


def across(value):
    return lax.ppermute(value, "band", [(i, i ^ 1) for i in range(32)])


def along_ring(value):
    groups = [[8 * quad + member for quad in range(4)] for member in range(8)]
    return lax.all_to_all(value, "band", 0, 0, axis_index_groups=groups, tiled=True)


def rounds_of(pair_src):
    band = jnp.arange(pair_src.shape[1], dtype=jnp.int32) // 2
    z, x = band // 2, band % 2
    z_own = pair_src // 8
    key = (z_own * 8 + (z % 4) * 2 + x).reshape(-1)
    moves = ((z_own - z) % 4 != 0).astype(jnp.int32).reshape(-1)
    shared = moves * jnp.sum((key[:, None] == key[None, :]).astype(jnp.int32), axis=1)
    return jnp.maximum(1, (jnp.max(shared) + CAP - 1) // CAP)


def per_device(targets, sources, pair_tgt, pair_src):
    table = {name: jnp.asarray(value) for name, value in tables().items()}
    band = lax.axis_index("band")
    rounds = rounds_of(pair_src)
    sixteen = struct((16, ROW, ROW), BF16)
    packets = [struct((CAP, ROW, ROW), BF16)] * 3

    def place_in(turn):
        turn = jnp.asarray(turn, jnp.int32)
        return jnp.stack([band // 2, band % 2, turn]).astype(jnp.int32)

    def sent_in(turn):
        return smem_call(sent_kernel, 3 * CAP, place_in(turn), pair_src)

    def found_in(turn):
        return smem_call(found_kernel, 16, place_in(turn), pair_src)

    ids = pair_tgt.reshape(4)
    wanted = targets[ids].reshape(4, ROW, ROW)
    wanted = along_ring(jnp.concatenate([wanted] * 4, axis=0))

    own = sources.reshape(8, ROW, ROW)
    other = across(own)

    def deliver(sent, found, before):
        packed = vmem_call(pack_rows_kernel, packets, (sent, own, other), scalars=1)
        near = tuple(shift(packet, step) for packet, step in zip(packed, STEPS))
        operands = (found, own, other) + near + before
        return vmem_call(place_rows_kernel, [sixteen], operands, scalars=1)[0]

    sent, found = sent_in(0), found_in(0)
    rows = lax.fori_loop(
        1,
        rounds,
        lambda turn, before: deliver(sent_in(turn), found_in(turn), (before,)),
        deliver(sent, found, ()),
    )
    where = (place_in(0), pair_src)
    (spectra,) = vmem_call(
        density_kernel,
        [sixteen],
        where + (rows, wanted, table["z_fwd"], table["y_fwd"]),
        scalars=2,
    )
    slabs = lax.all_to_all(spectra, "dom", 0, 0, tiled=True)
    (solved,) = vmem_call(
        solve_kernel,
        [sixteen],
        (slabs, table["spectrum"], table["x_fwd"], table["x_bwd"]),
        scratch=[pltpu.VMEM((8, 256, ROW), F32)] * 3,
    )
    back = lax.all_to_all(solved, "dom", 0, 0, tiled=True)
    terms, shares = vmem_call(
        term_kernel,
        [sixteen, sixteen],
        where + (back, rows, wanted, table["z_bwd"], table["y_bwd"]),
        scalars=2,
    )
    shares = along_ring(shares)

    def collect(sent, found, before):
        packed = vmem_call(pack_terms_kernel, packets, (found, terms), scalars=1)
        near = tuple(shift(packet, -step) for packet, step in zip(packed, STEPS))
        outs = [struct((8, ROW, ROW), F32), struct((8, ROW, ROW), BF16)]
        operands = (sent, found, terms) + near + before
        scratch = [pltpu.VMEM((8, ROW, ROW), F32)]
        return vmem_call(add_terms_kernel, outs, operands, scalars=2, scratch=scratch)

    mine, partner = lax.fori_loop(
        1,
        rounds,
        lambda turn, before: collect(sent_in(turn), found_in(turn), tuple(before)),
        collect(sent, found, ()),
    )
    owned = (mine + across(partner).astype(F32)).astype(BF16).reshape(sources.shape)

    (target_rows,) = vmem_call(
        target_kernel,
        [struct((4, ROW, ROW), BF16)],
        where + (pair_tgt, shares),
        scalars=3,
        scratch=[pltpu.VMEM((4, ROW, ROW), F32)],
    )
    flat = target_rows.reshape(4, targets.shape[1])
    slots = jnp.arange(targets.shape[0], dtype=jnp.int32)[:, None]
    summed = jnp.zeros(targets.shape, BF16)
    for p in range(4):
        summed = jnp.where(slots == ids[p], flat[p][None, :], summed)
    return summed, owned


def solution(mesh):
    return jax.shard_map(
        per_device,
        mesh=mesh,
        in_specs=(P("band", "dom"), P(None, "band", "dom"), P(None, "band"), P()),
        out_specs=(P("band", "dom"), P(None, "band", "dom")),
        check_vma=False,
    )
```

```python
import numpy as np
import jax
import jax.numpy as jnp
from jax import lax
from jax.experimental import pallas as pl
from jax.experimental.pallas import tpu as pltpu
from jax.sharding import PartitionSpec as P

SIDE = 64
SWEEPS = 8
RING = 16
CAP = 6
LANES = 3
ROW = 128
HALF = 64
VMEM_LIMIT = 48 * 1024 * 1024
F32 = jnp.float32
BF16 = jnp.bfloat16


def eigen_system():
    line = np.zeros((SIDE, SIDE))
    for delta, weight in ((0, 30.0), (1, -16.0), (2, 1.0)):
        for i in range(SIDE - delta):
            line[i, i + delta] = weight / 12.0
            line[i + delta, i] = weight / 12.0
    values, vectors = np.linalg.eigh(line)
    return values, vectors * np.where(vectors[0] < 0, -1.0, 1.0)[None, :]


def halves(matrix):
    high = np.asarray(matrix, np.float32).astype(jnp.bfloat16)
    low = (np.asarray(matrix, np.float64) - high.astype(np.float64)).astype(jnp.bfloat16)
    return np.stack([high, low])


def tables():
    values, v = eigen_system()
    along_z = np.kron(np.eye(2), v)
    even, odd = v[0::2], v[1::2]
    fwd = np.zeros((2, 32, 4, 2, 4, 32))
    bwd = np.zeros((2, 4, 32, 2, 32, 4))
    for x in range(4):
        fwd[0, :, x, 0, x, :] = even[:, 0::2].T
        fwd[0, :, x, 1, x, :] = odd[:, 0::2].T
        fwd[1, :, x, 0, x, :] = odd[:, 1::2].T
        fwd[1, :, x, 1, x, :] = even[:, 1::2].T
        bwd[0, x, :, 0, :, x] = even[:, 0::2]
        bwd[0, x, :, 1, :, x] = even[:, 1::2]
        bwd[1, x, :, 0, :, x] = odd[:, 1::2]
        bwd[1, x, :, 1, :, x] = odd[:, 0::2]
    along_x = np.zeros((2, SIDE, RING, 2, 4))
    for pick in range(2):
        along_x[pick, :, :, pick, :] = v.T.reshape(SIDE, RING, 4)
    rows = np.arange(SIDE).reshape(16, 2, 1, 2, 1)
    spectrum = values[rows] + values.reshape(1, 1, SIDE, 1, 1) + values.reshape(1, 1, 1, 1, SIDE)
    return dict(
        z_fwd=halves(along_z),
        z_bwd=halves(along_z.T),
        y_fwd=halves(fwd.reshape(256, 256)),
        y_bwd=halves(bwd.reshape(256, 256)),
        x_fwd=halves(along_x.reshape(ROW, ROW)),
        x_bwd=halves(along_x.reshape(ROW, ROW).T),
        spectrum=spectrum.reshape(8, 256, ROW).astype(np.float32),
    )


def split(value):
    high = value.astype(BF16)
    return high, (value - high.astype(F32)).astype(BF16)


def mm(left, right):
    return jnp.dot(left, right, preferred_element_type=F32)


def left_mul(table, value):
    high, low = split(value)
    return mm(table[0], high) + mm(table[0], low) + mm(table[1], high)


def right_mul(value, table):
    high, low = split(value)
    return mm(high, table[0]) + mm(low, table[0]) + mm(high, table[1])


def swap_halves(value):
    return jnp.concatenate([value[:, HALF:], value[:, :HALF]], axis=1)


def by_half(both):
    lane = lax.broadcasted_iota(jnp.int32, (ROW, ROW), 1)
    return jnp.where(lane < HALF, both[:ROW], both[ROW:])


def vmem_call(kernel, outs, operands, scalars=0, scratch=()):
    whole = pl.BlockSpec(memory_space=pltpu.VMEM)
    smem = pl.BlockSpec(memory_space=pltpu.SMEM)
    return pl.pallas_call(
        kernel,
        out_shape=outs,
        in_specs=[smem] * scalars + [whole] * (len(operands) - scalars),
        out_specs=[whole] * len(outs),
        scratch_shapes=list(scratch),
        compiler_params=pltpu.CompilerParams(vmem_limit_bytes=VMEM_LIMIT),
    )(*operands)


def smem_call(kernel, size, *operands):
    smem = pl.BlockSpec(memory_space=pltpu.SMEM)
    return pl.pallas_call(
        kernel,
        out_shape=struct((size,), jnp.int32),
        in_specs=[smem] * len(operands),
        out_specs=smem,
    )(*operands)


def struct(shape, dtype):
    return jax.ShapeDtypeStruct(shape, dtype)


def ring(value):
    return lax.bitwise_and(value, RING - 1)


def far_step(z):
    return 2 - 4 * lax.bitwise_and(z, 1)


def steps_of(z):
    return 1, -1, far_step(z)


def want_of(pair_src, z, x, want):
    quad, slot = lax.shift_right_logical(want, 2), lax.bitwise_and(want, 3)
    block = lax.shift_right_logical(slot, 1)
    band = 2 * (4 * quad + lax.bitwise_and(z, 3)) + x
    source = pair_src[block, 2 * band + lax.bitwise_and(slot, 1)]
    z_own = lax.shift_right_logical(source, 3)
    other = lax.bitwise_xor(lax.bitwise_and(lax.shift_right_logical(source, 2), 1), x)
    return z_own, 8 * other + 4 * block + lax.bitwise_and(source, 3)


def wants_of(pair_src, z, x):
    for want in range(16):
        yield (want,) + want_of(pair_src, z, x, jnp.int32(want))


def in_round(hit, count):
    return jnp.logical_and(hit, jnp.logical_and(count >= 0, count < CAP))


def sent_kernel(place, pair_src, sent):
    z, x = place[0], place[1]
    for lane, step in enumerate(steps_of(z)):
        for n in range(CAP):
            sent[lane * CAP + n] = -1
        count = -CAP * place[2]
        for _, z_own, row in wants_of(pair_src, z + step, x):
            hit = z_own == z

            @pl.when(in_round(hit, count))
            def _():
                sent[lane * CAP + count] = row

            count = count + hit.astype(jnp.int32)


def found_kernel(place, pair_src, found):
    z, x, turn = place[0], place[1], place[2]
    counts = [-CAP * turn] * LANES
    for want, z_own, row in wants_of(pair_src, z, x):
        at = jnp.where(jnp.logical_and(z_own == z, turn == 0), row, -1)
        for lane, step in enumerate(steps_of(z)):
            hit = z_own == ring(z - step)
            at = jnp.where(in_round(hit, counts[lane]), 16 + lane * CAP + counts[lane], at)
            counts[lane] = counts[lane] + hit.astype(jnp.int32)
        found[want] = at


def pack_rows_kernel(sent, own, other, *outs):
    for lane, out in enumerate(outs):
        for n in range(CAP):
            row = sent[lane * CAP + n]

            @pl.when(row >= 0)
            def _():
                @pl.when(row < 8)
                def _():
                    out[n] = own[row]

                @pl.when(row >= 8)
                def _():
                    out[n] = other[row - 8]


def place_rows_kernel(found, own, other, *refs):
    out = refs[-1]
    for before in refs[3:-1]:
        out[...] = before[...]
    spans = [(own, 0, 8), (other, 8, 16)]
    spans += [(near, 16 + lane * CAP, 16 + lane * CAP + CAP) for lane, near in enumerate(refs[:3])]
    for want in range(16):
        at = found[want]

        @pl.when(at >= 0)
        def _():
            for rows, first, last in spans:

                @pl.when(jnp.logical_and(at >= first, at < last))
                def _():
                    out[want] = rows[at - first]


def for_each_solved(place, pair_src, body):
    z, x = place[0], place[1]

    def step(want, carry):
        z_own, _ = want_of(pair_src, z, x, want)
        near = jnp.logical_or(ring(z - z_own + 1) <= 2, ring(z - z_own) == ring(far_step(z)))

        @pl.when(near)
        def _():
            body(want)

        return carry

    lax.fori_loop(0, 16, step, 0)


def density_kernel(place, pair_src, sources, wanted, z_fwd, y_fwd, spectra):
    def body(want):
        density = sources[want].astype(F32) * wanted[want].astype(F32)
        along = right_mul(density, z_fwd)
        mixed = left_mul(y_fwd, jnp.concatenate([along, swap_halves(along)], axis=0))
        spectra[want] = by_half(mixed).astype(BF16)

    for_each_solved(place, pair_src, body)


def solve_kernel(slabs, spectrum, x_fwd, x_bwd, out, residual, direction, total):
    def dot_of(value):
        return jnp.sum(value.reshape(32, 8, ROW), axis=0)

    zero = jnp.zeros((8, ROW), F32)

    def start(j, carry):
        norm, power = carry
        part = slabs[:, pl.ds(pl.multiple_of(16 * j, 16), 16), :].astype(F32)
        part = [part[:, :8].reshape(ROW, ROW), part[:, 8:].reshape(ROW, ROW)]
        part = jnp.concatenate(part, axis=1).astype(BF16)
        value = mm(x_fwd[0], part) + mm(x_fwd[1], part)
        value = jnp.concatenate([value[:, :ROW], value[:, ROW:]], axis=0)
        direction[j] = value
        square = value * value
        return norm + dot_of(square), power + dot_of(square * spectrum[j])

    norm, power = lax.fori_loop(0, 8, start, (zero, zero))
    norm, power = jnp.sum(norm), jnp.sum(power)
    step, ratio = norm / power, jnp.float32(0.0)
    for sweep in range(SWEEPS - 1):

        def advance(j, carry, sweep=sweep, step=step, ratio=ratio):
            new, power = carry
            lam = spectrum[j]
            if sweep == 0:
                d = direction[j]
                r = d - step * (lam * d)
                total[j] = step * d
            else:
                r = residual[j]
                d = r + ratio * direction[j]
                r = r - step * (lam * d)
                direction[j] = d
                total[j] = total[j] + step * d
            residual[j] = r
            square = r * r
            return new + dot_of(square), power + dot_of(square * lam)

        new, power = lax.fori_loop(0, 8, advance, (zero, zero))
        new, power = jnp.sum(new), jnp.sum(power)
        ratio = new / norm
        step = new / (power - ratio * new / step)
        norm = new

    def finish(j, carry):
        value = total[j] + step * (residual[j] + ratio * direction[j])
        part = left_mul(x_bwd, jnp.concatenate([value[:ROW], value[ROW:]], axis=1))
        part = [part[:, :ROW].reshape(RING, 8, ROW), part[:, ROW:].reshape(RING, 8, ROW)]
        part = jnp.concatenate(part, axis=1)
        out[:, pl.ds(pl.multiple_of(16 * j, 16), 16), :] = part.astype(out.dtype)
        return carry

    lax.fori_loop(0, 8, finish, 0)


def term_kernel(place, pair_src, spectra, sources, wanted, z_bwd, y_bwd, terms, shares):
    def body(want):
        rows = spectra[want]
        rows = jnp.concatenate([rows, swap_halves(rows)], axis=0)
        potential = right_mul(by_half(mm(y_bwd[0], rows) + mm(y_bwd[1], rows)), z_bwd)
        terms[want] = (-potential * wanted[want].astype(F32)).astype(BF16)
        shares[want] = (-potential * sources[want].astype(F32)).astype(BF16)

    for_each_solved(place, pair_src, body)


def pack_terms_kernel(found, terms, *outs):
    for want in range(16):
        at = found[want] - 16

        @pl.when(at >= 0)
        def _():
            for lane, out in enumerate(outs):

                @pl.when(jnp.logical_and(at >= lane * CAP, at < lane * CAP + CAP))
                def _():
                    out[at - lane * CAP] = terms[want]


def add_terms_kernel(sent, found, terms, *refs):
    near, before, (mine, partner, held) = refs[:3], refs[3:-3], refs[-3:]
    mine[...] = before[0][...] if before else jnp.zeros((8, ROW, ROW), F32)
    held[...] = before[1][...].astype(F32) if before else jnp.zeros((8, ROW, ROW), F32)

    def add(row, term):
        @pl.when(row < 8)
        def _():
            mine[row] = mine[row] + term[...].astype(F32)

        @pl.when(row >= 8)
        def _():
            held[row - 8] = held[row - 8] + term[...].astype(F32)

    for want in range(16):
        at = found[want]

        @pl.when(jnp.logical_and(at >= 0, at < 16))
        def _():
            add(at, terms.at[want])

    for lane in range(3):
        for n in range(CAP):
            row = sent[lane * CAP + n]

            @pl.when(row >= 0)
            def _():
                add(row, near[lane].at[n])

    partner[...] = held[...].astype(BF16)


def target_kernel(place, pair_src, pair_tgt, shares, rows, held):
    z, x = place[0], place[1]
    quad = lax.shift_right_logical(z, 2)
    for p in range(4):
        z_own, _ = want_of(pair_src, z, x, 4 * quad + p)
        ahead = lax.bitwise_and(z - z_own, 3)
        relay = ring(z_own + jnp.where(ahead == 3, -1, jnp.where(ahead == 2, far_step(z_own), ahead)))
        held[p] = shares[4 * lax.shift_right_logical(relay, 2) + p].astype(F32)
    for p in range(4):
        same = jnp.zeros((ROW, ROW), F32)
        for other in range(4):
            hit = pair_tgt[p // 2, p % 2] == pair_tgt[other // 2, other % 2]
            same = same + jnp.where(hit, held[other], 0.0)
        rows[p] = same.astype(BF16)


def hand_over(packets, sign):
    moves = (lambda z: 1, lambda z: -1, far_step_of)
    return tuple(
        lax.ppermute(
            packet,
            "band",
            [(2 * z + x, 2 * ((z + sign * move(z)) % RING) + x) for z in range(RING) for x in range(2)],
        )
        for packet, move in zip(packets, moves)
    )


def far_step_of(z):
    return -2 if z % 2 else 2


def across(value):
    return lax.ppermute(value, "band", [(i, i ^ 1) for i in range(32)])


def along_ring(value):
    groups = [[8 * quad + member for quad in range(4)] for member in range(8)]
    return lax.all_to_all(value, "band", 0, 0, axis_index_groups=groups, tiled=True)


def rounds_of(pair_src):
    band = jnp.arange(pair_src.shape[1], dtype=jnp.int32) // 2
    z, x = band // 2, band % 2
    z_own = pair_src // 8
    key = (z_own * 8 + (z % 4) * 2 + x).reshape(-1)
    moves = ((z_own - z) % 4 != 0).astype(jnp.int32).reshape(-1)
    shared = moves * jnp.sum((key[:, None] == key[None, :]).astype(jnp.int32), axis=1)
    return jnp.maximum(1, (jnp.max(shared) + CAP - 1) // CAP)


def per_device(targets, sources, pair_tgt, pair_src):
    table = {name: jnp.asarray(value) for name, value in tables().items()}
    band = lax.axis_index("band")
    rounds = rounds_of(pair_src)
    sixteen = struct((16, ROW, ROW), BF16)
    packets = [struct((CAP, ROW, ROW), BF16)] * 3

    def place_in(turn):
        turn = jnp.asarray(turn, jnp.int32)
        return jnp.stack([band // 2, band % 2, turn]).astype(jnp.int32)

    def sent_in(turn):
        return smem_call(sent_kernel, 3 * CAP, place_in(turn), pair_src)

    def found_in(turn):
        return smem_call(found_kernel, 16, place_in(turn), pair_src)

    own, ids = lax.optimization_barrier((sources.reshape(8, ROW, ROW), pair_tgt.reshape(4)))
    other = across(own)
    wanted = targets[ids].reshape(4, ROW, ROW)
    wanted = along_ring(jnp.concatenate([wanted] * 4, axis=0))

    def deliver(sent, found, before):
        packed = vmem_call(pack_rows_kernel, packets, (sent, own, other), scalars=1)
        near = hand_over(packed, 1)
        operands = (found, own, other) + near + before
        return vmem_call(place_rows_kernel, [sixteen], operands, scalars=1)[0]

    sent, found = sent_in(0), found_in(0)
    rows = lax.fori_loop(
        1,
        rounds,
        lambda turn, before: deliver(sent_in(turn), found_in(turn), (before,)),
        deliver(sent, found, ()),
    )
    where = (place_in(0), pair_src)
    (spectra,) = vmem_call(
        density_kernel,
        [sixteen],
        where + (rows, wanted, table["z_fwd"], table["y_fwd"]),
        scalars=2,
    )
    slabs = lax.all_to_all(spectra, "dom", 0, 0, tiled=True)
    (solved,) = vmem_call(
        solve_kernel,
        [sixteen],
        (slabs, table["spectrum"], table["x_fwd"], table["x_bwd"]),
        scratch=[pltpu.VMEM((8, 256, ROW), F32)] * 3,
    )
    back = lax.all_to_all(solved, "dom", 0, 0, tiled=True)
    terms, shares = vmem_call(
        term_kernel,
        [sixteen, sixteen],
        where + (back, rows, wanted, table["z_bwd"], table["y_bwd"]),
        scalars=2,
    )

    def give_back(found):
        return hand_over(vmem_call(pack_terms_kernel, packets, (found, terms), scalars=1), -1)

    def collect(sent, found, near, before):
        outs = [struct((8, ROW, ROW), F32), struct((8, ROW, ROW), BF16)]
        operands = (sent, found, terms) + near + before
        scratch = [pltpu.VMEM((8, ROW, ROW), F32)]
        return vmem_call(add_terms_kernel, outs, operands, scalars=2, scratch=scratch)

    def collect_in(turn, before):
        found = found_in(turn)
        return collect(sent_in(turn), found, give_back(found), tuple(before))

    near = give_back(found)
    near, shares = lax.optimization_barrier((near, shares))
    shares = along_ring(shares)
    mine, partner = lax.fori_loop(1, rounds, collect_in, collect(sent, found, near, ()))
    owned = (mine + across(partner).astype(F32)).astype(BF16).reshape(sources.shape)

    (target_rows,) = vmem_call(
        target_kernel,
        [struct((4, ROW, ROW), BF16)],
        where + (pair_tgt, shares),
        scalars=3,
        scratch=[pltpu.VMEM((4, ROW, ROW), F32)],
    )
    flat = target_rows.reshape(4, targets.shape[1])
    slots = jnp.arange(targets.shape[0], dtype=jnp.int32)[:, None]
    summed = jnp.zeros(targets.shape, BF16)
    for p in range(4):
        summed = jnp.where(slots == ids[p], flat[p][None, :], summed)
    return summed, owned


def solution(mesh):
    return jax.shard_map(
        per_device,
        mesh=mesh,
        in_specs=(P("band", "dom"), P(None, "band", "dom"), P(None, "band"), P()),
        out_specs=(P("band", "dom"), P(None, "band", "dom")),
        check_vma=False,
    )
```

```python
import numpy as np
import jax
import jax.numpy as jnp
from jax import lax
from jax.experimental import pallas as pl
from jax.experimental.pallas import tpu as pltpu
from jax.sharding import PartitionSpec as P

SIDE = 64
SWEEPS = 8
RING = 16
HOP = 5
CAPS = (5, 5, 5, 5, 3)
STARTS = (0, 5, 10, 15, 20)
WANTS = 12
ROW = 128
HALF = 64
VMEM_LIMIT = 48 * 1024 * 1024
F32 = jnp.float32
BF16 = jnp.bfloat16


def eigen_system():
    line = np.zeros((SIDE, SIDE))
    for delta, weight in ((0, 30.0), (1, -16.0), (2, 1.0)):
        for i in range(SIDE - delta):
            line[i, i + delta] = weight / 12.0
            line[i + delta, i] = weight / 12.0
    values, vectors = np.linalg.eigh(line)
    return values, vectors * np.where(vectors[0] < 0, -1.0, 1.0)[None, :]


def halves(matrix):
    high = np.asarray(matrix, np.float32).astype(jnp.bfloat16)
    low = (np.asarray(matrix, np.float64) - high.astype(np.float64)).astype(jnp.bfloat16)
    return np.stack([high, low])


def tables():
    values, v = eigen_system()
    along_z = np.kron(np.eye(2), v)
    even, odd = v[0::2], v[1::2]
    fwd = np.zeros((2, 32, 4, 2, 4, 32))
    bwd = np.zeros((2, 4, 32, 2, 32, 4))
    for x in range(4):
        fwd[0, :, x, 0, x, :] = even[:, 0::2].T
        fwd[0, :, x, 1, x, :] = odd[:, 0::2].T
        fwd[1, :, x, 0, x, :] = odd[:, 1::2].T
        fwd[1, :, x, 1, x, :] = even[:, 1::2].T
        bwd[0, x, :, 0, :, x] = even[:, 0::2]
        bwd[0, x, :, 1, :, x] = even[:, 1::2]
        bwd[1, x, :, 0, :, x] = odd[:, 1::2]
        bwd[1, x, :, 1, :, x] = odd[:, 0::2]
    along_x = np.zeros((2, SIDE, RING, 2, 4))
    for pick in range(2):
        along_x[pick, :, :, pick, :] = v.T.reshape(SIDE, RING, 4)
    rows = np.arange(SIDE).reshape(16, 2, 1, 2, 1)
    spectrum = values[rows] + values.reshape(1, 1, SIDE, 1, 1) + values.reshape(1, 1, 1, 1, SIDE)
    return dict(
        z_fwd=halves(along_z),
        z_bwd=halves(along_z.T),
        y_fwd=halves(fwd.reshape(256, 256)),
        y_bwd=halves(bwd.reshape(256, 256)),
        x_fwd=halves(along_x.reshape(ROW, ROW)),
        x_bwd=halves(along_x.reshape(ROW, ROW).T),
        spectrum=spectrum.reshape(8, 256, ROW).astype(np.float32),
    )


def split(value):
    high = value.astype(BF16)
    return high, (value - high.astype(F32)).astype(BF16)


def mm(left, right):
    return jnp.dot(left, right, preferred_element_type=F32)


def left_mul(table, value):
    high, low = split(value)
    return mm(table[0], high) + mm(table[0], low) + mm(table[1], high)


def right_mul(value, table):
    high, low = split(value)
    return mm(high, table[0]) + mm(low, table[0]) + mm(high, table[1])


def swap_halves(value):
    return jnp.concatenate([value[:, HALF:], value[:, :HALF]], axis=1)


def by_half(both):
    lane = lax.broadcasted_iota(jnp.int32, (ROW, ROW), 1)
    return jnp.where(lane < HALF, both[:ROW], both[ROW:])


def vmem_call(kernel, outs, operands, scalars=0, scratch=()):
    whole = pl.BlockSpec(memory_space=pltpu.VMEM)
    smem = pl.BlockSpec(memory_space=pltpu.SMEM)
    return pl.pallas_call(
        kernel,
        out_shape=outs,
        in_specs=[smem] * scalars + [whole] * (len(operands) - scalars),
        out_specs=[whole] * len(outs),
        scratch_shapes=list(scratch),
        compiler_params=pltpu.CompilerParams(vmem_limit_bytes=VMEM_LIMIT),
    )(*operands)


def smem_call(kernel, size, *operands):
    smem = pl.BlockSpec(memory_space=pltpu.SMEM)
    return pl.pallas_call(
        kernel,
        out_shape=struct((size,), jnp.int32),
        in_specs=[smem] * len(operands),
        out_specs=smem,
    )(*operands)


def struct(shape, dtype):
    return jax.ShapeDtypeStruct(shape, dtype)


def ring(value):
    return lax.bitwise_and(value, RING - 1)


def far_step(z):
    return 6 * lax.bitwise_and(z, 1) - 3


def steps_of(z):
    return 1, -1, 2, -2, far_step(z)


def far_kind(relay):
    return 2 - lax.bitwise_and(relay, 1)


def want_of(pair_src, z, x, want):
    kind, slot = lax.shift_right_logical(want, 2), lax.bitwise_and(want, 3)
    block = lax.shift_right_logical(slot, 1)
    band = 2 * ring(z + HOP * (jnp.where(kind == 2, 1, 0) - jnp.where(kind == 1, 1, 0))) + x
    source = pair_src[block, 2 * band + lax.bitwise_and(slot, 1)]
    z_own = lax.shift_right_logical(source, 3)
    other = lax.bitwise_xor(lax.bitwise_and(lax.shift_right_logical(source, 2), 1), x)
    return z_own, 8 * other + 4 * block + lax.bitwise_and(source, 3)


def wants_of(pair_src, z, x):
    for want in range(WANTS):
        yield (want,) + want_of(pair_src, z, x, jnp.int32(want))


def on_lane(lane, relay, want, hit):
    return hit if lane < 4 else jnp.logical_and(hit, far_kind(relay) == want // 4)


def in_round(lane, hit, count):
    return jnp.logical_and(hit, jnp.logical_and(count >= 0, count < CAPS[lane]))


def sent_kernel(place, pair_src, sent):
    z, x = place[0], place[1]
    for lane, step in enumerate(steps_of(z)):
        for n in range(CAPS[lane]):
            sent[STARTS[lane] + n] = -1
        count = -CAPS[lane] * place[2]
        for want, z_own, row in wants_of(pair_src, z + step, x):
            hit = on_lane(lane, z + step, want, z_own == z)

            @pl.when(in_round(lane, hit, count))
            def _():
                sent[STARTS[lane] + count] = row

            count = count + hit.astype(jnp.int32)


def found_kernel(place, pair_src, found):
    z, x, turn = place[0], place[1], place[2]
    counts = [-cap * turn for cap in CAPS]
    for want, z_own, row in wants_of(pair_src, z, x):
        at = jnp.where(jnp.logical_and(z_own == z, turn == 0), row, -1)
        for lane, step in enumerate(steps_of(z)):
            owner = ring(z - step if lane < 4 else z + step)
            hit = on_lane(lane, z, want, z_own == owner)
            at = jnp.where(in_round(lane, hit, counts[lane]), 16 + STARTS[lane] + counts[lane], at)
            counts[lane] = counts[lane] + hit.astype(jnp.int32)
        found[want] = at


def pack_rows_kernel(sent, own, other, *outs):
    for lane, out in enumerate(outs):
        for n in range(CAPS[lane]):
            row = sent[STARTS[lane] + n]

            @pl.when(row >= 0)
            def _():
                @pl.when(row < 8)
                def _():
                    out[n] = own[row]

                @pl.when(row >= 8)
                def _():
                    out[n] = other[row - 8]


def place_rows_kernel(found, own, other, *refs):
    out = refs[-1]
    for before in refs[5:-1]:
        out[...] = before[...]
    spans = [(own, 0, 8), (other, 8, 16)]
    spans += [(near, 16 + first, 16 + first + cap) for near, first, cap in zip(refs, STARTS, CAPS)]
    for want in range(WANTS):
        at = found[want]

        @pl.when(at >= 0)
        def _():
            for rows, first, last in spans:

                @pl.when(jnp.logical_and(at >= first, at < last))
                def _():
                    out[want] = rows[at - first]


def for_each_solved(place, pair_src, body):
    z, x = place[0], place[1]
    for kind in range(3):

        def step(slot, carry, kind=kind):
            want = 4 * kind + slot
            z_own, _ = want_of(pair_src, z, x, want)
            here = ring(z_own - z + 2) <= 4
            if kind:
                far = ring(z_own - z) == ring(far_step(z))
                here = jnp.logical_or(here, jnp.logical_and(far, far_kind(z) == kind))

            @pl.when(here)
            def _():
                body(kind, slot, want)

            return carry

        lax.fori_loop(0, 4, step, 0)


def density_kernel(place, pair_src, sources, here, below, above, z_fwd, y_fwd, spectra):
    wanted = (here, below, above)

    def body(kind, slot, want):
        density = sources[want].astype(F32) * wanted[kind][slot].astype(F32)
        along = right_mul(density, z_fwd)
        mixed = left_mul(y_fwd, jnp.concatenate([along, swap_halves(along)], axis=0))
        spectra[want] = by_half(mixed).astype(BF16)

    for_each_solved(place, pair_src, body)


def solve_kernel(slabs, spectrum, x_fwd, x_bwd, out, residual, direction, total):
    def dot_of(value):
        return jnp.sum(value.reshape(32, 8, ROW), axis=0)

    zero = jnp.zeros((8, ROW), F32)

    def start(j, carry):
        norm, power = carry
        part = slabs[:, pl.ds(pl.multiple_of(16 * j, 16), 16), :].astype(F32)
        part = [part[:, :8].reshape(ROW, ROW), part[:, 8:].reshape(ROW, ROW)]
        part = jnp.concatenate(part, axis=1).astype(BF16)
        value = mm(x_fwd[0], part) + mm(x_fwd[1], part)
        value = jnp.concatenate([value[:, :ROW], value[:, ROW:]], axis=0)
        direction[j] = value
        square = value * value
        return norm + dot_of(square), power + dot_of(square * spectrum[j])

    norm, power = lax.fori_loop(0, 8, start, (zero, zero))
    norm, power = jnp.sum(norm), jnp.sum(power)
    step, ratio = norm / power, jnp.float32(0.0)
    for sweep in range(SWEEPS - 1):

        def advance(j, carry, sweep=sweep, step=step, ratio=ratio):
            new, power = carry
            lam = spectrum[j]
            if sweep == 0:
                d = direction[j]
                r = d - step * (lam * d)
                total[j] = step * d
            else:
                r = residual[j]
                d = r + ratio * direction[j]
                r = r - step * (lam * d)
                direction[j] = d
                total[j] = total[j] + step * d
            residual[j] = r
            square = r * r
            return new + dot_of(square), power + dot_of(square * lam)

        new, power = lax.fori_loop(0, 8, advance, (zero, zero))
        new, power = jnp.sum(new), jnp.sum(power)
        ratio = new / norm
        step = new / (power - ratio * new / step)
        norm = new

    def finish(j, carry):
        value = total[j] + step * (residual[j] + ratio * direction[j])
        part = left_mul(x_bwd, jnp.concatenate([value[:ROW], value[ROW:]], axis=1))
        part = [part[:, :ROW].reshape(RING, 8, ROW), part[:, ROW:].reshape(RING, 8, ROW)]
        part = jnp.concatenate(part, axis=1)
        out[:, pl.ds(pl.multiple_of(16 * j, 16), 16), :] = part.astype(out.dtype)
        return carry

    lax.fori_loop(0, 8, finish, 0)


def term_kernel(place, pair_src, spectra, here, below, above, z_bwd, y_bwd, terms, potentials):
    wanted = (here, below, above)

    def body(kind, slot, want):
        rows = spectra[want]
        rows = jnp.concatenate([rows, swap_halves(rows)], axis=0)
        potential = right_mul(by_half(mm(y_bwd[0], rows) + mm(y_bwd[1], rows)), z_bwd)
        terms[want] = (-potential * wanted[kind][slot].astype(F32)).astype(BF16)
        potentials[want] = potential

    for_each_solved(place, pair_src, body)


def share_kernel(place, pair_src, potentials, sources, *shares):
    def body(kind, slot, want):
        shares[kind][slot] = (-potentials[want] * sources[want].astype(F32)).astype(BF16)

    for_each_solved(place, pair_src, body)


def pack_terms_kernel(found, terms, *outs):
    for want in range(WANTS):
        at = found[want] - 16

        @pl.when(at >= 0)
        def _():
            for out, first, cap in zip(outs, STARTS, CAPS):

                @pl.when(jnp.logical_and(at >= first, at < first + cap))
                def _():
                    out[at - first] = terms[want]


def add_terms_kernel(sent, found, terms, *refs):
    near, before, (mine, partner, held) = refs[:5], refs[5:-3], refs[-3:]
    mine[...] = before[0][...] if before else jnp.zeros((8, ROW, ROW), F32)
    held[...] = before[1][...].astype(F32) if before else jnp.zeros((8, ROW, ROW), F32)

    def add(row, term):
        @pl.when(row < 8)
        def _():
            mine[row] = mine[row] + term[...].astype(F32)

        @pl.when(row >= 8)
        def _():
            held[row - 8] = held[row - 8] + term[...].astype(F32)

    for want in range(WANTS):
        at = found[want]

        @pl.when(jnp.logical_and(at >= 0, at < 16))
        def _():
            add(at, terms.at[want])

    for lane in range(5):
        for n in range(CAPS[lane]):
            row = sent[STARTS[lane] + n]

            @pl.when(row >= 0)
            def _():
                add(row, near[lane].at[n])

    partner[...] = held[...].astype(BF16)


def target_kernel(place, pair_src, pair_tgt, here, above, below, rows, held):
    z, x = place[0], place[1]
    for p in range(4):
        z_own, _ = want_of(pair_src, z, x, jnp.int32(p))
        away = ring(z_own - z + 2)
        up = jnp.logical_or(away < 10, jnp.logical_and(away == 10, lax.bitwise_and(z_own, 1) == 0))
        close = away <= 4

        @pl.when(close)
        def _():
            held[p] = here[p].astype(F32)

        @pl.when(jnp.logical_and(jnp.logical_not(close), up))
        def _():
            held[p] = above[p].astype(F32)

        @pl.when(jnp.logical_not(up))
        def _():
            held[p] = below[p].astype(F32)

    for p in range(4):
        same = jnp.zeros((ROW, ROW), F32)
        for other in range(4):
            hit = pair_tgt[p // 2, p % 2] == pair_tgt[other // 2, other % 2]
            same = same + jnp.where(hit, held[other], 0.0)
        rows[p] = same.astype(BF16)


def shift(value, move):
    pairs = [(2 * z + x, 2 * ((z + move(z)) % RING) + x) for z in range(RING) for x in range(2)]
    return lax.ppermute(value, "band", pairs)


def hand_over(packets, sign):
    moves = [lambda z, step=step: sign * step for step in (1, -1, 2, -2)]
    moves.append(lambda z: 3 if z % 2 else -3)
    return tuple(shift(packet, move) for packet, move in zip(packets, moves))


def across(value):
    return lax.ppermute(value, "band", [(i, i ^ 1) for i in range(32)])


def rounds_of(pair_src):
    band = jnp.arange(pair_src.shape[1], dtype=jnp.int32) // 2
    z, x = band // 2, band % 2
    z_own = pair_src // 8
    away = (z_own - z + 2) % RING
    relay = jnp.where(away <= 4, z, jnp.where(away < 10, z + HOP, z - HOP)) % RING
    far = away == 10
    relay = jnp.where(far, RING, relay)
    key = ((z_own * 32 + relay) * 2 + x).reshape(-1)
    shared = jnp.sum((key[:, None] == key[None, :]).astype(jnp.int32), axis=1).reshape(pair_src.shape)
    turns = jnp.where(far, (shared + CAPS[4] - 1) // CAPS[4], (shared + CAPS[0] - 1) // CAPS[0])
    return jnp.max(jnp.where(relay == z_own, 1, turns))


def per_device(targets, sources, pair_tgt, pair_src):
    table = {name: jnp.asarray(value) for name, value in tables().items()}
    band = lax.axis_index("band")
    rounds = rounds_of(pair_src)
    sixteen = struct((16, ROW, ROW), BF16)
    four = struct((4, ROW, ROW), BF16)
    packets = [struct((cap, ROW, ROW), BF16) for cap in CAPS]

    def place_in(turn):
        turn = jnp.asarray(turn, jnp.int32)
        return jnp.stack([band // 2, band % 2, turn]).astype(jnp.int32)

    def sent_in(turn):
        return smem_call(sent_kernel, sum(CAPS), place_in(turn), pair_src)

    def found_in(turn):
        return smem_call(found_kernel, 16, place_in(turn), pair_src)

    own, ids = lax.optimization_barrier((sources.reshape(8, ROW, ROW), pair_tgt.reshape(4)))
    other = across(own)
    wanted = targets[ids].reshape(4, ROW, ROW)
    other, wanted = lax.optimization_barrier((other, wanted))
    wanted = (wanted, shift(wanted, lambda z: HOP), shift(wanted, lambda z: -HOP))

    def deliver(sent, found, before):
        packed = vmem_call(pack_rows_kernel, packets, (sent, own, other), scalars=1)
        near = hand_over(packed, 1)
        operands = (found, own, other) + near + before
        return vmem_call(place_rows_kernel, [sixteen], operands, scalars=1)[0]

    sent, found = sent_in(0), found_in(0)
    rows = lax.fori_loop(
        1,
        rounds,
        lambda turn, before: deliver(sent_in(turn), found_in(turn), (before,)),
        deliver(sent, found, ()),
    )
    where = (place_in(0), pair_src)
    (spectra,) = vmem_call(
        density_kernel,
        [sixteen],
        where + (rows,) + wanted + (table["z_fwd"], table["y_fwd"]),
        scalars=2,
    )
    slabs = lax.all_to_all(spectra, "dom", 0, 0, tiled=True)
    (solved,) = vmem_call(
        solve_kernel,
        [sixteen],
        (slabs, table["spectrum"], table["x_fwd"], table["x_bwd"]),
        scratch=[pltpu.VMEM((8, 256, ROW), F32)] * 3,
    )
    back = lax.all_to_all(solved, "dom", 0, 0, tiled=True)
    terms, potentials = vmem_call(
        term_kernel,
        [sixteen, struct((16, ROW, ROW), F32)],
        where + (back,) + wanted + (table["z_bwd"], table["y_bwd"]),
        scalars=2,
    )

    def pack_in(found):
        return vmem_call(pack_terms_kernel, packets, (found, terms), scalars=1)

    def collect(sent, found, near, before):
        outs = [struct((8, ROW, ROW), F32), struct((8, ROW, ROW), BF16)]
        operands = (sent, found, terms) + near + before
        scratch = [pltpu.VMEM((8, ROW, ROW), F32)]
        return vmem_call(add_terms_kernel, outs, operands, scalars=2, scratch=scratch)

    def collect_in(turn, before):
        found = found_in(turn)
        return collect(sent_in(turn), found, hand_over(pack_in(found), -1), tuple(before))

    near = hand_over(pack_in(found), -1)
    last, potentials = lax.optimization_barrier((near[4], potentials))
    near = near[:4] + (last,)
    shares = vmem_call(share_kernel, [four] * 3, where + (potentials, rows), scalars=2)
    above, below = shift(shares[1], lambda z: -HOP), shift(shares[2], lambda z: HOP)
    mine, partner = lax.fori_loop(1, rounds, collect_in, collect(sent, found, near, ()))
    owned = (mine + across(partner).astype(F32)).astype(BF16).reshape(sources.shape)

    (target_rows,) = vmem_call(
        target_kernel,
        [four],
        where + (pair_tgt, shares[0], above, below),
        scalars=3,
        scratch=[pltpu.VMEM((4, ROW, ROW), F32)],
    )
    flat = target_rows.reshape(4, targets.shape[1])
    slots = jnp.arange(targets.shape[0], dtype=jnp.int32)[:, None]
    summed = jnp.zeros(targets.shape, BF16)
    for p in range(4):
        summed = jnp.where(slots == ids[p], flat[p][None, :], summed)
    return summed, owned


def solution(mesh):
    return jax.shard_map(
        per_device,
        mesh=mesh,
        in_specs=(P("band", "dom"), P(None, "band", "dom"), P(None, "band"), P()),
        out_specs=(P("band", "dom"), P(None, "band", "dom")),
        check_vma=False,
    )
```

```python
import numpy as np
import jax
import jax.numpy as jnp
from jax import lax
from jax.experimental import pallas as pl
from jax.experimental.pallas import tpu as pltpu
from jax.sharding import PartitionSpec as P

SIDE = 64
SWEEPS = 8
RING = 16
CAP = 6
LANES = 3
ROW = 128
HALF = 64
VMEM_LIMIT = 48 * 1024 * 1024
F32 = jnp.float32
BF16 = jnp.bfloat16


def eigen_system():
    line = np.zeros((SIDE, SIDE))
    for delta, weight in ((0, 30.0), (1, -16.0), (2, 1.0)):
        for i in range(SIDE - delta):
            line[i, i + delta] = weight / 12.0
            line[i + delta, i] = weight / 12.0
    values, vectors = np.linalg.eigh(line)
    return values, vectors * np.where(vectors[0] < 0, -1.0, 1.0)[None, :]


def halves(matrix):
    high = np.asarray(matrix, np.float32).astype(jnp.bfloat16)
    low = (np.asarray(matrix, np.float64) - high.astype(np.float64)).astype(jnp.bfloat16)
    return np.stack([high, low])


def tables():
    values, v = eigen_system()
    along_z = np.kron(np.eye(2), v)
    even, odd = v[0::2], v[1::2]
    fwd = np.zeros((2, 32, 4, 2, 4, 32))
    bwd = np.zeros((2, 4, 32, 2, 32, 4))
    for x in range(4):
        fwd[0, :, x, 0, x, :] = even[:, 0::2].T
        fwd[0, :, x, 1, x, :] = odd[:, 0::2].T
        fwd[1, :, x, 0, x, :] = odd[:, 1::2].T
        fwd[1, :, x, 1, x, :] = even[:, 1::2].T
        bwd[0, x, :, 0, :, x] = even[:, 0::2]
        bwd[0, x, :, 1, :, x] = even[:, 1::2]
        bwd[1, x, :, 0, :, x] = odd[:, 1::2]
        bwd[1, x, :, 1, :, x] = odd[:, 0::2]
    along_x = np.zeros((2, SIDE, RING, 2, 4))
    for pick in range(2):
        along_x[pick, :, :, pick, :] = v.T.reshape(SIDE, RING, 4)
    rows = np.arange(SIDE).reshape(16, 2, 1, 2, 1)
    spectrum = values[rows] + values.reshape(1, 1, SIDE, 1, 1) + values.reshape(1, 1, 1, 1, SIDE)
    return dict(
        z_fwd=halves(along_z),
        z_bwd=halves(along_z.T),
        y_fwd=halves(fwd.reshape(256, 256)),
        y_bwd=halves(bwd.reshape(256, 256)),
        x_fwd=halves(along_x.reshape(ROW, ROW)),
        x_bwd=halves(along_x.reshape(ROW, ROW).T),
        spectrum=spectrum.reshape(8, 256, ROW).astype(np.float32),
    )


def split(value):
    high = value.astype(BF16)
    return high, (value - high.astype(F32)).astype(BF16)


def mm(left, right):
    return jnp.dot(left, right, preferred_element_type=F32)


def left_mul(table, value):
    high, low = split(value)
    return mm(table[0], high) + mm(table[0], low) + mm(table[1], high)


def right_mul(value, table):
    high, low = split(value)
    return mm(high, table[0]) + mm(low, table[0]) + mm(high, table[1])


def swap_halves(value):
    return jnp.concatenate([value[:, HALF:], value[:, :HALF]], axis=1)


def by_half(both):
    lane = lax.broadcasted_iota(jnp.int32, (ROW, ROW), 1)
    return jnp.where(lane < HALF, both[:ROW], both[ROW:])


def vmem_call(kernel, outs, operands, scalars=0, scratch=()):
    whole = pl.BlockSpec(memory_space=pltpu.VMEM)
    smem = pl.BlockSpec(memory_space=pltpu.SMEM)
    return pl.pallas_call(
        kernel,
        out_shape=outs,
        in_specs=[smem] * scalars + [whole] * (len(operands) - scalars),
        out_specs=[whole] * len(outs),
        scratch_shapes=list(scratch),
        compiler_params=pltpu.CompilerParams(vmem_limit_bytes=VMEM_LIMIT),
    )(*operands)


def smem_call(kernel, size, *operands):
    smem = pl.BlockSpec(memory_space=pltpu.SMEM)
    return pl.pallas_call(
        kernel,
        out_shape=struct((size,), jnp.int32),
        in_specs=[smem] * len(operands),
        out_specs=smem,
    )(*operands)


def struct(shape, dtype):
    return jax.ShapeDtypeStruct(shape, dtype)


def ring(value):
    return lax.bitwise_and(value, RING - 1)


def far_step(z):
    return 2 - 4 * lax.bitwise_and(z, 1)


def steps_of(z):
    return 1, -1, far_step(z)


def want_of(pair_src, z, x, want):
    quad, slot = lax.shift_right_logical(want, 2), lax.bitwise_and(want, 3)
    block = lax.shift_right_logical(slot, 1)
    band = 2 * (4 * quad + lax.bitwise_and(z, 3)) + x
    source = pair_src[block, 2 * band + lax.bitwise_and(slot, 1)]
    z_own = lax.shift_right_logical(source, 3)
    other = lax.bitwise_xor(lax.bitwise_and(lax.shift_right_logical(source, 2), 1), x)
    return z_own, 8 * other + 4 * block + lax.bitwise_and(source, 3)


def wants_of(pair_src, z, x):
    for want in range(16):
        yield (want,) + want_of(pair_src, z, x, jnp.int32(want))


def in_round(hit, count):
    return jnp.logical_and(hit, jnp.logical_and(count >= 0, count < CAP))


def sent_kernel(place, pair_src, sent):
    z, x = place[0], place[1]
    for lane, step in enumerate(steps_of(z)):
        for n in range(CAP):
            sent[lane * CAP + n] = -1
        count = -CAP * place[2]
        for _, z_own, row in wants_of(pair_src, z + step, x):
            hit = z_own == z

            @pl.when(in_round(hit, count))
            def _():
                sent[lane * CAP + count] = row

            count = count + hit.astype(jnp.int32)


def found_kernel(place, pair_src, found):
    z, x, turn = place[0], place[1], place[2]
    counts = [-CAP * turn] * LANES
    for want, z_own, row in wants_of(pair_src, z, x):
        at = jnp.where(jnp.logical_and(z_own == z, turn == 0), row, -1)
        for lane, step in enumerate(steps_of(z)):
            hit = z_own == ring(z - step)
            at = jnp.where(in_round(hit, counts[lane]), 16 + lane * CAP + counts[lane], at)
            counts[lane] = counts[lane] + hit.astype(jnp.int32)
        found[want] = at


def pack_rows_kernel(sent, own, other, *outs):
    for lane, out in enumerate(outs):
        for n in range(CAP):
            row = sent[lane * CAP + n]

            @pl.when(row >= 0)
            def _():
                @pl.when(row < 8)
                def _():
                    out[n] = own[row]

                @pl.when(row >= 8)
                def _():
                    out[n] = other[row - 8]


def place_rows_kernel(found, own, other, *refs):
    out = refs[-1]
    for before in refs[3:-1]:
        out[...] = before[...]
    spans = [(own, 0, 8), (other, 8, 16)]
    spans += [(near, 16 + lane * CAP, 16 + lane * CAP + CAP) for lane, near in enumerate(refs[:3])]
    for want in range(16):
        at = found[want]

        @pl.when(at >= 0)
        def _():
            for rows, first, last in spans:

                @pl.when(jnp.logical_and(at >= first, at < last))
                def _():
                    out[want] = rows[at - first]


def for_each_solved(place, pair_src, body):
    z, x = place[0], place[1]

    def step(want, carry):
        z_own, _ = want_of(pair_src, z, x, want)
        near = jnp.logical_or(ring(z - z_own + 1) <= 2, ring(z - z_own) == ring(far_step(z)))

        @pl.when(near)
        def _():
            body(want)

        return carry

    lax.fori_loop(0, 16, step, 0)


def density_kernel(place, pair_src, sources, wanted, z_fwd, y_fwd, spectra):
    def body(want):
        density = sources[want].astype(F32) * wanted[want].astype(F32)
        along = right_mul(density, z_fwd)
        mixed = left_mul(y_fwd, jnp.concatenate([along, swap_halves(along)], axis=0))
        spectra[want] = by_half(mixed).astype(BF16)

    for_each_solved(place, pair_src, body)


def solve_kernel(slabs, spectrum, x_fwd, x_bwd, out, residual, direction, total):
    def dot_of(value):
        return jnp.sum(value.reshape(32, 8, ROW), axis=0)

    zero = jnp.zeros((8, ROW), F32)

    def start(j, carry):
        norm, power = carry
        part = slabs[:, pl.ds(pl.multiple_of(16 * j, 16), 16), :].astype(F32)
        part = [part[:, :8].reshape(ROW, ROW), part[:, 8:].reshape(ROW, ROW)]
        part = jnp.concatenate(part, axis=1).astype(BF16)
        value = mm(x_fwd[0], part) + mm(x_fwd[1], part)
        value = jnp.concatenate([value[:, :ROW], value[:, ROW:]], axis=0)
        direction[j] = value
        square = value * value
        return norm + dot_of(square), power + dot_of(square * spectrum[j])

    norm, power = lax.fori_loop(0, 8, start, (zero, zero))
    norm, power = jnp.sum(norm), jnp.sum(power)
    step, ratio = norm / power, jnp.float32(0.0)
    for sweep in range(SWEEPS - 1):

        def advance(j, carry, sweep=sweep, step=step, ratio=ratio):
            new, power = carry
            lam = spectrum[j]
            if sweep == 0:
                d = direction[j]
                r = d - step * (lam * d)
                total[j] = step * d
            else:
                r = residual[j]
                d = r + ratio * direction[j]
                r = r - step * (lam * d)
                direction[j] = d
                total[j] = total[j] + step * d
            residual[j] = r
            square = r * r
            return new + dot_of(square), power + dot_of(square * lam)

        new, power = lax.fori_loop(0, 8, advance, (zero, zero))
        new, power = jnp.sum(new), jnp.sum(power)
        ratio = new / norm
        step = new / (power - ratio * new / step)
        norm = new

    def finish(j, carry):
        value = total[j] + step * (residual[j] + ratio * direction[j])
        part = left_mul(x_bwd, jnp.concatenate([value[:ROW], value[ROW:]], axis=1))
        part = [part[:, :ROW].reshape(RING, 8, ROW), part[:, ROW:].reshape(RING, 8, ROW)]
        part = jnp.concatenate(part, axis=1)
        out[:, pl.ds(pl.multiple_of(16 * j, 16), 16), :] = part.astype(out.dtype)
        return carry

    lax.fori_loop(0, 8, finish, 0)


def term_kernel(place, pair_src, spectra, sources, wanted, z_bwd, y_bwd, terms, shares):
    shares[...] = jnp.zeros((16, ROW, ROW), BF16)

    def body(want):
        rows = spectra[want]
        rows = jnp.concatenate([rows, swap_halves(rows)], axis=0)
        potential = right_mul(by_half(mm(y_bwd[0], rows) + mm(y_bwd[1], rows)), z_bwd)
        terms[want] = (-potential * wanted[want].astype(F32)).astype(BF16)
        shares[want] = (-potential * sources[want].astype(F32)).astype(BF16)

    for_each_solved(place, pair_src, body)


def pack_terms_kernel(found, terms, *outs):
    for want in range(16):
        at = found[want] - 16

        @pl.when(at >= 0)
        def _():
            for lane, out in enumerate(outs):

                @pl.when(jnp.logical_and(at >= lane * CAP, at < lane * CAP + CAP))
                def _():
                    out[at - lane * CAP] = terms[want]


def add_terms_kernel(sent, found, terms, *refs):
    near, before, (mine, partner, held) = refs[:3], refs[3:-3], refs[-3:]
    mine[...] = before[0][...] if before else jnp.zeros((8, ROW, ROW), F32)
    held[...] = before[1][...].astype(F32) if before else jnp.zeros((8, ROW, ROW), F32)

    def add(row, term):
        @pl.when(row < 8)
        def _():
            mine[row] = mine[row] + term[...].astype(F32)

        @pl.when(row >= 8)
        def _():
            held[row - 8] = held[row - 8] + term[...].astype(F32)

    for want in range(16):
        at = found[want]

        @pl.when(jnp.logical_and(at >= 0, at < 16))
        def _():
            add(at, terms.at[want])

    for lane in range(3):
        for n in range(CAP):
            row = sent[lane * CAP + n]

            @pl.when(row >= 0)
            def _():
                add(row, near[lane].at[n])

    partner[...] = held[...].astype(BF16)


def hand_over(packets, sign):
    moves = (lambda z: 1, lambda z: -1, far_step_of)
    return tuple(
        lax.ppermute(
            packet,
            "band",
            [(2 * z + x, 2 * ((z + sign * move(z)) % RING) + x) for z in range(RING) for x in range(2)],
        )
        for packet, move in zip(packets, moves)
    )


def far_step_of(z):
    return -2 if z % 2 else 2


def across(value):
    return lax.ppermute(value, "band", [(i, i ^ 1) for i in range(32)])


RING_GROUPS = [[8 * quad + member for quad in range(4)] for member in range(8)]


def to_relays(value):
    return lax.all_gather(value, "band", axis_index_groups=RING_GROUPS, tiled=True)


def from_relays(value):
    return lax.psum_scatter(value, "band", axis_index_groups=RING_GROUPS, tiled=True)


def rounds_of(pair_src):
    band = jnp.arange(pair_src.shape[1], dtype=jnp.int32) // 2
    z, x = band // 2, band % 2
    z_own = pair_src // 8
    key = (z_own * 8 + (z % 4) * 2 + x).reshape(-1)
    moves = ((z_own - z) % 4 != 0).astype(jnp.int32).reshape(-1)
    shared = moves * jnp.sum((key[:, None] == key[None, :]).astype(jnp.int32), axis=1)
    return jnp.maximum(1, (jnp.max(shared) + CAP - 1) // CAP)


def per_device(targets, sources, pair_tgt, pair_src):
    table = {name: jnp.asarray(value) for name, value in tables().items()}
    band = lax.axis_index("band")
    rounds = rounds_of(pair_src)
    sixteen = struct((16, ROW, ROW), BF16)
    packets = [struct((CAP, ROW, ROW), BF16)] * 3

    def place_in(turn):
        turn = jnp.asarray(turn, jnp.int32)
        return jnp.stack([band // 2, band % 2, turn]).astype(jnp.int32)

    def sent_in(turn):
        return smem_call(sent_kernel, 3 * CAP, place_in(turn), pair_src)

    def found_in(turn):
        return smem_call(found_kernel, 16, place_in(turn), pair_src)

    own, ids = lax.optimization_barrier((sources.reshape(8, ROW, ROW), pair_tgt.reshape(4)))
    other = across(own)
    wanted = targets[ids].reshape(4, ROW, ROW)

    def pack_rows_in(sent):
        return vmem_call(pack_rows_kernel, packets, (sent, own, other), scalars=1)

    def deliver(packed, found, before):
        near = hand_over(packed, 1)
        operands = (found, own, other) + near + before
        return vmem_call(place_rows_kernel, [sixteen], operands, scalars=1)[0]

    def deliver_in(turn, before):
        return deliver(pack_rows_in(sent_in(turn)), found_in(turn), (before,))

    sent, found = sent_in(0), found_in(0)
    packed, wanted = lax.optimization_barrier((pack_rows_in(sent), wanted))
    wanted = to_relays(wanted)
    rows = lax.fori_loop(1, rounds, deliver_in, deliver(packed, found, ()))
    where = (place_in(0), pair_src)
    (spectra,) = vmem_call(
        density_kernel,
        [sixteen],
        where + (rows, wanted, table["z_fwd"], table["y_fwd"]),
        scalars=2,
    )
    slabs = lax.all_to_all(spectra, "dom", 0, 0, tiled=True)
    (solved,) = vmem_call(
        solve_kernel,
        [sixteen],
        (slabs, table["spectrum"], table["x_fwd"], table["x_bwd"]),
        scratch=[pltpu.VMEM((8, 256, ROW), F32)] * 3,
    )
    back = lax.all_to_all(solved, "dom", 0, 0, tiled=True)
    terms, shares = vmem_call(
        term_kernel,
        [sixteen, sixteen],
        where + (back, rows, wanted, table["z_bwd"], table["y_bwd"]),
        scalars=2,
    )

    def give_back(found):
        return hand_over(vmem_call(pack_terms_kernel, packets, (found, terms), scalars=1), -1)

    def collect(sent, found, near, before):
        outs = [struct((8, ROW, ROW), F32), struct((8, ROW, ROW), BF16)]
        operands = (sent, found, terms) + near + before
        scratch = [pltpu.VMEM((8, ROW, ROW), F32)]
        return vmem_call(add_terms_kernel, outs, operands, scalars=2, scratch=scratch)

    def collect_in(turn, before):
        found = found_in(turn)
        return collect(sent_in(turn), found, give_back(found), tuple(before))

    near = give_back(found)
    shares = from_relays(shares)
    mine, partner = lax.fori_loop(1, rounds, collect_in, collect(sent, found, near, ()))
    owned = (mine + across(partner).astype(F32)).astype(BF16).reshape(sources.shape)

    flat = shares.reshape(4, targets.shape[1]).astype(F32)
    slots = jnp.arange(targets.shape[0], dtype=jnp.int32)[:, None]
    summed = jnp.zeros(targets.shape, F32)
    for p in range(4):
        summed = summed + jnp.where(slots == ids[p], flat[p][None, :], 0.0)
    return summed.astype(BF16), owned


def solution(mesh):
    return jax.shard_map(
        per_device,
        mesh=mesh,
        in_specs=(P("band", "dom"), P(None, "band", "dom"), P(None, "band"), P()),
        out_specs=(P("band", "dom"), P(None, "band", "dom")),
        check_vma=False,
    )
```

```python
import numpy as np
import jax
import jax.numpy as jnp
from jax import lax
from jax.experimental import pallas as pl
from jax.experimental.pallas import tpu as pltpu
from jax.sharding import PartitionSpec as P

SIDE = 64
SWEEPS = 8
RING = 16
CAP = 6
LANES = 3
ROW = 128
HALF = 64
VMEM_LIMIT = 48 * 1024 * 1024
F32 = jnp.float32
BF16 = jnp.bfloat16


def eigen_system():
    line = np.zeros((SIDE, SIDE))
    for delta, weight in ((0, 30.0), (1, -16.0), (2, 1.0)):
        for i in range(SIDE - delta):
            line[i, i + delta] = weight / 12.0
            line[i + delta, i] = weight / 12.0
    values, vectors = np.linalg.eigh(line)
    return values, vectors * np.where(vectors[0] < 0, -1.0, 1.0)[None, :]


def halves(matrix):
    high = np.asarray(matrix, np.float32).astype(jnp.bfloat16)
    low = (np.asarray(matrix, np.float64) - high.astype(np.float64)).astype(jnp.bfloat16)
    return np.stack([high, low])


def tables():
    values, v = eigen_system()
    along_z = np.kron(np.eye(2), v)
    even, odd = v[0::2], v[1::2]
    fwd = np.zeros((2, 32, 4, 2, 4, 32))
    bwd = np.zeros((2, 4, 32, 2, 32, 4))
    for x in range(4):
        fwd[0, :, x, 0, x, :] = even[:, 0::2].T
        fwd[0, :, x, 1, x, :] = odd[:, 0::2].T
        fwd[1, :, x, 0, x, :] = odd[:, 1::2].T
        fwd[1, :, x, 1, x, :] = even[:, 1::2].T
        bwd[0, x, :, 0, :, x] = even[:, 0::2]
        bwd[0, x, :, 1, :, x] = even[:, 1::2]
        bwd[1, x, :, 0, :, x] = odd[:, 1::2]
        bwd[1, x, :, 1, :, x] = odd[:, 0::2]
    along_x = np.zeros((2, SIDE, RING, 2, 4))
    for pick in range(2):
        along_x[pick, :, :, pick, :] = v.T.reshape(SIDE, RING, 4)
    rows = np.arange(SIDE).reshape(16, 2, 1, 2, 1)
    spectrum = values[rows] + values.reshape(1, 1, SIDE, 1, 1) + values.reshape(1, 1, 1, 1, SIDE)
    return dict(
        z_fwd=halves(along_z),
        z_bwd=halves(along_z.T),
        y_fwd=halves(fwd.reshape(256, 256)),
        y_bwd=halves(bwd.reshape(256, 256)),
        x_fwd=halves(along_x.reshape(ROW, ROW)),
        x_bwd=halves(along_x.reshape(ROW, ROW).T),
        spectrum=spectrum.reshape(8, 256, ROW).astype(np.float32),
    )


def split(value):
    high = value.astype(BF16)
    return high, (value - high.astype(F32)).astype(BF16)


def mm(left, right):
    return jnp.dot(left, right, preferred_element_type=F32)


def left_mul(table, value):
    high, low = split(value)
    return mm(table[0], high) + mm(table[0], low) + mm(table[1], high)


def right_mul(value, table):
    high, low = split(value)
    return mm(high, table[0]) + mm(low, table[0]) + mm(high, table[1])


def swap_halves(value):
    return jnp.concatenate([value[:, HALF:], value[:, :HALF]], axis=1)


def by_half(both):
    lane = lax.broadcasted_iota(jnp.int32, (ROW, ROW), 1)
    return jnp.where(lane < HALF, both[:ROW], both[ROW:])


def vmem_call(kernel, outs, operands, scalars=0, scratch=()):
    whole = pl.BlockSpec(memory_space=pltpu.VMEM)
    smem = pl.BlockSpec(memory_space=pltpu.SMEM)
    return pl.pallas_call(
        kernel,
        out_shape=outs,
        in_specs=[smem] * scalars + [whole] * (len(operands) - scalars),
        out_specs=[whole] * len(outs),
        scratch_shapes=list(scratch),
        compiler_params=pltpu.CompilerParams(vmem_limit_bytes=VMEM_LIMIT),
    )(*operands)


def smem_call(kernel, size, *operands):
    smem = pl.BlockSpec(memory_space=pltpu.SMEM)
    return pl.pallas_call(
        kernel,
        out_shape=struct((size,), jnp.int32),
        in_specs=[smem] * len(operands),
        out_specs=smem,
    )(*operands)


def struct(shape, dtype):
    return jax.ShapeDtypeStruct(shape, dtype)


def ring(value):
    return lax.bitwise_and(value, RING - 1)


def far_step(z):
    return 2 - 4 * lax.bitwise_and(z, 1)


def steps_of(z):
    return 1, -1, far_step(z)


def want_of(pair_src, z, x, want):
    quad, slot = lax.shift_right_logical(want, 2), lax.bitwise_and(want, 3)
    block = lax.shift_right_logical(slot, 1)
    band = 2 * (4 * quad + lax.bitwise_and(z, 3)) + x
    source = pair_src[block, 2 * band + lax.bitwise_and(slot, 1)]
    z_own = lax.shift_right_logical(source, 3)
    other = lax.bitwise_xor(lax.bitwise_and(lax.shift_right_logical(source, 2), 1), x)
    return z_own, 8 * other + 4 * block + lax.bitwise_and(source, 3)


def wants_of(pair_src, z, x):
    for want in range(16):
        yield (want,) + want_of(pair_src, z, x, jnp.int32(want))


def in_round(hit, count):
    return jnp.logical_and(hit, jnp.logical_and(count >= 0, count < CAP))


def sent_kernel(place, pair_src, sent):
    z, x = place[0], place[1]
    for lane, step in enumerate(steps_of(z)):
        for n in range(CAP):
            sent[lane * CAP + n] = -1
        count = -CAP * place[2]
        for _, z_own, row in wants_of(pair_src, z + step, x):
            hit = z_own == z

            @pl.when(in_round(hit, count))
            def _():
                sent[lane * CAP + count] = row

            count = count + hit.astype(jnp.int32)


def found_kernel(place, pair_src, found):
    z, x, turn = place[0], place[1], place[2]
    counts = [-CAP * turn] * LANES
    for want, z_own, row in wants_of(pair_src, z, x):
        at = jnp.where(jnp.logical_and(z_own == z, turn == 0), row, -1)
        for lane, step in enumerate(steps_of(z)):
            hit = z_own == ring(z - step)
            at = jnp.where(in_round(hit, counts[lane]), 16 + lane * CAP + counts[lane], at)
            counts[lane] = counts[lane] + hit.astype(jnp.int32)
        found[want] = at


def pack_rows_kernel(sent, own, other, *outs):
    for lane, out in enumerate(outs):
        for n in range(CAP):
            row = sent[lane * CAP + n]

            @pl.when(row >= 0)
            def _():
                @pl.when(row < 8)
                def _():
                    out[n] = own[row]

                @pl.when(row >= 8)
                def _():
                    out[n] = other[row - 8]


def place_rows_kernel(found, own, other, *refs):
    out = refs[-1]
    for before in refs[3:-1]:
        out[...] = before[...]
    spans = [(own, 0, 8), (other, 8, 16)]
    spans += [(near, 16 + lane * CAP, 16 + lane * CAP + CAP) for lane, near in enumerate(refs[:3])]
    for want in range(16):
        at = found[want]

        @pl.when(at >= 0)
        def _():
            for rows, first, last in spans:

                @pl.when(jnp.logical_and(at >= first, at < last))
                def _():
                    out[want] = rows[at - first]


def for_each_solved(place, pair_src, queue, body):
    z, x = place[0], place[1]

    def note(want, count):
        z_own, _ = want_of(pair_src, z, x, want)
        near = jnp.logical_or(ring(z - z_own + 1) <= 2, ring(z - z_own) == ring(far_step(z)))

        @pl.when(near)
        def _():
            queue[count] = want

        return count + near.astype(jnp.int32)

    count = lax.fori_loop(0, 16, note, jnp.int32(0))

    def step(turn, carry):
        body((queue[2 * turn], queue[jnp.minimum(2 * turn + 1, count - 1)]))
        return carry

    lax.fori_loop(0, lax.shift_right_logical(count + 1, 1), step, 0)


def density_kernel(place, pair_src, sources, wanted, z_fwd, y_fwd, spectra, queue):
    def body(wants):
        pairs = [sources[want].astype(F32) * wanted[want].astype(F32) for want in wants]
        pairs = [right_mul(pair, z_fwd) for pair in pairs]
        pairs = [jnp.concatenate([pair, swap_halves(pair)], axis=0) for pair in pairs]
        pairs = [by_half(left_mul(y_fwd, pair)).astype(BF16) for pair in pairs]
        for want, pair in zip(wants, pairs):
            spectra[want] = pair

    for_each_solved(place, pair_src, queue, body)


def solve_kernel(slabs, spectrum, x_fwd, x_bwd, out, residual, directions):
    def dot_of(value):
        return jnp.sum(value.reshape(32, 8, ROW), axis=0)

    zero = jnp.zeros((8, ROW), F32)

    def start(j, carry):
        norm, power = carry
        part = slabs[:, pl.ds(pl.multiple_of(16 * j, 16), 16), :].astype(F32)
        part = [part[:, :8].reshape(ROW, ROW), part[:, 8:].reshape(ROW, ROW)]
        part = jnp.concatenate(part, axis=1).astype(BF16)
        value = mm(x_fwd[0], part) + mm(x_fwd[1], part)
        value = jnp.concatenate([value[:, :ROW], value[:, ROW:]], axis=0)
        directions[0, j] = value
        square = value * value
        return norm + dot_of(square), power + dot_of(square * spectrum[j])

    norm, power = lax.fori_loop(0, 8, start, (zero, zero))
    norm, power = jnp.sum(norm), jnp.sum(power)
    steps, ratio = [norm / power], jnp.float32(0.0)
    for sweep in range(SWEEPS - 1):
        step = steps[-1]

        def advance(j, carry, sweep=sweep, step=step, ratio=ratio):
            new, power = carry
            lam = spectrum[j]
            if sweep == 0:
                r = d = directions[0, j]
            else:
                r = residual[j]
                d = r + ratio * directions[sweep - 1, j]
                directions[sweep, j] = d
            r = r - step * (lam * d)
            residual[j] = r
            square = r * r
            return new + dot_of(square), power + dot_of(square * lam)

        new, power = lax.fori_loop(0, 8, advance, (zero, zero))
        new, power = jnp.sum(new), jnp.sum(power)
        ratio = new / norm
        steps.append(new / (power - ratio * new / step))
        norm = new

    def finish(j, carry):
        value = steps[-1] * (residual[j] + ratio * directions[SWEEPS - 2, j])
        for sweep in range(SWEEPS - 1):
            value = value + steps[sweep] * directions[sweep, j]
        part = left_mul(x_bwd, jnp.concatenate([value[:ROW], value[ROW:]], axis=1))
        part = [part[:, :ROW].reshape(RING, 8, ROW), part[:, ROW:].reshape(RING, 8, ROW)]
        part = jnp.concatenate(part, axis=1)
        out[:, pl.ds(pl.multiple_of(16 * j, 16), 16), :] = part.astype(out.dtype)
        return carry

    lax.fori_loop(0, 8, finish, 0)


def term_kernel(place, pair_src, spectra, sources, wanted, z_bwd, y_bwd, terms, shares, queue):
    def body(wants):
        pairs = [spectra[want] for want in wants]
        pairs = [jnp.concatenate([pair, swap_halves(pair)], axis=0) for pair in pairs]
        pairs = [by_half(mm(y_bwd[0], pair) + mm(y_bwd[1], pair)) for pair in pairs]
        pairs = [-right_mul(pair, z_bwd) for pair in pairs]
        for want, pair in zip(wants, pairs):
            terms[want] = (pair * wanted[want].astype(F32)).astype(BF16)
            shares[want] = (pair * sources[want].astype(F32)).astype(BF16)

    for_each_solved(place, pair_src, queue, body)


def pack_terms_kernel(found, terms, *outs):
    for want in range(16):
        at = found[want] - 16

        @pl.when(at >= 0)
        def _():
            for lane, out in enumerate(outs):

                @pl.when(jnp.logical_and(at >= lane * CAP, at < lane * CAP + CAP))
                def _():
                    out[at - lane * CAP] = terms[want]


def add_terms_kernel(sent, found, terms, *refs):
    near, before, (mine, partner, held) = refs[:3], refs[3:-3], refs[-3:]
    mine[...] = before[0][...] if before else jnp.zeros((8, ROW, ROW), F32)
    held[...] = before[1][...].astype(F32) if before else jnp.zeros((8, ROW, ROW), F32)

    def add(row, term):
        @pl.when(row < 8)
        def _():
            mine[row] = mine[row] + term[...].astype(F32)

        @pl.when(row >= 8)
        def _():
            held[row - 8] = held[row - 8] + term[...].astype(F32)

    for want in range(16):
        at = found[want]

        @pl.when(jnp.logical_and(at >= 0, at < 16))
        def _():
            add(at, terms.at[want])

    for lane in range(3):
        for n in range(CAP):
            row = sent[lane * CAP + n]

            @pl.when(row >= 0)
            def _():
                add(row, near[lane].at[n])

    partner[...] = held[...].astype(BF16)


def target_kernel(place, pair_src, pair_tgt, shares, rows, held):
    z, x = place[0], place[1]
    quad = lax.shift_right_logical(z, 2)
    for p in range(4):
        z_own, _ = want_of(pair_src, z, x, 4 * quad + p)
        ahead = lax.bitwise_and(z - z_own, 3)
        relay = ring(z_own + jnp.where(ahead == 3, -1, jnp.where(ahead == 2, far_step(z_own), ahead)))
        held[p] = shares[4 * lax.shift_right_logical(relay, 2) + p].astype(F32)
    for p in range(4):
        same = jnp.zeros((ROW, ROW), F32)
        for other in range(4):
            hit = pair_tgt[p // 2, p % 2] == pair_tgt[other // 2, other % 2]
            same = same + jnp.where(hit, held[other], 0.0)
        rows[p] = same.astype(BF16)


def hand_over(packets, sign):
    moves = (lambda z: 1, lambda z: -1, far_step_of)
    return tuple(
        lax.ppermute(
            packet,
            "band",
            [(2 * z + x, 2 * ((z + sign * move(z)) % RING) + x) for z in range(RING) for x in range(2)],
        )
        for packet, move in zip(packets, moves)
    )


def far_step_of(z):
    return -2 if z % 2 else 2


def across(value):
    return lax.ppermute(value, "band", [(i, i ^ 1) for i in range(32)])


def along_ring(value):
    groups = [[8 * quad + member for quad in range(4)] for member in range(8)]
    return lax.all_to_all(value, "band", 0, 0, axis_index_groups=groups, tiled=True)


def rounds_of(pair_src):
    band = jnp.arange(pair_src.shape[1], dtype=jnp.int32) // 2
    z, x = band // 2, band % 2
    z_own = pair_src // 8
    key = (z_own * 8 + (z % 4) * 2 + x).reshape(-1)
    moves = ((z_own - z) % 4 != 0).astype(jnp.int32).reshape(-1)
    shared = moves * jnp.sum((key[:, None] == key[None, :]).astype(jnp.int32), axis=1)
    return jnp.maximum(1, (jnp.max(shared) + CAP - 1) // CAP)


def per_device(targets, sources, pair_tgt, pair_src):
    table = {name: jnp.asarray(value) for name, value in tables().items()}
    band = lax.axis_index("band")
    sixteen = struct((16, ROW, ROW), BF16)
    packets = [struct((CAP, ROW, ROW), BF16)] * 3

    def place_in(turn):
        turn = jnp.asarray(turn, jnp.int32)
        return jnp.stack([band // 2, band % 2, turn]).astype(jnp.int32)

    def sent_in(turn):
        return smem_call(sent_kernel, 3 * CAP, place_in(turn), pair_src)

    def found_in(turn):
        return smem_call(found_kernel, 16, place_in(turn), pair_src)

    own, ids = lax.optimization_barrier((sources.reshape(8, ROW, ROW), pair_tgt.reshape(4)))
    other = across(own)
    wanted = targets[ids].reshape(4, ROW, ROW)

    def pack_rows_in(sent):
        return vmem_call(pack_rows_kernel, packets, (sent, own, other), scalars=1)

    def deliver(near, found, before):
        operands = (found, own, other) + near + before
        return vmem_call(place_rows_kernel, [sixteen], operands, scalars=1)[0]

    def deliver_in(turn, before):
        return deliver(hand_over(pack_rows_in(sent_in(turn)), 1), found_in(turn), (before,))

    sent, found = sent_in(0), found_in(0)
    packed, found, wanted = lax.optimization_barrier((pack_rows_in(sent), found, wanted))
    wanted = along_ring(jnp.concatenate([wanted] * 4, axis=0))
    near = hand_over(packed, 1)
    first, wants = lax.optimization_barrier((near[0], pair_src))
    rounds = rounds_of(wants)
    rows = lax.fori_loop(1, rounds, deliver_in, deliver((first,) + near[1:], found, ()))
    where = (place_in(0), pair_src)
    (spectra,) = vmem_call(
        density_kernel,
        [sixteen],
        where + (rows, wanted, table["z_fwd"], table["y_fwd"]),
        scalars=2,
        scratch=[pltpu.SMEM((16,), jnp.int32)],
    )
    slabs = lax.all_to_all(spectra, "dom", 0, 0, tiled=True)
    (solved,) = vmem_call(
        solve_kernel,
        [sixteen],
        (slabs, table["spectrum"], table["x_fwd"], table["x_bwd"]),
        scratch=[pltpu.VMEM((8, 256, ROW), F32), pltpu.VMEM((SWEEPS - 1, 8, 256, ROW), F32)],
    )
    back = lax.all_to_all(solved, "dom", 0, 0, tiled=True)
    terms, shares = vmem_call(
        term_kernel,
        [sixteen, sixteen],
        where + (back, rows, wanted, table["z_bwd"], table["y_bwd"]),
        scalars=2,
        scratch=[pltpu.SMEM((16,), jnp.int32)],
    )

    def give_back(found):
        return hand_over(vmem_call(pack_terms_kernel, packets, (found, terms), scalars=1), -1)

    def collect(sent, found, near, before):
        outs = [struct((8, ROW, ROW), F32), struct((8, ROW, ROW), BF16)]
        operands = (sent, found, terms) + near + before
        scratch = [pltpu.VMEM((8, ROW, ROW), F32)]
        return vmem_call(add_terms_kernel, outs, operands, scalars=2, scratch=scratch)

    def collect_in(turn, before):
        found = found_in(turn)
        return collect(sent_in(turn), found, give_back(found), tuple(before))

    near = give_back(found)
    near, shares = lax.optimization_barrier((near, shares))
    shares = along_ring(shares)
    mine, partner = lax.fori_loop(1, rounds, collect_in, collect(sent, found, near, ()))
    owned = (mine + across(partner).astype(F32)).astype(BF16).reshape(sources.shape)

    (target_rows,) = vmem_call(
        target_kernel,
        [struct((4, ROW, ROW), BF16)],
        where + (pair_tgt, shares),
        scalars=3,
        scratch=[pltpu.VMEM((4, ROW, ROW), F32)],
    )
    flat = target_rows.reshape(4, targets.shape[1])
    slots = jnp.arange(targets.shape[0], dtype=jnp.int32)[:, None]
    summed = jnp.zeros(targets.shape, BF16)
    for p in range(4):
        summed = jnp.where(slots == ids[p], flat[p][None, :], summed)
    return summed, owned


def solution(mesh):
    return jax.shard_map(
        per_device,
        mesh=mesh,
        in_specs=(P("band", "dom"), P(None, "band", "dom"), P(None, "band"), P()),
        out_specs=(P("band", "dom"), P(None, "band", "dom")),
        check_vma=False,
    )
```

```python
import numpy as np
import jax
import jax.numpy as jnp
from jax import lax
from jax.experimental import pallas as pl
from jax.experimental.pallas import tpu as pltpu
from jax.sharding import PartitionSpec as P

SIDE = 64
SWEEPS = 8
RING = 16
CAP = 6
LANES = 3
ROW = 128
HALF = 64
VMEM_LIMIT = 48 * 1024 * 1024
F32 = jnp.float32
BF16 = jnp.bfloat16


def eigen_system():
    line = np.zeros((SIDE, SIDE))
    for delta, weight in ((0, 30.0), (1, -16.0), (2, 1.0)):
        for i in range(SIDE - delta):
            line[i, i + delta] = weight / 12.0
            line[i + delta, i] = weight / 12.0
    values, vectors = np.linalg.eigh(line)
    return values, vectors * np.where(vectors[0] < 0, -1.0, 1.0)[None, :]


def halves(matrix):
    high = np.asarray(matrix, np.float32).astype(jnp.bfloat16)
    low = (np.asarray(matrix, np.float64) - high.astype(np.float64)).astype(jnp.bfloat16)
    return np.stack([high, low])


def tables():
    values, v = eigen_system()
    along_z = np.kron(np.eye(2), v)
    even, odd = v[0::2], v[1::2]
    fwd = np.zeros((2, 32, 4, 2, 4, 32))
    bwd = np.zeros((2, 4, 32, 2, 32, 4))
    for x in range(4):
        fwd[0, :, x, 0, x, :] = even[:, 0::2].T
        fwd[0, :, x, 1, x, :] = odd[:, 0::2].T
        fwd[1, :, x, 0, x, :] = odd[:, 1::2].T
        fwd[1, :, x, 1, x, :] = even[:, 1::2].T
        bwd[0, x, :, 0, :, x] = even[:, 0::2]
        bwd[0, x, :, 1, :, x] = even[:, 1::2]
        bwd[1, x, :, 0, :, x] = odd[:, 1::2]
        bwd[1, x, :, 1, :, x] = odd[:, 0::2]
    along_x = np.zeros((2, SIDE, RING, 2, 4))
    for pick in range(2):
        along_x[pick, :, :, pick, :] = v.T.reshape(SIDE, RING, 4)
    rows = np.arange(SIDE).reshape(16, 2, 1, 2, 1)
    spectrum = values[rows] + values.reshape(1, 1, SIDE, 1, 1) + values.reshape(1, 1, 1, 1, SIDE)
    return dict(
        z_fwd=halves(along_z),
        z_bwd=halves(along_z.T),
        y_fwd=halves(fwd.reshape(256, 256)),
        y_bwd=halves(bwd.reshape(256, 256)),
        x_fwd=halves(along_x.reshape(ROW, ROW)),
        x_bwd=halves(along_x.reshape(ROW, ROW).T),
        spectrum=spectrum.reshape(8, 256, ROW).astype(np.float32),
    )


def split(value):
    high = value.astype(BF16)
    return high, (value - high.astype(F32)).astype(BF16)


def mm(left, right):
    return jnp.dot(left, right, preferred_element_type=F32)


def left_mul(table, value):
    high, low = split(value)
    return mm(table[0], high) + mm(table[0], low) + mm(table[1], high)


def right_mul(value, table):
    high, low = split(value)
    return mm(high, table[0]) + mm(low, table[0]) + mm(high, table[1])


def swap_halves(value):
    return jnp.concatenate([value[:, HALF:], value[:, :HALF]], axis=1)


def by_half(both):
    lane = lax.broadcasted_iota(jnp.int32, (ROW, ROW), 1)
    return jnp.where(lane < HALF, both[:ROW], both[ROW:])


def vmem_call(kernel, outs, operands, scalars=0, scratch=()):
    whole = pl.BlockSpec(memory_space=pltpu.VMEM)
    smem = pl.BlockSpec(memory_space=pltpu.SMEM)
    return pl.pallas_call(
        kernel,
        out_shape=outs,
        in_specs=[smem] * scalars + [whole] * (len(operands) - scalars),
        out_specs=[whole] * len(outs),
        scratch_shapes=list(scratch),
        compiler_params=pltpu.CompilerParams(vmem_limit_bytes=VMEM_LIMIT),
    )(*operands)


def smem_call(kernel, size, *operands):
    smem = pl.BlockSpec(memory_space=pltpu.SMEM)
    return pl.pallas_call(
        kernel,
        out_shape=struct((size,), jnp.int32),
        in_specs=[smem] * len(operands),
        out_specs=smem,
    )(*operands)


def struct(shape, dtype):
    return jax.ShapeDtypeStruct(shape, dtype)


def ring(value):
    return lax.bitwise_and(value, RING - 1)


def far_step(z):
    return 2 - 4 * lax.bitwise_and(z, 1)


def steps_of(z):
    return 1, -1, far_step(z)


def want_of(pair_src, z, x, want):
    quad, slot = lax.shift_right_logical(want, 2), lax.bitwise_and(want, 3)
    block = lax.shift_right_logical(slot, 1)
    band = 2 * (4 * quad + lax.bitwise_and(z, 3)) + x
    source = pair_src[block, 2 * band + lax.bitwise_and(slot, 1)]
    z_own = lax.shift_right_logical(source, 3)
    other = lax.bitwise_xor(lax.bitwise_and(lax.shift_right_logical(source, 2), 1), x)
    return z_own, 8 * other + 4 * block + lax.bitwise_and(source, 3)


def wants_of(pair_src, z, x):
    for want in range(16):
        yield (want,) + want_of(pair_src, z, x, jnp.int32(want))


def in_round(hit, count):
    return jnp.logical_and(hit, jnp.logical_and(count >= 0, count < CAP))


def sent_kernel(place, pair_src, sent):
    z, x = place[0], place[1]
    for lane, step in enumerate(steps_of(z)):
        for n in range(CAP):
            sent[lane * CAP + n] = -1
        count = -CAP * place[2]
        for _, z_own, row in wants_of(pair_src, z + step, x):
            hit = z_own == z

            @pl.when(in_round(hit, count))
            def _():
                sent[lane * CAP + count] = row

            count = count + hit.astype(jnp.int32)


def found_kernel(place, pair_src, found):
    z, x, turn = place[0], place[1], place[2]
    counts = [-CAP * turn] * LANES
    for want, z_own, row in wants_of(pair_src, z, x):
        at = jnp.where(jnp.logical_and(z_own == z, turn == 0), row, -1)
        for lane, step in enumerate(steps_of(z)):
            hit = z_own == ring(z - step)
            at = jnp.where(in_round(hit, counts[lane]), 16 + lane * CAP + counts[lane], at)
            counts[lane] = counts[lane] + hit.astype(jnp.int32)
        found[want] = at


def pack_rows_kernel(sent, own, other, *outs):
    for lane, out in enumerate(outs):
        for n in range(CAP):
            row = sent[lane * CAP + n]

            @pl.when(row >= 0)
            def _():
                @pl.when(row < 8)
                def _():
                    out[n] = own[row]

                @pl.when(row >= 8)
                def _():
                    out[n] = other[row - 8]


def place_rows_kernel(found, own, other, *refs):
    out = refs[-1]
    for before in refs[3:-1]:
        out[...] = before[...]
    spans = [(own, 0, 8), (other, 8, 16)]
    spans += [(near, 16 + lane * CAP, 16 + lane * CAP + CAP) for lane, near in enumerate(refs[:3])]
    for want in range(16):
        at = found[want]

        @pl.when(at >= 0)
        def _():
            for rows, first, last in spans:

                @pl.when(jnp.logical_and(at >= first, at < last))
                def _():
                    out[want] = rows[at - first]


def for_each_solved(place, pair_src, queue, body):
    z, x = place[0], place[1]

    def note(want, count):
        z_own, _ = want_of(pair_src, z, x, want)
        near = jnp.logical_or(ring(z - z_own + 1) <= 2, ring(z - z_own) == ring(far_step(z)))

        @pl.when(near)
        def _():
            queue[count] = want

        return count + near.astype(jnp.int32)

    count = lax.fori_loop(0, 16, note, jnp.int32(0))

    def step(turn, carry):
        body((queue[2 * turn], queue[jnp.minimum(2 * turn + 1, count - 1)]))
        return carry

    lax.fori_loop(0, lax.shift_right_logical(count + 1, 1), step, 0)


def density_kernel(place, pair_src, sources, wanted, z_fwd, y_fwd, spectra, queue):
    def body(wants):
        pairs = [sources[want].astype(F32) * wanted[want].astype(F32) for want in wants]
        pairs = [right_mul(pair, z_fwd) for pair in pairs]
        pairs = [jnp.concatenate([pair, swap_halves(pair)], axis=0) for pair in pairs]
        pairs = [by_half(left_mul(y_fwd, pair)).astype(BF16) for pair in pairs]
        for want, pair in zip(wants, pairs):
            spectra[want] = pair

    for_each_solved(place, pair_src, queue, body)


def solve_kernel(slabs, spectrum, x_fwd, x_bwd, out, residual, directions):
    def dot_of(value):
        return jnp.sum(value.reshape(32, 8, ROW), axis=0)

    zero = jnp.zeros((8, ROW), F32)

    def start(j, carry):
        norm, power = carry
        part = slabs[:, pl.ds(pl.multiple_of(16 * j, 16), 16), :].astype(F32)
        part = [part[:, :8].reshape(ROW, ROW), part[:, 8:].reshape(ROW, ROW)]
        part = jnp.concatenate(part, axis=1).astype(BF16)
        value = mm(x_fwd[0], part) + mm(x_fwd[1], part)
        value = jnp.concatenate([value[:, :ROW], value[:, ROW:]], axis=0)
        directions[0, j] = value
        square = value * value
        return norm + dot_of(square), power + dot_of(square * spectrum[j])

    norm, power = lax.fori_loop(0, 8, start, (zero, zero))
    norm, power = jnp.sum(norm), jnp.sum(power)
    steps, ratio = [norm / power], jnp.float32(0.0)
    for sweep in range(SWEEPS - 1):
        step = steps[-1]

        def advance(j, carry, sweep=sweep, step=step, ratio=ratio):
            new, power = carry
            lam = spectrum[j]
            if sweep == 0:
                r = d = directions[0, j]
            else:
                r = residual[j]
                d = r + ratio * directions[sweep - 1, j]
                directions[sweep, j] = d
            r = r - step * (lam * d)
            residual[j] = r
            square = r * r
            return new + dot_of(square), power + dot_of(square * lam)

        new, power = lax.fori_loop(0, 8, advance, (zero, zero))
        new, power = jnp.sum(new), jnp.sum(power)
        ratio = new / norm
        steps.append(new / (power - ratio * new / step))
        norm = new

    def finish(j, carry):
        value = steps[-1] * (residual[j] + ratio * directions[SWEEPS - 2, j])
        for sweep in range(SWEEPS - 1):
            value = value + steps[sweep] * directions[sweep, j]
        part = left_mul(x_bwd, jnp.concatenate([value[:ROW], value[ROW:]], axis=1))
        part = [part[:, :ROW].reshape(RING, 8, ROW), part[:, ROW:].reshape(RING, 8, ROW)]
        part = jnp.concatenate(part, axis=1)
        out[:, pl.ds(pl.multiple_of(16 * j, 16), 16), :] = part.astype(out.dtype)
        return carry

    lax.fori_loop(0, 8, finish, 0)


def term_kernel(place, pair_src, spectra, sources, wanted, z_bwd, y_bwd, terms, shares, queue):
    def body(wants):
        pairs = [spectra[want] for want in wants]
        pairs = [jnp.concatenate([pair, swap_halves(pair)], axis=0) for pair in pairs]
        pairs = [by_half(mm(y_bwd[0], pair) + mm(y_bwd[1], pair)) for pair in pairs]
        pairs = [-right_mul(pair, z_bwd) for pair in pairs]
        for want, pair in zip(wants, pairs):
            terms[want] = (pair * wanted[want].astype(F32)).astype(BF16)
            shares[want] = (pair * sources[want].astype(F32)).astype(BF16)

    for_each_solved(place, pair_src, queue, body)


def pack_terms_kernel(found, terms, *outs):
    for want in range(16):
        at = found[want] - 16

        @pl.when(at >= 0)
        def _():
            for lane, out in enumerate(outs):

                @pl.when(jnp.logical_and(at >= lane * CAP, at < lane * CAP + CAP))
                def _():
                    out[at - lane * CAP] = terms[want]


def add_terms_kernel(sent, found, terms, *refs):
    near, before, (mine, partner, held) = refs[:3], refs[3:-3], refs[-3:]
    mine[...] = before[0][...] if before else jnp.zeros((8, ROW, ROW), F32)
    held[...] = before[1][...].astype(F32) if before else jnp.zeros((8, ROW, ROW), F32)

    def add(row, term):
        @pl.when(row < 8)
        def _():
            mine[row] = mine[row] + term[...].astype(F32)

        @pl.when(row >= 8)
        def _():
            held[row - 8] = held[row - 8] + term[...].astype(F32)

    for want in range(16):
        at = found[want]

        @pl.when(jnp.logical_and(at >= 0, at < 16))
        def _():
            add(at, terms.at[want])

    for lane in range(3):
        for n in range(CAP):
            row = sent[lane * CAP + n]

            @pl.when(row >= 0)
            def _():
                add(row, near[lane].at[n])

    partner[...] = held[...].astype(BF16)


def target_kernel(place, pair_src, pair_tgt, shares, rows, held):
    z, x = place[0], place[1]
    quad = lax.shift_right_logical(z, 2)
    for p in range(4):
        z_own, _ = want_of(pair_src, z, x, 4 * quad + p)
        ahead = lax.bitwise_and(z - z_own, 3)
        relay = ring(z_own + jnp.where(ahead == 3, -1, jnp.where(ahead == 2, far_step(z_own), ahead)))
        held[p] = shares[4 * lax.shift_right_logical(relay, 2) + p].astype(F32)
    for p in range(4):
        same = jnp.zeros((ROW, ROW), F32)
        for other in range(4):
            hit = pair_tgt[p // 2, p % 2] == pair_tgt[other // 2, other % 2]
            same = same + jnp.where(hit, held[other], 0.0)
        rows[p] = same.astype(BF16)


def hand_over(packets, sign):
    moves = (lambda z: 1, lambda z: -1, far_step_of)
    return tuple(
        lax.ppermute(
            packet,
            "band",
            [(2 * z + x, 2 * ((z + sign * move(z)) % RING) + x) for z in range(RING) for x in range(2)],
        )
        for packet, move in zip(packets, moves)
    )


def far_step_of(z):
    return -2 if z % 2 else 2


def across(value):
    return lax.ppermute(value, "band", [(i, i ^ 1) for i in range(32)])


RING_GROUPS = [[8 * quad + member for quad in range(4)] for member in range(8)]


def to_relays(value):
    return lax.all_gather(value, "band", axis_index_groups=RING_GROUPS, tiled=True)


def from_relays(value):
    return lax.all_to_all(value, "band", 0, 0, axis_index_groups=RING_GROUPS, tiled=True)


def rounds_of(pair_src):
    band = jnp.arange(pair_src.shape[1], dtype=jnp.int32) // 2
    z, x = band // 2, band % 2
    z_own = pair_src // 8
    key = (z_own * 8 + (z % 4) * 2 + x).reshape(-1)
    moves = ((z_own - z) % 4 != 0).astype(jnp.int32).reshape(-1)
    shared = moves * jnp.sum((key[:, None] == key[None, :]).astype(jnp.int32), axis=1)
    return jnp.maximum(1, (jnp.max(shared) + CAP - 1) // CAP)


def per_device(targets, sources, pair_tgt, pair_src):
    table = {name: jnp.asarray(value) for name, value in tables().items()}
    band = lax.axis_index("band")
    sixteen = struct((16, ROW, ROW), BF16)
    packets = [struct((CAP, ROW, ROW), BF16)] * 3

    def place_in(turn):
        turn = jnp.asarray(turn, jnp.int32)
        return jnp.stack([band // 2, band % 2, turn]).astype(jnp.int32)

    def sent_in(turn):
        return smem_call(sent_kernel, 3 * CAP, place_in(turn), pair_src)

    def found_in(turn):
        return smem_call(found_kernel, 16, place_in(turn), pair_src)

    own, ids = lax.optimization_barrier((sources.reshape(8, ROW, ROW), pair_tgt.reshape(4)))
    other = across(own)
    wanted = to_relays(targets[ids].reshape(4, ROW, ROW))
    other, wanted = lax.optimization_barrier((other, wanted))

    def pack_rows_in(sent):
        return vmem_call(pack_rows_kernel, packets, (sent, own, other), scalars=1)

    def deliver(near, found, before):
        operands = (found, own, other) + near + before
        return vmem_call(place_rows_kernel, [sixteen], operands, scalars=1)[0]

    def deliver_in(turn, before):
        return deliver(hand_over(pack_rows_in(sent_in(turn)), 1), found_in(turn), (before,))

    sent, found = sent_in(0), found_in(0)
    near = hand_over(pack_rows_in(sent), 1)
    first, wants = lax.optimization_barrier((near[0], pair_src))
    rounds = rounds_of(wants)
    rows = lax.fori_loop(1, rounds, deliver_in, deliver((first,) + near[1:], found, ()))
    where = (place_in(0), pair_src)
    (spectra,) = vmem_call(
        density_kernel,
        [sixteen],
        where + (rows, wanted, table["z_fwd"], table["y_fwd"]),
        scalars=2,
        scratch=[pltpu.SMEM((16,), jnp.int32)],
    )
    slabs = lax.all_to_all(spectra, "dom", 0, 0, tiled=True)
    (solved,) = vmem_call(
        solve_kernel,
        [sixteen],
        (slabs, table["spectrum"], table["x_fwd"], table["x_bwd"]),
        scratch=[pltpu.VMEM((8, 256, ROW), F32), pltpu.VMEM((SWEEPS - 1, 8, 256, ROW), F32)],
    )
    back = lax.all_to_all(solved, "dom", 0, 0, tiled=True)
    terms, shares = vmem_call(
        term_kernel,
        [sixteen, sixteen],
        where + (back, rows, wanted, table["z_bwd"], table["y_bwd"]),
        scalars=2,
        scratch=[pltpu.SMEM((16,), jnp.int32)],
    )

    def give_back(found):
        return hand_over(vmem_call(pack_terms_kernel, packets, (found, terms), scalars=1), -1)

    def collect(sent, found, near, before):
        outs = [struct((8, ROW, ROW), F32), struct((8, ROW, ROW), BF16)]
        operands = (sent, found, terms) + near + before
        scratch = [pltpu.VMEM((8, ROW, ROW), F32)]
        return vmem_call(add_terms_kernel, outs, operands, scalars=2, scratch=scratch)

    def collect_in(turn, before):
        found = found_in(turn)
        return collect(sent_in(turn), found, give_back(found), tuple(before))

    near = give_back(found)
    near, shares = lax.optimization_barrier((near, shares))
    shares = from_relays(shares)
    mine, partner = lax.fori_loop(1, rounds, collect_in, collect(sent, found, near, ()))
    owned = (mine + across(partner).astype(F32)).astype(BF16).reshape(sources.shape)

    (target_rows,) = vmem_call(
        target_kernel,
        [struct((4, ROW, ROW), BF16)],
        where + (pair_tgt, shares),
        scalars=3,
        scratch=[pltpu.VMEM((4, ROW, ROW), F32)],
    )
    flat = target_rows.reshape(4, targets.shape[1])
    slots = jnp.arange(targets.shape[0], dtype=jnp.int32)[:, None]
    summed = jnp.zeros(targets.shape, BF16)
    for p in range(4):
        summed = jnp.where(slots == ids[p], flat[p][None, :], summed)
    return summed, owned


def solution(mesh):
    return jax.shard_map(
        per_device,
        mesh=mesh,
        in_specs=(P("band", "dom"), P(None, "band", "dom"), P(None, "band"), P()),
        out_specs=(P("band", "dom"), P(None, "band", "dom")),
        check_vma=False,
    )
```

```python
import numpy as np
import jax
import jax.numpy as jnp
from jax import lax
from jax.experimental import pallas as pl
from jax.experimental.pallas import tpu as pltpu
from jax.sharding import PartitionSpec as P

SIDE = 64
SWEEPS = 8
RING = 16
CAP = 6
LANES = 3
ROW = 128
HALF = 64
VMEM_LIMIT = 48 * 1024 * 1024
F32 = jnp.float32
BF16 = jnp.bfloat16


def eigen_system():
    line = np.zeros((SIDE, SIDE))
    for delta, weight in ((0, 30.0), (1, -16.0), (2, 1.0)):
        for i in range(SIDE - delta):
            line[i, i + delta] = weight / 12.0
            line[i + delta, i] = weight / 12.0
    values, vectors = np.linalg.eigh(line)
    return values, vectors * np.where(vectors[0] < 0, -1.0, 1.0)[None, :]


def halves(matrix):
    high = np.asarray(matrix, np.float32).astype(jnp.bfloat16)
    low = (np.asarray(matrix, np.float64) - high.astype(np.float64)).astype(jnp.bfloat16)
    return np.stack([high, low])


def tables():
    values, v = eigen_system()
    along_z = np.kron(np.eye(2), v)
    even, odd = v[0::2], v[1::2]
    fwd = np.zeros((2, 32, 4, 2, 4, 32))
    bwd = np.zeros((2, 4, 32, 2, 32, 4))
    for x in range(4):
        fwd[0, :, x, 0, x, :] = even[:, 0::2].T
        fwd[0, :, x, 1, x, :] = odd[:, 0::2].T
        fwd[1, :, x, 0, x, :] = odd[:, 1::2].T
        fwd[1, :, x, 1, x, :] = even[:, 1::2].T
        bwd[0, x, :, 0, :, x] = even[:, 0::2]
        bwd[0, x, :, 1, :, x] = even[:, 1::2]
        bwd[1, x, :, 0, :, x] = odd[:, 1::2]
        bwd[1, x, :, 1, :, x] = odd[:, 0::2]
    along_x = np.zeros((2, SIDE, RING, 2, 4))
    for pick in range(2):
        along_x[pick, :, :, pick, :] = v.T.reshape(SIDE, RING, 4)
    rows = np.arange(SIDE).reshape(16, 2, 1, 2, 1)
    spectrum = values[rows] + values.reshape(1, 1, SIDE, 1, 1) + values.reshape(1, 1, 1, 1, SIDE)
    return dict(
        z_fwd=halves(along_z),
        z_bwd=halves(along_z.T),
        y_fwd=halves(fwd.reshape(256, 256)),
        y_bwd=halves(bwd.reshape(256, 256)),
        x_fwd=halves(along_x.reshape(ROW, ROW)),
        x_bwd=halves(along_x.reshape(ROW, ROW).T),
        spectrum=spectrum.reshape(8, 256, ROW).astype(np.float32),
    )


def split(value):
    high = value.astype(BF16)
    return high, (value - high.astype(F32)).astype(BF16)


def mm(left, right):
    return jnp.dot(left, right, preferred_element_type=F32)


def left_mul(table, value):
    high, low = split(value)
    return mm(table[0], high) + mm(table[0], low) + mm(table[1], high)


def right_mul(value, table):
    high, low = split(value)
    return mm(high, table[0]) + mm(low, table[0]) + mm(high, table[1])


def swap_halves(value):
    return jnp.concatenate([value[:, HALF:], value[:, :HALF]], axis=1)


def by_half(both):
    lane = lax.broadcasted_iota(jnp.int32, (ROW, ROW), 1)
    return jnp.where(lane < HALF, both[:ROW], both[ROW:])


def vmem_call(kernel, outs, operands, scalars=0, scratch=()):
    whole = pl.BlockSpec(memory_space=pltpu.VMEM)
    smem = pl.BlockSpec(memory_space=pltpu.SMEM)
    return pl.pallas_call(
        kernel,
        out_shape=outs,
        in_specs=[smem] * scalars + [whole] * (len(operands) - scalars),
        out_specs=[whole] * len(outs),
        scratch_shapes=list(scratch),
        compiler_params=pltpu.CompilerParams(vmem_limit_bytes=VMEM_LIMIT),
    )(*operands)


def smem_call(kernel, size, *operands):
    smem = pl.BlockSpec(memory_space=pltpu.SMEM)
    return pl.pallas_call(
        kernel,
        out_shape=struct((size,), jnp.int32),
        in_specs=[smem] * len(operands),
        out_specs=smem,
    )(*operands)


def struct(shape, dtype):
    return jax.ShapeDtypeStruct(shape, dtype)


def ring(value):
    return lax.bitwise_and(value, RING - 1)


def far_step(z):
    return 2 - 4 * lax.bitwise_and(z, 1)


def steps_of(z):
    return 1, -1, far_step(z)


def want_of(pair_src, z, x, want):
    quad, slot = lax.shift_right_logical(want, 2), lax.bitwise_and(want, 3)
    block = lax.shift_right_logical(slot, 1)
    band = 2 * (4 * quad + lax.bitwise_and(z, 3)) + x
    source = pair_src[block, 2 * band + lax.bitwise_and(slot, 1)]
    z_own = lax.shift_right_logical(source, 3)
    other = lax.bitwise_xor(lax.bitwise_and(lax.shift_right_logical(source, 2), 1), x)
    return z_own, 8 * other + 4 * block + lax.bitwise_and(source, 3)


def wants_of(pair_src, z, x):
    for want in range(16):
        yield (want,) + want_of(pair_src, z, x, jnp.int32(want))


def in_round(hit, count):
    return jnp.logical_and(hit, jnp.logical_and(count >= 0, count < CAP))


def sent_kernel(place, pair_src, sent):
    z, x = place[0], place[1]
    for lane, step in enumerate(steps_of(z)):
        for n in range(CAP):
            sent[lane * CAP + n] = -1
        count = -CAP * place[2]
        for _, z_own, row in wants_of(pair_src, z + step, x):
            hit = z_own == z

            @pl.when(in_round(hit, count))
            def _():
                sent[lane * CAP + count] = row

            count = count + hit.astype(jnp.int32)


def found_kernel(place, pair_src, found):
    z, x, turn = place[0], place[1], place[2]
    counts = [-CAP * turn] * LANES
    for want, z_own, row in wants_of(pair_src, z, x):
        at = jnp.where(jnp.logical_and(z_own == z, turn == 0), row, -1)
        for lane, step in enumerate(steps_of(z)):
            hit = z_own == ring(z - step)
            at = jnp.where(in_round(hit, counts[lane]), 16 + lane * CAP + counts[lane], at)
            counts[lane] = counts[lane] + hit.astype(jnp.int32)
        found[want] = at


def pack_rows_kernel(sent, own, other, *outs):
    for lane, out in enumerate(outs):
        for n in range(CAP):
            row = sent[lane * CAP + n]

            @pl.when(row >= 0)
            def _():
                @pl.when(row < 8)
                def _():
                    out[n] = own[row]

                @pl.when(row >= 8)
                def _():
                    out[n] = other[row - 8]


def place_rows_kernel(found, own, other, *refs):
    out = refs[-1]
    for before in refs[3:-1]:
        out[...] = before[...]
    spans = [(own, 0, 8), (other, 8, 16)]
    spans += [(near, 16 + lane * CAP, 16 + lane * CAP + CAP) for lane, near in enumerate(refs[:3])]
    for want in range(16):
        at = found[want]

        @pl.when(at >= 0)
        def _():
            for rows, first, last in spans:

                @pl.when(jnp.logical_and(at >= first, at < last))
                def _():
                    out[want] = rows[at - first]


def for_each_solved(place, pair_src, queue, body):
    z, x = place[0], place[1]

    def note(want, count):
        z_own, _ = want_of(pair_src, z, x, want)
        near = jnp.logical_or(ring(z - z_own + 1) <= 2, ring(z - z_own) == ring(far_step(z)))

        @pl.when(near)
        def _():
            queue[count] = want

        return count + near.astype(jnp.int32)

    count = lax.fori_loop(0, 16, note, jnp.int32(0))

    def step(turn, carry):
        body((queue[2 * turn], queue[jnp.minimum(2 * turn + 1, count - 1)]))
        return carry

    lax.fori_loop(0, lax.shift_right_logical(count + 1, 1), step, 0)


def density_kernel(place, pair_src, sources, wanted, z_fwd, y_fwd, spectra, queue):
    def body(wants):
        pairs = [sources[want].astype(F32) * wanted[want].astype(F32) for want in wants]
        pairs = [right_mul(pair, z_fwd) for pair in pairs]
        pairs = [jnp.concatenate([pair, swap_halves(pair)], axis=0) for pair in pairs]
        pairs = [by_half(left_mul(y_fwd, pair)).astype(BF16) for pair in pairs]
        for want, pair in zip(wants, pairs):
            spectra[want] = pair

    for_each_solved(place, pair_src, queue, body)


def solve_kernel(slabs, spectrum, x_fwd, x_bwd, out, residual, directions):
    def dot_of(value):
        return jnp.sum(value.reshape(32, 8, ROW), axis=0)

    zero = jnp.zeros((8, ROW), F32)

    def start(j, carry):
        norm, power = carry
        part = slabs[:, pl.ds(pl.multiple_of(16 * j, 16), 16), :].astype(F32)
        part = [part[:, :8].reshape(ROW, ROW), part[:, 8:].reshape(ROW, ROW)]
        part = jnp.concatenate(part, axis=1).astype(BF16)
        value = mm(x_fwd[0], part) + mm(x_fwd[1], part)
        value = jnp.concatenate([value[:, :ROW], value[:, ROW:]], axis=0)
        directions[0, j] = value
        square = value * value
        return norm + dot_of(square), power + dot_of(square * spectrum[j])

    norm, power = lax.fori_loop(0, 8, start, (zero, zero))
    norm, power = jnp.sum(norm), jnp.sum(power)
    steps, ratio = [norm / power], jnp.float32(0.0)
    for sweep in range(SWEEPS - 1):
        step = steps[-1]

        def advance(j, carry, sweep=sweep, step=step, ratio=ratio):
            new, power = carry
            lam = spectrum[j]
            if sweep == 0:
                r = d = directions[0, j]
            else:
                r = residual[j]
                d = r + ratio * directions[sweep - 1, j]
                directions[sweep, j] = d
            r = r - step * (lam * d)
            residual[j] = r
            square = r * r
            return new + dot_of(square), power + dot_of(square * lam)

        new, power = lax.fori_loop(0, 8, advance, (zero, zero))
        new, power = jnp.sum(new), jnp.sum(power)
        ratio = new / norm
        steps.append(new / (power - ratio * new / step))
        norm = new

    def finish(j, carry):
        value = steps[-1] * (residual[j] + ratio * directions[SWEEPS - 2, j])
        for sweep in range(SWEEPS - 1):
            value = value + steps[sweep] * directions[sweep, j]
        part = left_mul(x_bwd, jnp.concatenate([value[:ROW], value[ROW:]], axis=1))
        part = [part[:, :ROW].reshape(RING, 8, ROW), part[:, ROW:].reshape(RING, 8, ROW)]
        part = jnp.concatenate(part, axis=1)
        out[:, pl.ds(pl.multiple_of(16 * j, 16), 16), :] = part.astype(out.dtype)
        return carry

    lax.fori_loop(0, 8, finish, 0)


def term_kernel(place, pair_src, spectra, sources, wanted, z_bwd, y_bwd, terms, shares, queue):
    def body(wants):
        pairs = [spectra[want] for want in wants]
        pairs = [jnp.concatenate([pair, swap_halves(pair)], axis=0) for pair in pairs]
        pairs = [by_half(mm(y_bwd[0], pair) + mm(y_bwd[1], pair)) for pair in pairs]
        pairs = [-right_mul(pair, z_bwd) for pair in pairs]
        for want, pair in zip(wants, pairs):
            terms[want] = (pair * wanted[want].astype(F32)).astype(BF16)
            shares[want] = (pair * sources[want].astype(F32)).astype(BF16)

    for_each_solved(place, pair_src, queue, body)


def pack_terms_kernel(found, terms, *outs):
    for want in range(16):
        at = found[want] - 16

        @pl.when(at >= 0)
        def _():
            for lane, out in enumerate(outs):

                @pl.when(jnp.logical_and(at >= lane * CAP, at < lane * CAP + CAP))
                def _():
                    out[at - lane * CAP] = terms[want]


def add_terms_kernel(sent, found, terms, *refs):
    near, before, (mine, partner, held) = refs[:3], refs[3:-3], refs[-3:]
    mine[...] = before[0][...] if before else jnp.zeros((8, ROW, ROW), F32)
    held[...] = before[1][...].astype(F32) if before else jnp.zeros((8, ROW, ROW), F32)

    def add(row, term):
        @pl.when(row < 8)
        def _():
            mine[row] = mine[row] + term[...].astype(F32)

        @pl.when(row >= 8)
        def _():
            held[row - 8] = held[row - 8] + term[...].astype(F32)

    for want in range(16):
        at = found[want]

        @pl.when(jnp.logical_and(at >= 0, at < 16))
        def _():
            add(at, terms.at[want])

    for lane in range(3):
        for n in range(CAP):
            row = sent[lane * CAP + n]

            @pl.when(row >= 0)
            def _():
                add(row, near[lane].at[n])

    partner[...] = held[...].astype(BF16)


def target_kernel(place, pair_src, pair_tgt, shares, rows, held):
    z, x = place[0], place[1]
    quad = lax.shift_right_logical(z, 2)
    for p in range(4):
        z_own, _ = want_of(pair_src, z, x, 4 * quad + p)
        ahead = lax.bitwise_and(z - z_own, 3)
        relay = ring(z_own + jnp.where(ahead == 3, -1, jnp.where(ahead == 2, far_step(z_own), ahead)))
        held[p] = shares[4 * lax.shift_right_logical(relay, 2) + p].astype(F32)
    for p in range(4):
        same = jnp.zeros((ROW, ROW), F32)
        for other in range(4):
            hit = pair_tgt[p // 2, p % 2] == pair_tgt[other // 2, other % 2]
            same = same + jnp.where(hit, held[other], 0.0)
        rows[p] = same.astype(BF16)


def hand_over(packets, sign):
    moves = (lambda z: 1, lambda z: -1, far_step_of)
    return tuple(
        lax.ppermute(
            packet,
            "band",
            [(2 * z + x, 2 * ((z + sign * move(z)) % RING) + x) for z in range(RING) for x in range(2)],
        )
        for packet, move in zip(packets, moves)
    )


def far_step_of(z):
    return -2 if z % 2 else 2


def across(value):
    return lax.ppermute(value, "band", [(i, i ^ 1) for i in range(32)])


def along_ring(value):
    groups = [[8 * quad + member for quad in range(4)] for member in range(8)]
    return lax.all_to_all(value, "band", 0, 0, axis_index_groups=groups, tiled=True)


def rounds_of(pair_src):
    band = jnp.arange(pair_src.shape[1], dtype=jnp.int32) // 2
    z, x = band // 2, band % 2
    z_own = pair_src // 8
    key = (z_own * 8 + (z % 4) * 2 + x).reshape(-1)
    moves = ((z_own - z) % 4 != 0).astype(jnp.int32).reshape(-1)
    shared = moves * jnp.sum((key[:, None] == key[None, :]).astype(jnp.int32), axis=1)
    return jnp.maximum(1, (jnp.max(shared) + CAP - 1) // CAP)


def per_device(targets, sources, pair_tgt, pair_src):
    table = {name: jnp.asarray(value) for name, value in tables().items()}
    band = lax.axis_index("band")
    sixteen = struct((16, ROW, ROW), BF16)
    packets = [struct((CAP, ROW, ROW), BF16)] * 3

    def place_in(turn):
        turn = jnp.asarray(turn, jnp.int32)
        return jnp.stack([band // 2, band % 2, turn]).astype(jnp.int32)

    def sent_in(turn):
        return smem_call(sent_kernel, 3 * CAP, place_in(turn), pair_src)

    def found_in(turn):
        return smem_call(found_kernel, 16, place_in(turn), pair_src)

    own, ids = lax.optimization_barrier((sources.reshape(8, ROW, ROW), pair_tgt.reshape(4)))
    other = across(own)
    wanted = targets[ids].reshape(4, ROW, ROW)
    wanted = along_ring(jnp.concatenate([wanted] * 4, axis=0))

    def pack_rows_in(sent):
        return vmem_call(pack_rows_kernel, packets, (sent, own, other), scalars=1)

    def deliver(near, found, before):
        operands = (found, own, other) + near + before
        return vmem_call(place_rows_kernel, [sixteen], operands, scalars=1)[0]

    def deliver_in(turn, before):
        return deliver(hand_over(pack_rows_in(sent_in(turn)), 1), found_in(turn), (before,))

    sent, found = sent_in(0), found_in(0)
    near = hand_over(pack_rows_in(sent), 1)
    first, wants = lax.optimization_barrier((near[0], pair_src))
    rounds = rounds_of(wants)
    rows = lax.fori_loop(1, rounds, deliver_in, deliver((first,) + near[1:], found, ()))
    where = (place_in(0), pair_src)
    (spectra,) = vmem_call(
        density_kernel,
        [sixteen],
        where + (rows, wanted, table["z_fwd"], table["y_fwd"]),
        scalars=2,
        scratch=[pltpu.SMEM((16,), jnp.int32)],
    )
    slabs = lax.all_to_all(spectra, "dom", 0, 0, tiled=True)
    (solved,) = vmem_call(
        solve_kernel,
        [sixteen],
        (slabs, table["spectrum"], table["x_fwd"], table["x_bwd"]),
        scratch=[pltpu.VMEM((8, 256, ROW), F32), pltpu.VMEM((SWEEPS - 1, 8, 256, ROW), F32)],
    )
    back = lax.all_to_all(solved, "dom", 0, 0, tiled=True)
    terms, shares = vmem_call(
        term_kernel,
        [sixteen, sixteen],
        where + (back, rows, wanted, table["z_bwd"], table["y_bwd"]),
        scalars=2,
        scratch=[pltpu.SMEM((16,), jnp.int32)],
    )

    def give_back(found):
        return hand_over(vmem_call(pack_terms_kernel, packets, (found, terms), scalars=1), -1)

    def collect(sent, found, near, before):
        outs = [struct((8, ROW, ROW), F32), struct((8, ROW, ROW), BF16)]
        operands = (sent, found, terms) + near + before
        scratch = [pltpu.VMEM((8, ROW, ROW), F32)]
        return vmem_call(add_terms_kernel, outs, operands, scalars=2, scratch=scratch)

    def collect_in(turn, before):
        found = found_in(turn)
        return collect(sent_in(turn), found, give_back(found), tuple(before))

    near = give_back(found)
    shares = along_ring(shares)
    mine, partner = lax.fori_loop(1, rounds, collect_in, collect(sent, found, near, ()))
    owned = (mine + across(partner).astype(F32)).astype(BF16).reshape(sources.shape)

    (target_rows,) = vmem_call(
        target_kernel,
        [struct((4, ROW, ROW), BF16)],
        where + (pair_tgt, shares),
        scalars=3,
        scratch=[pltpu.VMEM((4, ROW, ROW), F32)],
    )
    flat = target_rows.reshape(4, targets.shape[1])
    slots = jnp.arange(targets.shape[0], dtype=jnp.int32)[:, None]
    summed = jnp.zeros(targets.shape, BF16)
    for p in range(4):
        summed = jnp.where(slots == ids[p], flat[p][None, :], summed)
    return summed, owned


def solution(mesh):
    return jax.shard_map(
        per_device,
        mesh=mesh,
        in_specs=(P("band", "dom"), P(None, "band", "dom"), P(None, "band"), P()),
        out_specs=(P("band", "dom"), P(None, "band", "dom")),
        check_vma=False,
    )
```

```python
import numpy as np
import jax
import jax.numpy as jnp
from jax import lax
from jax.experimental import pallas as pl
from jax.experimental.pallas import tpu as pltpu
from jax.sharding import PartitionSpec as P

SIDE = 64
SWEEPS = 8
RING = 16
CAP = 6
LANES = 3
ROW = 128
HALF = 64
VMEM_LIMIT = 48 * 1024 * 1024
F32 = jnp.float32
BF16 = jnp.bfloat16


def eigen_system():
    line = np.zeros((SIDE, SIDE))
    for delta, weight in ((0, 30.0), (1, -16.0), (2, 1.0)):
        for i in range(SIDE - delta):
            line[i, i + delta] = weight / 12.0
            line[i + delta, i] = weight / 12.0
    values, vectors = np.linalg.eigh(line)
    return values, vectors * np.where(vectors[0] < 0, -1.0, 1.0)[None, :]


def halves(matrix):
    high = np.asarray(matrix, np.float32).astype(jnp.bfloat16)
    low = (np.asarray(matrix, np.float64) - high.astype(np.float64)).astype(jnp.bfloat16)
    return np.stack([high, low])


def tables():
    values, v = eigen_system()
    along_z = np.kron(np.eye(2), v)
    even, odd = v[0::2], v[1::2]
    fwd = np.zeros((2, 32, 4, 2, 4, 32))
    bwd = np.zeros((2, 4, 32, 2, 32, 4))
    for x in range(4):
        fwd[0, :, x, 0, x, :] = even[:, 0::2].T
        fwd[0, :, x, 1, x, :] = odd[:, 0::2].T
        fwd[1, :, x, 0, x, :] = odd[:, 1::2].T
        fwd[1, :, x, 1, x, :] = even[:, 1::2].T
        bwd[0, x, :, 0, :, x] = even[:, 0::2]
        bwd[0, x, :, 1, :, x] = even[:, 1::2]
        bwd[1, x, :, 0, :, x] = odd[:, 1::2]
        bwd[1, x, :, 1, :, x] = odd[:, 0::2]
    along_x = np.zeros((2, SIDE, RING, 2, 4))
    for pick in range(2):
        along_x[pick, :, :, pick, :] = v.T.reshape(SIDE, RING, 4)
    rows = np.arange(SIDE).reshape(16, 2, 1, 2, 1)
    spectrum = values[rows] + values.reshape(1, 1, SIDE, 1, 1) + values.reshape(1, 1, 1, 1, SIDE)
    return dict(
        z_fwd=halves(along_z),
        z_bwd=halves(along_z.T),
        y_fwd=halves(fwd.reshape(256, 256)),
        y_bwd=halves(bwd.reshape(256, 256)),
        x_fwd=halves(along_x.reshape(ROW, ROW)),
        x_bwd=halves(along_x.reshape(ROW, ROW).T),
        spectrum=spectrum.reshape(8, 256, ROW).astype(np.float32),
    )


def split(value):
    high = value.astype(BF16)
    return high, (value - high.astype(F32)).astype(BF16)


def mm(left, right):
    return jnp.dot(left, right, preferred_element_type=F32)


def left_mul(table, value):
    high, low = split(value)
    return mm(table[0], high) + mm(table[0], low) + mm(table[1], high)


def right_mul(value, table):
    high, low = split(value)
    return mm(high, table[0]) + mm(low, table[0]) + mm(high, table[1])


def swap_halves(value):
    return jnp.concatenate([value[:, HALF:], value[:, :HALF]], axis=1)


def by_half(both):
    lane = lax.broadcasted_iota(jnp.int32, (ROW, ROW), 1)
    return jnp.where(lane < HALF, both[:ROW], both[ROW:])


def vmem_call(kernel, outs, operands, scalars=0, scratch=()):
    whole = pl.BlockSpec(memory_space=pltpu.VMEM)
    smem = pl.BlockSpec(memory_space=pltpu.SMEM)
    return pl.pallas_call(
        kernel,
        out_shape=outs,
        in_specs=[smem] * scalars + [whole] * (len(operands) - scalars),
        out_specs=[whole] * len(outs),
        scratch_shapes=list(scratch),
        compiler_params=pltpu.CompilerParams(vmem_limit_bytes=VMEM_LIMIT),
    )(*operands)


def smem_call(kernel, size, *operands):
    smem = pl.BlockSpec(memory_space=pltpu.SMEM)
    return pl.pallas_call(
        kernel,
        out_shape=struct((size,), jnp.int32),
        in_specs=[smem] * len(operands),
        out_specs=smem,
    )(*operands)


def struct(shape, dtype):
    return jax.ShapeDtypeStruct(shape, dtype)


def ring(value):
    return lax.bitwise_and(value, RING - 1)


def far_step(z):
    return 2 - 4 * lax.bitwise_and(z, 1)


def steps_of(z):
    return 1, -1, far_step(z)


def want_of(pair_src, z, x, want):
    quad, slot = lax.shift_right_logical(want, 2), lax.bitwise_and(want, 3)
    block = lax.shift_right_logical(slot, 1)
    band = 2 * (4 * quad + lax.bitwise_and(z, 3)) + x
    source = pair_src[block, 2 * band + lax.bitwise_and(slot, 1)]
    z_own = lax.shift_right_logical(source, 3)
    other = lax.bitwise_xor(lax.bitwise_and(lax.shift_right_logical(source, 2), 1), x)
    return z_own, 8 * other + 4 * block + lax.bitwise_and(source, 3)


def wants_of(pair_src, z, x):
    for want in range(16):
        yield (want,) + want_of(pair_src, z, x, jnp.int32(want))


def in_round(hit, count):
    return jnp.logical_and(hit, jnp.logical_and(count >= 0, count < CAP))


def sent_kernel(place, pair_src, sent):
    z, x = place[0], place[1]
    for lane, step in enumerate(steps_of(z)):
        for n in range(CAP):
            sent[lane * CAP + n] = -1
        count = -CAP * place[2]
        for _, z_own, row in wants_of(pair_src, z + step, x):
            hit = z_own == z

            @pl.when(in_round(hit, count))
            def _():
                sent[lane * CAP + count] = row

            count = count + hit.astype(jnp.int32)


def found_kernel(place, pair_src, found):
    z, x, turn = place[0], place[1], place[2]
    counts = [-CAP * turn] * LANES
    for want, z_own, row in wants_of(pair_src, z, x):
        at = jnp.where(jnp.logical_and(z_own == z, turn == 0), row, -1)
        for lane, step in enumerate(steps_of(z)):
            hit = z_own == ring(z - step)
            at = jnp.where(in_round(hit, counts[lane]), 16 + lane * CAP + counts[lane], at)
            counts[lane] = counts[lane] + hit.astype(jnp.int32)
        found[want] = at


def pack_rows_kernel(sent, own, other, *outs):
    for lane, out in enumerate(outs):
        for n in range(CAP):
            row = sent[lane * CAP + n]

            @pl.when(row >= 0)
            def _():
                @pl.when(row < 8)
                def _():
                    out[n] = own[row]

                @pl.when(row >= 8)
                def _():
                    out[n] = other[row - 8]


def place_rows_kernel(found, own, other, *refs):
    out = refs[-1]
    for before in refs[3:-1]:
        out[...] = before[...]
    spans = [(own, 0, 8), (other, 8, 16)]
    spans += [(near, 16 + lane * CAP, 16 + lane * CAP + CAP) for lane, near in enumerate(refs[:3])]
    for want in range(16):
        at = found[want]

        @pl.when(at >= 0)
        def _():
            for rows, first, last in spans:

                @pl.when(jnp.logical_and(at >= first, at < last))
                def _():
                    out[want] = rows[at - first]


def for_each_solved(place, pair_src, queue, body):
    z, x = place[0], place[1]

    def note(want, count):
        z_own, _ = want_of(pair_src, z, x, want)
        near = jnp.logical_or(ring(z - z_own + 1) <= 2, ring(z - z_own) == ring(far_step(z)))

        @pl.when(near)
        def _():
            queue[count] = want

        return count + near.astype(jnp.int32)

    count = lax.fori_loop(0, 16, note, jnp.int32(0))

    def step(turn, carry):
        body((queue[2 * turn], queue[jnp.minimum(2 * turn + 1, count - 1)]))
        return carry

    lax.fori_loop(0, lax.shift_right_logical(count + 1, 1), step, 0)


def density_kernel(place, pair_src, sources, wanted, z_fwd, y_fwd, spectra, queue):
    def body(wants):
        pairs = [sources[want].astype(F32) * wanted[want].astype(F32) for want in wants]
        pairs = [right_mul(pair, z_fwd) for pair in pairs]
        pairs = [jnp.concatenate([pair, swap_halves(pair)], axis=0) for pair in pairs]
        pairs = [by_half(left_mul(y_fwd, pair)).astype(BF16) for pair in pairs]
        for want, pair in zip(wants, pairs):
            spectra[want] = pair

    for_each_solved(place, pair_src, queue, body)


def solve_kernel(slabs, spectrum, x_fwd, x_bwd, out, residual, directions):
    def dot_of(value):
        return jnp.sum(value.reshape(32, 8, ROW), axis=0)

    zero = jnp.zeros((8, ROW), F32)

    def start(j, carry):
        norm, power = carry
        part = slabs[:, pl.ds(pl.multiple_of(16 * j, 16), 16), :].astype(F32)
        part = [part[:, :8].reshape(ROW, ROW), part[:, 8:].reshape(ROW, ROW)]
        part = jnp.concatenate(part, axis=1).astype(BF16)
        value = mm(x_fwd[0], part) + mm(x_fwd[1], part)
        value = jnp.concatenate([value[:, :ROW], value[:, ROW:]], axis=0)
        directions[0, j] = value
        square = value * value
        return norm + dot_of(square), power + dot_of(square * spectrum[j])

    norm, power = lax.fori_loop(0, 8, start, (zero, zero), unroll=2)
    norm, power = jnp.sum(norm), jnp.sum(power)
    steps, ratio = [norm / power], jnp.float32(0.0)
    for sweep in range(SWEEPS - 1):
        step = steps[-1]

        def advance(j, carry, sweep=sweep, step=step, ratio=ratio):
            new, power = carry
            lam = spectrum[j]
            if sweep == 0:
                r = d = directions[0, j]
            else:
                r = residual[j]
                d = r + ratio * directions[sweep - 1, j]
                directions[sweep, j] = d
            r = r - step * (lam * d)
            residual[j] = r
            square = r * r
            return new + dot_of(square), power + dot_of(square * lam)

        new, power = lax.fori_loop(0, 8, advance, (zero, zero), unroll=2)
        new, power = jnp.sum(new), jnp.sum(power)
        ratio = new / norm
        steps.append(new / (power - ratio * new / step))
        norm = new

    def finish(j, carry):
        value = steps[-1] * (residual[j] + ratio * directions[SWEEPS - 2, j])
        for sweep in range(SWEEPS - 1):
            value = value + steps[sweep] * directions[sweep, j]
        part = left_mul(x_bwd, jnp.concatenate([value[:ROW], value[ROW:]], axis=1))
        part = [part[:, :ROW].reshape(RING, 8, ROW), part[:, ROW:].reshape(RING, 8, ROW)]
        part = jnp.concatenate(part, axis=1)
        out[:, pl.ds(pl.multiple_of(16 * j, 16), 16), :] = part.astype(out.dtype)
        return carry

    lax.fori_loop(0, 8, finish, 0, unroll=2)


def term_kernel(place, pair_src, spectra, sources, wanted, z_bwd, y_bwd, terms, shares, queue):
    def body(wants):
        pairs = [spectra[want] for want in wants]
        pairs = [jnp.concatenate([pair, swap_halves(pair)], axis=0) for pair in pairs]
        pairs = [by_half(mm(y_bwd[0], pair) + mm(y_bwd[1], pair)) for pair in pairs]
        pairs = [-right_mul(pair, z_bwd) for pair in pairs]
        for want, pair in zip(wants, pairs):
            terms[want] = (pair * wanted[want].astype(F32)).astype(BF16)
            shares[want] = (pair * sources[want].astype(F32)).astype(BF16)

    for_each_solved(place, pair_src, queue, body)


def pack_terms_kernel(found, terms, *outs):
    for want in range(16):
        at = found[want] - 16

        @pl.when(at >= 0)
        def _():
            for lane, out in enumerate(outs):

                @pl.when(jnp.logical_and(at >= lane * CAP, at < lane * CAP + CAP))
                def _():
                    out[at - lane * CAP] = terms[want]


def add_terms_kernel(sent, found, terms, *refs):
    near, before, (mine, partner, held) = refs[:3], refs[3:-3], refs[-3:]
    mine[...] = before[0][...] if before else jnp.zeros((8, ROW, ROW), F32)
    held[...] = before[1][...].astype(F32) if before else jnp.zeros((8, ROW, ROW), F32)

    def add(row, term):
        @pl.when(row < 8)
        def _():
            mine[row] = mine[row] + term[...].astype(F32)

        @pl.when(row >= 8)
        def _():
            held[row - 8] = held[row - 8] + term[...].astype(F32)

    for want in range(16):
        at = found[want]

        @pl.when(jnp.logical_and(at >= 0, at < 16))
        def _():
            add(at, terms.at[want])

    for lane in range(3):
        for n in range(CAP):
            row = sent[lane * CAP + n]

            @pl.when(row >= 0)
            def _():
                add(row, near[lane].at[n])

    partner[...] = held[...].astype(BF16)


def target_kernel(place, pair_src, pair_tgt, shares, rows, held):
    z, x = place[0], place[1]
    quad = lax.shift_right_logical(z, 2)
    for p in range(4):
        z_own, _ = want_of(pair_src, z, x, 4 * quad + p)
        ahead = lax.bitwise_and(z - z_own, 3)
        relay = ring(z_own + jnp.where(ahead == 3, -1, jnp.where(ahead == 2, far_step(z_own), ahead)))
        held[p] = shares[4 * lax.shift_right_logical(relay, 2) + p].astype(F32)
    for p in range(4):
        same = jnp.zeros((ROW, ROW), F32)
        for other in range(4):
            hit = pair_tgt[p // 2, p % 2] == pair_tgt[other // 2, other % 2]
            same = same + jnp.where(hit, held[other], 0.0)
        rows[p] = same.astype(BF16)


def hand_over(packets, sign):
    moves = (lambda z: 1, lambda z: -1, far_step_of)
    return tuple(
        lax.ppermute(
            packet,
            "band",
            [(2 * z + x, 2 * ((z + sign * move(z)) % RING) + x) for z in range(RING) for x in range(2)],
        )
        for packet, move in zip(packets, moves)
    )


def far_step_of(z):
    return -2 if z % 2 else 2


def across(value):
    return lax.ppermute(value, "band", [(i, i ^ 1) for i in range(32)])


def along_ring(value):
    groups = [[8 * quad + member for quad in range(4)] for member in range(8)]
    return lax.all_to_all(value, "band", 0, 0, axis_index_groups=groups, tiled=True)


def rounds_of(pair_src):
    band = jnp.arange(pair_src.shape[1], dtype=jnp.int32) // 2
    z, x = band // 2, band % 2
    z_own = pair_src // 8
    key = (z_own * 8 + (z % 4) * 2 + x).reshape(-1)
    moves = ((z_own - z) % 4 != 0).astype(jnp.int32).reshape(-1)
    shared = moves * jnp.sum((key[:, None] == key[None, :]).astype(jnp.int32), axis=1)
    return jnp.maximum(1, (jnp.max(shared) + CAP - 1) // CAP)


def per_device(targets, sources, pair_tgt, pair_src):
    table = {name: jnp.asarray(value) for name, value in tables().items()}
    band = lax.axis_index("band")
    sixteen = struct((16, ROW, ROW), BF16)
    packets = [struct((CAP, ROW, ROW), BF16)] * 3

    def place_in(turn):
        turn = jnp.asarray(turn, jnp.int32)
        return jnp.stack([band // 2, band % 2, turn]).astype(jnp.int32)

    def sent_in(turn):
        return smem_call(sent_kernel, 3 * CAP, place_in(turn), pair_src)

    def found_in(turn):
        return smem_call(found_kernel, 16, place_in(turn), pair_src)

    own, ids = lax.optimization_barrier((sources.reshape(8, ROW, ROW), pair_tgt.reshape(4)))
    other = across(own)
    wanted = targets[ids].reshape(4, ROW, ROW)
    wanted = along_ring(jnp.concatenate([wanted] * 4, axis=0))

    def pack_rows_in(sent):
        return vmem_call(pack_rows_kernel, packets, (sent, own, other), scalars=1)

    def deliver(near, found, before):
        operands = (found, own, other) + near + before
        return vmem_call(place_rows_kernel, [sixteen], operands, scalars=1)[0]

    def deliver_in(turn, before):
        return deliver(hand_over(pack_rows_in(sent_in(turn)), 1), found_in(turn), (before,))

    sent, found = sent_in(0), found_in(0)
    near = hand_over(pack_rows_in(sent), 1)
    first, wants = lax.optimization_barrier((near[0], pair_src))
    rounds = rounds_of(wants)
    rows = lax.fori_loop(1, rounds, deliver_in, deliver((first,) + near[1:], found, ()))
    where = (place_in(0), pair_src)
    (spectra,) = vmem_call(
        density_kernel,
        [sixteen],
        where + (rows, wanted, table["z_fwd"], table["y_fwd"]),
        scalars=2,
        scratch=[pltpu.SMEM((16,), jnp.int32)],
    )
    slabs = lax.all_to_all(spectra, "dom", 0, 0, tiled=True)
    (solved,) = vmem_call(
        solve_kernel,
        [sixteen],
        (slabs, table["spectrum"], table["x_fwd"], table["x_bwd"]),
        scratch=[pltpu.VMEM((8, 256, ROW), F32), pltpu.VMEM((SWEEPS - 1, 8, 256, ROW), F32)],
    )
    back = lax.all_to_all(solved, "dom", 0, 0, tiled=True)
    terms, shares = vmem_call(
        term_kernel,
        [sixteen, sixteen],
        where + (back, rows, wanted, table["z_bwd"], table["y_bwd"]),
        scalars=2,
        scratch=[pltpu.SMEM((16,), jnp.int32)],
    )

    def give_back(found):
        return hand_over(vmem_call(pack_terms_kernel, packets, (found, terms), scalars=1), -1)

    def collect(sent, found, near, before):
        outs = [struct((8, ROW, ROW), F32), struct((8, ROW, ROW), BF16)]
        operands = (sent, found, terms) + near + before
        scratch = [pltpu.VMEM((8, ROW, ROW), F32)]
        return vmem_call(add_terms_kernel, outs, operands, scalars=2, scratch=scratch)

    def collect_in(turn, before):
        found = found_in(turn)
        return collect(sent_in(turn), found, give_back(found), tuple(before))

    near = give_back(found)
    shares = along_ring(shares)
    mine, partner = lax.fori_loop(1, rounds, collect_in, collect(sent, found, near, ()))
    (target_rows,) = vmem_call(
        target_kernel,
        [struct((4, ROW, ROW), BF16)],
        where + (pair_tgt, shares),
        scalars=3,
        scratch=[pltpu.VMEM((4, ROW, ROW), F32)],
    )
    partner, flat = lax.optimization_barrier((across(partner), target_rows.reshape(4, targets.shape[1])))
    owned = (mine + partner.astype(F32)).astype(BF16).reshape(sources.shape)
    slots = jnp.arange(targets.shape[0], dtype=jnp.int32)[:, None]
    summed = jnp.zeros(targets.shape, BF16)
    for p in range(4):
        summed = jnp.where(slots == ids[p], flat[p][None, :], summed)
    return summed, owned


def solution(mesh):
    return jax.shard_map(
        per_device,
        mesh=mesh,
        in_specs=(P("band", "dom"), P(None, "band", "dom"), P(None, "band"), P()),
        out_specs=(P("band", "dom"), P(None, "band", "dom")),
        check_vma=False,
    )
```

```python
import numpy as np
import jax
import jax.numpy as jnp
from jax import lax
from jax.experimental import pallas as pl
from jax.experimental.pallas import tpu as pltpu
from jax.sharding import PartitionSpec as P

SIDE = 64
SWEEPS = 8
RING = 16
CAP = 6
LANES = 3
ROW = 128
HALF = 64
VMEM_LIMIT = 48 * 1024 * 1024
F32 = jnp.float32
BF16 = jnp.bfloat16


def eigen_system():
    line = np.zeros((SIDE, SIDE))
    for delta, weight in ((0, 30.0), (1, -16.0), (2, 1.0)):
        for i in range(SIDE - delta):
            line[i, i + delta] = weight / 12.0
            line[i + delta, i] = weight / 12.0
    values, vectors = np.linalg.eigh(line)
    return values, vectors * np.where(vectors[0] < 0, -1.0, 1.0)[None, :]


def halves(matrix):
    high = np.asarray(matrix, np.float32).astype(jnp.bfloat16)
    low = (np.asarray(matrix, np.float64) - high.astype(np.float64)).astype(jnp.bfloat16)
    return np.stack([high, low])


def tables():
    values, v = eigen_system()
    along_z = np.kron(np.eye(2), v)
    even, odd = v[0::2], v[1::2]
    fwd = np.zeros((2, 32, 4, 2, 4, 32))
    bwd = np.zeros((2, 4, 32, 2, 32, 4))
    for x in range(4):
        fwd[0, :, x, 0, x, :] = even[:, 0::2].T
        fwd[0, :, x, 1, x, :] = odd[:, 0::2].T
        fwd[1, :, x, 0, x, :] = odd[:, 1::2].T
        fwd[1, :, x, 1, x, :] = even[:, 1::2].T
        bwd[0, x, :, 0, :, x] = even[:, 0::2]
        bwd[0, x, :, 1, :, x] = even[:, 1::2]
        bwd[1, x, :, 0, :, x] = odd[:, 1::2]
        bwd[1, x, :, 1, :, x] = odd[:, 0::2]
    along_x = np.zeros((2, SIDE, RING, 2, 4))
    for pick in range(2):
        along_x[pick, :, :, pick, :] = v.T.reshape(SIDE, RING, 4)
    rows = np.arange(SIDE).reshape(16, 2, 1, 2, 1)
    spectrum = values[rows] + values.reshape(1, 1, SIDE, 1, 1) + values.reshape(1, 1, 1, 1, SIDE)
    return dict(
        z_fwd=halves(along_z),
        z_bwd=halves(along_z.T),
        y_fwd=halves(fwd.reshape(256, 256)),
        y_bwd=halves(bwd.reshape(256, 256)),
        x_fwd=halves(along_x.reshape(ROW, ROW)),
        x_bwd=halves(along_x.reshape(ROW, ROW).T),
        spectrum=spectrum.reshape(8, 256, ROW).astype(np.float32),
    )


def split(value):
    high = value.astype(BF16)
    return high, (value - high.astype(F32)).astype(BF16)


def mm(left, right):
    return jnp.dot(left, right, preferred_element_type=F32)


def left_mul(table, value):
    high, low = split(value)
    return mm(table[0], high) + mm(table[0], low) + mm(table[1], high)


def right_mul(value, table):
    high, low = split(value)
    return mm(high, table[0]) + mm(low, table[0]) + mm(high, table[1])


def swap_halves(value):
    return jnp.concatenate([value[:, HALF:], value[:, :HALF]], axis=1)


def by_half(both):
    lane = lax.broadcasted_iota(jnp.int32, (ROW, ROW), 1)
    return jnp.where(lane < HALF, both[:ROW], both[ROW:])


def vmem_call(kernel, outs, operands, scalars=0, scratch=()):
    whole = pl.BlockSpec(memory_space=pltpu.VMEM)
    smem = pl.BlockSpec(memory_space=pltpu.SMEM)
    return pl.pallas_call(
        kernel,
        out_shape=outs,
        in_specs=[smem] * scalars + [whole] * (len(operands) - scalars),
        out_specs=[whole] * len(outs),
        scratch_shapes=list(scratch),
        compiler_params=pltpu.CompilerParams(vmem_limit_bytes=VMEM_LIMIT),
    )(*operands)


def smem_call(kernel, size, *operands):
    smem = pl.BlockSpec(memory_space=pltpu.SMEM)
    return pl.pallas_call(
        kernel,
        out_shape=struct((size,), jnp.int32),
        in_specs=[smem] * len(operands),
        out_specs=smem,
    )(*operands)


def struct(shape, dtype):
    return jax.ShapeDtypeStruct(shape, dtype)


def ring(value):
    return lax.bitwise_and(value, RING - 1)


def far_step(z):
    return 2 - 4 * lax.bitwise_and(z, 1)


def steps_of(z):
    return 1, -1, far_step(z)


def want_of(pair_src, z, x, want):
    quad, slot = lax.shift_right_logical(want, 2), lax.bitwise_and(want, 3)
    block = lax.shift_right_logical(slot, 1)
    band = 2 * (4 * quad + lax.bitwise_and(z, 3)) + x
    source = pair_src[block, 2 * band + lax.bitwise_and(slot, 1)]
    z_own = lax.shift_right_logical(source, 3)
    other = lax.bitwise_xor(lax.bitwise_and(lax.shift_right_logical(source, 2), 1), x)
    return z_own, 8 * other + 4 * block + lax.bitwise_and(source, 3)


def wants_of(pair_src, z, x):
    for want in range(16):
        yield (want,) + want_of(pair_src, z, x, jnp.int32(want))


def in_round(hit, count):
    return jnp.logical_and(hit, jnp.logical_and(count >= 0, count < CAP))


def sent_kernel(place, pair_src, sent):
    z, x = place[0], place[1]
    for lane, step in enumerate(steps_of(z)):
        for n in range(CAP):
            sent[lane * CAP + n] = -1
        count = -CAP * place[2]
        for _, z_own, row in wants_of(pair_src, z + step, x):
            hit = z_own == z

            @pl.when(in_round(hit, count))
            def _():
                sent[lane * CAP + count] = row

            count = count + hit.astype(jnp.int32)


def found_kernel(place, pair_src, found):
    z, x, turn = place[0], place[1], place[2]
    counts = [-CAP * turn] * LANES
    for want, z_own, row in wants_of(pair_src, z, x):
        at = jnp.where(jnp.logical_and(z_own == z, turn == 0), row, -1)
        for lane, step in enumerate(steps_of(z)):
            hit = z_own == ring(z - step)
            at = jnp.where(in_round(hit, counts[lane]), 16 + lane * CAP + counts[lane], at)
            counts[lane] = counts[lane] + hit.astype(jnp.int32)
        found[want] = at


def pack_rows_kernel(sent, own, other, *outs):
    for lane, out in enumerate(outs):
        for n in range(CAP):
            row = sent[lane * CAP + n]

            @pl.when(row >= 0)
            def _():
                @pl.when(row < 8)
                def _():
                    out[n] = own[row]

                @pl.when(row >= 8)
                def _():
                    out[n] = other[row - 8]


def place_rows_kernel(found, own, other, *refs):
    out = refs[-1]
    for before in refs[3:-1]:
        out[...] = before[...]
    spans = [(own, 0, 8), (other, 8, 16)]
    spans += [(near, 16 + lane * CAP, 16 + lane * CAP + CAP) for lane, near in enumerate(refs[:3])]
    for want in range(16):
        at = found[want]

        @pl.when(at >= 0)
        def _():
            for rows, first, last in spans:

                @pl.when(jnp.logical_and(at >= first, at < last))
                def _():
                    out[want] = rows[at - first]


def for_each_solved(place, pair_src, queue, body):
    z, x = place[0], place[1]

    def note(want, count):
        z_own, _ = want_of(pair_src, z, x, want)
        near = jnp.logical_or(ring(z - z_own + 1) <= 2, ring(z - z_own) == ring(far_step(z)))

        @pl.when(near)
        def _():
            queue[count] = want

        return count + near.astype(jnp.int32)

    count = lax.fori_loop(0, 16, note, jnp.int32(0))

    def step(turn, carry):
        body((queue[2 * turn], queue[jnp.minimum(2 * turn + 1, count - 1)]))
        return carry

    lax.fori_loop(0, lax.shift_right_logical(count + 1, 1), step, 0)


def density_kernel(place, pair_src, sources, wanted, z_fwd, y_fwd, spectra, queue):
    def body(wants):
        pairs = [sources[want].astype(F32) * wanted[want].astype(F32) for want in wants]
        pairs = [right_mul(pair, z_fwd) for pair in pairs]
        pairs = [jnp.concatenate([pair, swap_halves(pair)], axis=0) for pair in pairs]
        pairs = [by_half(left_mul(y_fwd, pair)).astype(BF16) for pair in pairs]
        for want, pair in zip(wants, pairs):
            spectra[want] = pair

    for_each_solved(place, pair_src, queue, body)


def solve_kernel(slabs, spectrum, x_fwd, x_bwd, out, residual, directions):
    def dot_of(value):
        return jnp.sum(value.reshape(32, 8, ROW), axis=0)

    zero = jnp.zeros((8, ROW), F32)

    def start(j, carry):
        norm, power = carry
        part = slabs[:, pl.ds(pl.multiple_of(16 * j, 16), 16), :].astype(F32)
        part = [part[:, :8].reshape(ROW, ROW), part[:, 8:].reshape(ROW, ROW)]
        part = jnp.concatenate(part, axis=1).astype(BF16)
        value = mm(x_fwd[0], part) + mm(x_fwd[1], part)
        value = jnp.concatenate([value[:, :ROW], value[:, ROW:]], axis=0)
        directions[0, j] = value
        square = value * value
        return norm + dot_of(square), power + dot_of(square * spectrum[j])

    norm, power = lax.fori_loop(0, 8, start, (zero, zero), unroll=4)
    norm, power = jnp.sum(norm), jnp.sum(power)
    steps, ratio = [norm / power], jnp.float32(0.0)
    for sweep in range(SWEEPS - 1):
        step = steps[-1]

        def advance(j, carry, sweep=sweep, step=step, ratio=ratio):
            new, power = carry
            lam = spectrum[j]
            if sweep == 0:
                r = d = directions[0, j]
            else:
                r = residual[j]
                d = r + ratio * directions[sweep - 1, j]
                directions[sweep, j] = d
            r = r - step * (lam * d)
            residual[j] = r
            square = r * r
            return new + dot_of(square), power + dot_of(square * lam)

        new, power = lax.fori_loop(0, 8, advance, (zero, zero), unroll=4)
        new, power = jnp.sum(new), jnp.sum(power)
        ratio = new / norm
        steps.append(new / (power - ratio * new / step))
        norm = new

    def finish(j, carry):
        value = steps[-1] * (residual[j] + ratio * directions[SWEEPS - 2, j])
        for sweep in range(SWEEPS - 1):
            value = value + steps[sweep] * directions[sweep, j]
        part = left_mul(x_bwd, jnp.concatenate([value[:ROW], value[ROW:]], axis=1))
        part = [part[:, :ROW].reshape(RING, 8, ROW), part[:, ROW:].reshape(RING, 8, ROW)]
        part = jnp.concatenate(part, axis=1)
        out[:, pl.ds(pl.multiple_of(16 * j, 16), 16), :] = part.astype(out.dtype)
        return carry

    lax.fori_loop(0, 8, finish, 0, unroll=4)


def term_kernel(place, pair_src, spectra, sources, wanted, z_bwd, y_bwd, terms, shares, queue):
    def body(wants):
        pairs = [spectra[want] for want in wants]
        pairs = [jnp.concatenate([pair, swap_halves(pair)], axis=0) for pair in pairs]
        pairs = [by_half(mm(y_bwd[0], pair) + mm(y_bwd[1], pair)) for pair in pairs]
        pairs = [-right_mul(pair, z_bwd) for pair in pairs]
        for want, pair in zip(wants, pairs):
            terms[want] = (pair * wanted[want].astype(F32)).astype(BF16)
            shares[want] = (pair * sources[want].astype(F32)).astype(BF16)

    for_each_solved(place, pair_src, queue, body)


def pack_terms_kernel(found, terms, *outs):
    for want in range(16):
        at = found[want] - 16

        @pl.when(at >= 0)
        def _():
            for lane, out in enumerate(outs):

                @pl.when(jnp.logical_and(at >= lane * CAP, at < lane * CAP + CAP))
                def _():
                    out[at - lane * CAP] = terms[want]


def add_terms_kernel(sent, found, terms, *refs):
    near, before, (mine, partner, held) = refs[:3], refs[3:-3], refs[-3:]
    mine[...] = before[0][...] if before else jnp.zeros((8, ROW, ROW), F32)
    held[...] = before[1][...].astype(F32) if before else jnp.zeros((8, ROW, ROW), F32)

    def add(row, term):
        @pl.when(row < 8)
        def _():
            mine[row] = mine[row] + term[...].astype(F32)

        @pl.when(row >= 8)
        def _():
            held[row - 8] = held[row - 8] + term[...].astype(F32)

    for want in range(16):
        at = found[want]

        @pl.when(jnp.logical_and(at >= 0, at < 16))
        def _():
            add(at, terms.at[want])

    for lane in range(3):
        for n in range(CAP):
            row = sent[lane * CAP + n]

            @pl.when(row >= 0)
            def _():
                add(row, near[lane].at[n])

    partner[...] = held[...].astype(BF16)


def target_kernel(place, pair_src, pair_tgt, shares, rows, held):
    z, x = place[0], place[1]
    quad = lax.shift_right_logical(z, 2)
    for p in range(4):
        z_own, _ = want_of(pair_src, z, x, 4 * quad + p)
        ahead = lax.bitwise_and(z - z_own, 3)
        relay = ring(z_own + jnp.where(ahead == 3, -1, jnp.where(ahead == 2, far_step(z_own), ahead)))
        held[p] = shares[4 * lax.shift_right_logical(relay, 2) + p].astype(F32)
    for p in range(4):
        same = jnp.zeros((ROW, ROW), F32)
        for other in range(4):
            hit = pair_tgt[p // 2, p % 2] == pair_tgt[other // 2, other % 2]
            same = same + jnp.where(hit, held[other], 0.0)
        rows[p] = same.astype(BF16)


def hand_over(packets, sign):
    moves = (lambda z: 1, lambda z: -1, far_step_of)
    return tuple(
        lax.ppermute(
            packet,
            "band",
            [(2 * z + x, 2 * ((z + sign * move(z)) % RING) + x) for z in range(RING) for x in range(2)],
        )
        for packet, move in zip(packets, moves)
    )


def far_step_of(z):
    return -2 if z % 2 else 2


def across(value):
    return lax.ppermute(value, "band", [(i, i ^ 1) for i in range(32)])


def along_ring(value):
    groups = [[8 * quad + member for quad in range(4)] for member in range(8)]
    return lax.all_to_all(value, "band", 0, 0, axis_index_groups=groups, tiled=True)


def rounds_of(pair_src):
    band = jnp.arange(pair_src.shape[1], dtype=jnp.int32) // 2
    z, x = band // 2, band % 2
    z_own = pair_src // 8
    key = (z_own * 8 + (z % 4) * 2 + x).reshape(-1)
    moves = ((z_own - z) % 4 != 0).astype(jnp.int32).reshape(-1)
    shared = moves * jnp.sum((key[:, None] == key[None, :]).astype(jnp.int32), axis=1)
    return jnp.maximum(1, (jnp.max(shared) + CAP - 1) // CAP)


def per_device(targets, sources, pair_tgt, pair_src):
    table = {name: jnp.asarray(value) for name, value in tables().items()}
    band = lax.axis_index("band")
    sixteen = struct((16, ROW, ROW), BF16)
    packets = [struct((CAP, ROW, ROW), BF16)] * 3

    def place_in(turn):
        turn = jnp.asarray(turn, jnp.int32)
        return jnp.stack([band // 2, band % 2, turn]).astype(jnp.int32)

    def sent_in(turn):
        return smem_call(sent_kernel, 3 * CAP, place_in(turn), pair_src)

    def found_in(turn):
        return smem_call(found_kernel, 16, place_in(turn), pair_src)

    own, ids = lax.optimization_barrier((sources.reshape(8, ROW, ROW), pair_tgt.reshape(4)))
    other = across(own)
    wanted = targets[ids].reshape(4, ROW, ROW)
    wanted = along_ring(jnp.concatenate([wanted] * 4, axis=0))

    def pack_rows_in(sent):
        return vmem_call(pack_rows_kernel, packets, (sent, own, other), scalars=1)

    def deliver(near, found, before):
        operands = (found, own, other) + near + before
        return vmem_call(place_rows_kernel, [sixteen], operands, scalars=1)[0]

    def deliver_in(turn, before):
        return deliver(hand_over(pack_rows_in(sent_in(turn)), 1), found_in(turn), (before,))

    sent, found = sent_in(0), found_in(0)
    near = hand_over(pack_rows_in(sent), 1)
    first, wants = lax.optimization_barrier((near[0], pair_src))
    rounds = rounds_of(wants)
    rows = lax.fori_loop(1, rounds, deliver_in, deliver((first,) + near[1:], found, ()))
    where = (place_in(0), pair_src)
    (spectra,) = vmem_call(
        density_kernel,
        [sixteen],
        where + (rows, wanted, table["z_fwd"], table["y_fwd"]),
        scalars=2,
        scratch=[pltpu.SMEM((16,), jnp.int32)],
    )
    slabs = lax.all_to_all(spectra, "dom", 0, 0, tiled=True)
    (solved,) = vmem_call(
        solve_kernel,
        [sixteen],
        (slabs, table["spectrum"], table["x_fwd"], table["x_bwd"]),
        scratch=[pltpu.VMEM((8, 256, ROW), F32), pltpu.VMEM((SWEEPS - 1, 8, 256, ROW), F32)],
    )
    back = lax.all_to_all(solved, "dom", 0, 0, tiled=True)
    terms, shares = vmem_call(
        term_kernel,
        [sixteen, sixteen],
        where + (back, rows, wanted, table["z_bwd"], table["y_bwd"]),
        scalars=2,
        scratch=[pltpu.SMEM((16,), jnp.int32)],
    )

    def give_back(found):
        return hand_over(vmem_call(pack_terms_kernel, packets, (found, terms), scalars=1), -1)

    def collect(sent, found, near, before):
        outs = [struct((8, ROW, ROW), F32), struct((8, ROW, ROW), BF16)]
        operands = (sent, found, terms) + near + before
        scratch = [pltpu.VMEM((8, ROW, ROW), F32)]
        return vmem_call(add_terms_kernel, outs, operands, scalars=2, scratch=scratch)

    def collect_in(turn, before):
        found = found_in(turn)
        return collect(sent_in(turn), found, give_back(found), tuple(before))

    near = give_back(found)
    shares = along_ring(shares)
    mine, partner = lax.fori_loop(1, rounds, collect_in, collect(sent, found, near, ()))
    (target_rows,) = vmem_call(
        target_kernel,
        [struct((4, ROW, ROW), BF16)],
        where + (pair_tgt, shares),
        scalars=3,
        scratch=[pltpu.VMEM((4, ROW, ROW), F32)],
    )
    flat = target_rows.reshape(4, targets.shape[1])
    slots = jnp.arange(targets.shape[0], dtype=jnp.int32)[:, None]
    summed = jnp.zeros(targets.shape, BF16)
    for p in range(4):
        summed = jnp.where(slots == ids[p], flat[p][None, :], summed)
    partner, summed = lax.optimization_barrier((across(partner), summed))
    owned = (mine + partner.astype(F32)).astype(BF16).reshape(sources.shape)
    return summed, owned


def solution(mesh):
    return jax.shard_map(
        per_device,
        mesh=mesh,
        in_specs=(P("band", "dom"), P(None, "band", "dom"), P(None, "band"), P()),
        out_specs=(P("band", "dom"), P(None, "band", "dom")),
        check_vma=False,
    )
```

```python
import numpy as np
import jax
import jax.numpy as jnp
from jax import lax
from jax.experimental import pallas as pl
from jax.experimental.pallas import tpu as pltpu
from jax.sharding import PartitionSpec as P

SIDE = 64
SWEEPS = 8
RING = 16
CAP = 6
LANES = 3
ROW = 128
HALF = 64
VMEM_LIMIT = 48 * 1024 * 1024
F32 = jnp.float32
BF16 = jnp.bfloat16


def eigen_system():
    line = np.zeros((SIDE, SIDE))
    for delta, weight in ((0, 30.0), (1, -16.0), (2, 1.0)):
        for i in range(SIDE - delta):
            line[i, i + delta] = weight / 12.0
            line[i + delta, i] = weight / 12.0
    values, vectors = np.linalg.eigh(line)
    return values, vectors * np.where(vectors[0] < 0, -1.0, 1.0)[None, :]


def halves(matrix):
    high = np.asarray(matrix, np.float32).astype(jnp.bfloat16)
    low = (np.asarray(matrix, np.float64) - high.astype(np.float64)).astype(jnp.bfloat16)
    return np.stack([high, low])


def tables():
    values, v = eigen_system()
    along_z = np.kron(np.eye(2), v)
    even, odd = v[0::2], v[1::2]
    fwd = np.zeros((2, 32, 4, 2, 4, 32))
    bwd = np.zeros((2, 4, 32, 2, 32, 4))
    for x in range(4):
        fwd[0, :, x, 0, x, :] = even[:, 0::2].T
        fwd[0, :, x, 1, x, :] = odd[:, 0::2].T
        fwd[1, :, x, 0, x, :] = odd[:, 1::2].T
        fwd[1, :, x, 1, x, :] = even[:, 1::2].T
        bwd[0, x, :, 0, :, x] = even[:, 0::2]
        bwd[0, x, :, 1, :, x] = even[:, 1::2]
        bwd[1, x, :, 0, :, x] = odd[:, 1::2]
        bwd[1, x, :, 1, :, x] = odd[:, 0::2]
    along_x = np.zeros((2, SIDE, RING, 2, 4))
    for pick in range(2):
        along_x[pick, :, :, pick, :] = v.T.reshape(SIDE, RING, 4)
    rows = np.arange(SIDE).reshape(16, 2, 1, 2, 1)
    spectrum = values[rows] + values.reshape(1, 1, SIDE, 1, 1) + values.reshape(1, 1, 1, 1, SIDE)
    return dict(
        z_fwd=halves(along_z),
        z_bwd=halves(along_z.T),
        y_fwd=halves(fwd.reshape(256, 256)),
        y_bwd=halves(bwd.reshape(256, 256)),
        x_fwd=halves(along_x.reshape(ROW, ROW)),
        x_bwd=halves(along_x.reshape(ROW, ROW).T),
        spectrum=spectrum.reshape(8, 256, ROW).astype(np.float32),
    )


def split(value):
    high = value.astype(BF16)
    return high, (value - high.astype(F32)).astype(BF16)


def mm(left, right):
    return jnp.dot(left, right, preferred_element_type=F32)


def left_mul(table, value):
    high, low = split(value)
    return mm(table[0], high) + mm(table[0], low) + mm(table[1], high)


def right_mul(value, table):
    high, low = split(value)
    return mm(high, table[0]) + mm(low, table[0]) + mm(high, table[1])


def swap_halves(value):
    return jnp.concatenate([value[:, HALF:], value[:, :HALF]], axis=1)


def by_half(both):
    lane = lax.broadcasted_iota(jnp.int32, (ROW, ROW), 1)
    return jnp.where(lane < HALF, both[:ROW], both[ROW:])


def vmem_call(kernel, outs, operands, scalars=0, scratch=()):
    whole = pl.BlockSpec(memory_space=pltpu.VMEM)
    smem = pl.BlockSpec(memory_space=pltpu.SMEM)
    return pl.pallas_call(
        kernel,
        out_shape=outs,
        in_specs=[smem] * scalars + [whole] * (len(operands) - scalars),
        out_specs=[whole] * len(outs),
        scratch_shapes=list(scratch),
        compiler_params=pltpu.CompilerParams(vmem_limit_bytes=VMEM_LIMIT),
    )(*operands)


def smem_call(kernel, size, *operands):
    smem = pl.BlockSpec(memory_space=pltpu.SMEM)
    return pl.pallas_call(
        kernel,
        out_shape=struct((size,), jnp.int32),
        in_specs=[smem] * len(operands),
        out_specs=smem,
    )(*operands)


def struct(shape, dtype):
    return jax.ShapeDtypeStruct(shape, dtype)


def ring(value):
    return lax.bitwise_and(value, RING - 1)


def far_step(z):
    return 2 - 4 * lax.bitwise_and(z, 1)


def steps_of(z):
    return 1, -1, far_step(z)


def want_of(pair_src, z, x, want):
    quad, slot = lax.shift_right_logical(want, 2), lax.bitwise_and(want, 3)
    block = lax.shift_right_logical(slot, 1)
    band = 2 * (4 * quad + lax.bitwise_and(z, 3)) + x
    source = pair_src[block, 2 * band + lax.bitwise_and(slot, 1)]
    z_own = lax.shift_right_logical(source, 3)
    other = lax.bitwise_xor(lax.bitwise_and(lax.shift_right_logical(source, 2), 1), x)
    return z_own, 8 * other + 4 * block + lax.bitwise_and(source, 3)


def wants_of(pair_src, z, x):
    for want in range(16):
        yield (want,) + want_of(pair_src, z, x, jnp.int32(want))


def in_round(hit, count):
    return jnp.logical_and(hit, jnp.logical_and(count >= 0, count < CAP))


def sent_kernel(place, pair_src, sent):
    z, x = place[0], place[1]
    for lane, step in enumerate(steps_of(z)):
        for n in range(CAP):
            sent[lane * CAP + n] = -1
        count = -CAP * place[2]
        for _, z_own, row in wants_of(pair_src, z + step, x):
            hit = z_own == z

            @pl.when(in_round(hit, count))
            def _():
                sent[lane * CAP + count] = row

            count = count + hit.astype(jnp.int32)


def found_kernel(place, pair_src, found):
    z, x, turn = place[0], place[1], place[2]
    counts = [-CAP * turn] * LANES
    for want, z_own, row in wants_of(pair_src, z, x):
        at = jnp.where(jnp.logical_and(z_own == z, turn == 0), row, -1)
        for lane, step in enumerate(steps_of(z)):
            hit = z_own == ring(z - step)
            at = jnp.where(in_round(hit, counts[lane]), 16 + lane * CAP + counts[lane], at)
            counts[lane] = counts[lane] + hit.astype(jnp.int32)
        found[want] = at


def pack_rows_kernel(sent, own, other, *outs):
    for lane, out in enumerate(outs):
        for n in range(CAP):
            row = sent[lane * CAP + n]

            @pl.when(row >= 0)
            def _():
                @pl.when(row < 8)
                def _():
                    out[n] = own[row]

                @pl.when(row >= 8)
                def _():
                    out[n] = other[row - 8]


def place_rows_kernel(found, own, other, *refs):
    out = refs[-1]
    for before in refs[3:-1]:
        out[...] = before[...]
    spans = [(own, 0, 8), (other, 8, 16)]
    spans += [(near, 16 + lane * CAP, 16 + lane * CAP + CAP) for lane, near in enumerate(refs[:3])]
    for want in range(16):
        at = found[want]

        @pl.when(at >= 0)
        def _():
            for rows, first, last in spans:

                @pl.when(jnp.logical_and(at >= first, at < last))
                def _():
                    out[want] = rows[at - first]


def for_each_solved(place, pair_src, queue, body):
    z, x = place[0], place[1]

    def note(want, count):
        z_own, _ = want_of(pair_src, z, x, want)
        near = jnp.logical_or(ring(z - z_own + 1) <= 2, ring(z - z_own) == ring(far_step(z)))

        @pl.when(near)
        def _():
            queue[count] = want

        return count + near.astype(jnp.int32)

    count = lax.fori_loop(0, 16, note, jnp.int32(0))

    def step(turn, carry):
        body((queue[2 * turn], queue[jnp.minimum(2 * turn + 1, count - 1)]))
        return carry

    lax.fori_loop(0, lax.shift_right_logical(count + 1, 1), step, 0)


def density_kernel(place, pair_src, sources, wanted, z_fwd, y_fwd, spectra, queue):
    def body(wants):
        pairs = [sources[want].astype(F32) * wanted[want].astype(F32) for want in wants]
        pairs = [right_mul(pair, z_fwd) for pair in pairs]
        pairs = [jnp.concatenate([pair, swap_halves(pair)], axis=0) for pair in pairs]
        pairs = [by_half(left_mul(y_fwd, pair)).astype(BF16) for pair in pairs]
        for want, pair in zip(wants, pairs):
            spectra[want] = pair

    for_each_solved(place, pair_src, queue, body)


def solve_kernel(slabs, spectrum, x_fwd, x_bwd, out, residual, directions):
    def dot_of(value):
        return jnp.sum(value.reshape(32, 8, ROW), axis=0)

    zero = jnp.zeros((8, ROW), F32)

    def start(j, carry):
        norm, power = carry
        part = slabs[:, pl.ds(pl.multiple_of(16 * j, 16), 16), :].astype(F32)
        part = [part[:, :8].reshape(ROW, ROW), part[:, 8:].reshape(ROW, ROW)]
        part = jnp.concatenate(part, axis=1).astype(BF16)
        value = mm(x_fwd[0], part) + mm(x_fwd[1], part)
        value = jnp.concatenate([value[:, :ROW], value[:, ROW:]], axis=0)
        directions[0, j] = value
        square = value * value
        return norm + dot_of(square), power + dot_of(square * spectrum[j])

    norm, power = lax.fori_loop(0, 8, start, (zero, zero), unroll=8)
    norm, power = jnp.sum(norm), jnp.sum(power)
    steps, ratio = [norm / power], jnp.float32(0.0)
    for sweep in range(SWEEPS - 1):
        step = steps[-1]

        def advance(j, carry, sweep=sweep, step=step, ratio=ratio):
            new, power = carry
            lam = spectrum[j]
            if sweep == 0:
                r = d = directions[0, j]
            else:
                r = residual[j]
                d = r + ratio * directions[sweep - 1, j]
                directions[sweep, j] = d
            r = r - step * (lam * d)
            residual[j] = r
            square = r * r
            return new + dot_of(square), power + dot_of(square * lam)

        new, power = lax.fori_loop(0, 8, advance, (zero, zero), unroll=8)
        new, power = jnp.sum(new), jnp.sum(power)
        ratio = new / norm
        steps.append(new / (power - ratio * new / step))
        norm = new

    def finish(j, carry):
        value = steps[-1] * (residual[j] + ratio * directions[SWEEPS - 2, j])
        for sweep in range(SWEEPS - 1):
            value = value + steps[sweep] * directions[sweep, j]
        part = left_mul(x_bwd, jnp.concatenate([value[:ROW], value[ROW:]], axis=1))
        part = [part[:, :ROW].reshape(RING, 8, ROW), part[:, ROW:].reshape(RING, 8, ROW)]
        part = jnp.concatenate(part, axis=1)
        out[:, pl.ds(pl.multiple_of(16 * j, 16), 16), :] = part.astype(out.dtype)
        return carry

    lax.fori_loop(0, 8, finish, 0, unroll=8)


def term_kernel(place, pair_src, spectra, sources, wanted, z_bwd, y_bwd, terms, shares, queue):
    def body(wants):
        pairs = [spectra[want] for want in wants]
        pairs = [jnp.concatenate([pair, swap_halves(pair)], axis=0) for pair in pairs]
        pairs = [by_half(mm(y_bwd[0], pair) + mm(y_bwd[1], pair)) for pair in pairs]
        pairs = [-right_mul(pair, z_bwd) for pair in pairs]
        for want, pair in zip(wants, pairs):
            terms[want] = (pair * wanted[want].astype(F32)).astype(BF16)
            shares[want] = (pair * sources[want].astype(F32)).astype(BF16)

    for_each_solved(place, pair_src, queue, body)


def pack_terms_kernel(found, terms, *outs):
    for want in range(16):
        at = found[want] - 16

        @pl.when(at >= 0)
        def _():
            for lane, out in enumerate(outs):

                @pl.when(jnp.logical_and(at >= lane * CAP, at < lane * CAP + CAP))
                def _():
                    out[at - lane * CAP] = terms[want]


def add_terms_kernel(sent, found, terms, *refs):
    near, before, (mine, partner, held) = refs[:3], refs[3:-3], refs[-3:]
    mine[...] = before[0][...] if before else jnp.zeros((8, ROW, ROW), F32)
    held[...] = before[1][...].astype(F32) if before else jnp.zeros((8, ROW, ROW), F32)

    def add(row, term):
        @pl.when(row < 8)
        def _():
            mine[row] = mine[row] + term[...].astype(F32)

        @pl.when(row >= 8)
        def _():
            held[row - 8] = held[row - 8] + term[...].astype(F32)

    for want in range(16):
        at = found[want]

        @pl.when(jnp.logical_and(at >= 0, at < 16))
        def _():
            add(at, terms.at[want])

    for lane in range(3):
        for n in range(CAP):
            row = sent[lane * CAP + n]

            @pl.when(row >= 0)
            def _():
                add(row, near[lane].at[n])

    partner[...] = held[...].astype(BF16)


def target_kernel(place, pair_src, pair_tgt, shares, rows, held):
    z, x = place[0], place[1]
    quad = lax.shift_right_logical(z, 2)
    for p in range(4):
        z_own, _ = want_of(pair_src, z, x, 4 * quad + p)
        ahead = lax.bitwise_and(z - z_own, 3)
        relay = ring(z_own + jnp.where(ahead == 3, -1, jnp.where(ahead == 2, far_step(z_own), ahead)))
        held[p] = shares[4 * lax.shift_right_logical(relay, 2) + p].astype(F32)
    for p in range(4):
        same = jnp.zeros((ROW, ROW), F32)
        for other in range(4):
            hit = pair_tgt[p // 2, p % 2] == pair_tgt[other // 2, other % 2]
            same = same + jnp.where(hit, held[other], 0.0)
        rows[p] = same.astype(BF16)


def hand_over(packets, sign):
    moves = (lambda z: 1, lambda z: -1, far_step_of)
    return tuple(
        lax.ppermute(
            packet,
            "band",
            [(2 * z + x, 2 * ((z + sign * move(z)) % RING) + x) for z in range(RING) for x in range(2)],
        )
        for packet, move in zip(packets, moves)
    )


def far_step_of(z):
    return -2 if z % 2 else 2


def across(value):
    return lax.ppermute(value, "band", [(i, i ^ 1) for i in range(32)])


def along_ring(value):
    groups = [[8 * quad + member for quad in range(4)] for member in range(8)]
    return lax.all_to_all(value, "band", 0, 0, axis_index_groups=groups, tiled=True)


def rounds_of(pair_src):
    band = jnp.arange(pair_src.shape[1], dtype=jnp.int32) // 2
    z, x = band // 2, band % 2
    z_own = pair_src // 8
    key = (z_own * 8 + (z % 4) * 2 + x).reshape(-1)
    moves = ((z_own - z) % 4 != 0).astype(jnp.int32).reshape(-1)
    shared = moves * jnp.sum((key[:, None] == key[None, :]).astype(jnp.int32), axis=1)
    return jnp.maximum(1, (jnp.max(shared) + CAP - 1) // CAP)


def per_device(targets, sources, pair_tgt, pair_src):
    table = {name: jnp.asarray(value) for name, value in tables().items()}
    band = lax.axis_index("band")
    sixteen = struct((16, ROW, ROW), BF16)
    packets = [struct((CAP, ROW, ROW), BF16)] * 3

    def place_in(turn):
        turn = jnp.asarray(turn, jnp.int32)
        return jnp.stack([band // 2, band % 2, turn]).astype(jnp.int32)

    def sent_in(turn):
        return smem_call(sent_kernel, 3 * CAP, place_in(turn), pair_src)

    def found_in(turn):
        return smem_call(found_kernel, 16, place_in(turn), pair_src)

    own, ids = lax.optimization_barrier((sources.reshape(8, ROW, ROW), pair_tgt.reshape(4)))
    other = across(own)
    wanted = targets[ids].reshape(4, ROW, ROW)
    wanted = along_ring(jnp.concatenate([wanted] * 4, axis=0))

    def pack_rows_in(sent):
        return vmem_call(pack_rows_kernel, packets, (sent, own, other), scalars=1)

    def deliver(near, found, before):
        operands = (found, own, other) + near + before
        return vmem_call(place_rows_kernel, [sixteen], operands, scalars=1)[0]

    def deliver_in(turn, before):
        return deliver(hand_over(pack_rows_in(sent_in(turn)), 1), found_in(turn), (before,))

    sent, found = sent_in(0), found_in(0)
    near = hand_over(pack_rows_in(sent), 1)
    first, wants = lax.optimization_barrier((near[0], pair_src))
    rounds = rounds_of(wants)
    rows = lax.fori_loop(1, rounds, deliver_in, deliver((first,) + near[1:], found, ()))
    where = (place_in(0), pair_src)
    (spectra,) = vmem_call(
        density_kernel,
        [sixteen],
        where + (rows, wanted, table["z_fwd"], table["y_fwd"]),
        scalars=2,
        scratch=[pltpu.SMEM((16,), jnp.int32)],
    )
    slabs = lax.all_to_all(spectra, "dom", 0, 0, tiled=True)
    (solved,) = vmem_call(
        solve_kernel,
        [sixteen],
        (slabs, table["spectrum"], table["x_fwd"], table["x_bwd"]),
        scratch=[pltpu.VMEM((8, 256, ROW), F32), pltpu.VMEM((SWEEPS - 1, 8, 256, ROW), F32)],
    )
    back = lax.all_to_all(solved, "dom", 0, 0, tiled=True)
    terms, shares = vmem_call(
        term_kernel,
        [sixteen, sixteen],
        where + (back, rows, wanted, table["z_bwd"], table["y_bwd"]),
        scalars=2,
        scratch=[pltpu.SMEM((16,), jnp.int32)],
    )

    def give_back(found):
        return hand_over(vmem_call(pack_terms_kernel, packets, (found, terms), scalars=1), -1)

    def collect(sent, found, near, before):
        outs = [struct((8, ROW, ROW), F32), struct((8, ROW, ROW), BF16)]
        operands = (sent, found, terms) + near + before
        scratch = [pltpu.VMEM((8, ROW, ROW), F32)]
        return vmem_call(add_terms_kernel, outs, operands, scalars=2, scratch=scratch)

    def collect_in(turn, before):
        found = found_in(turn)
        return collect(sent_in(turn), found, give_back(found), tuple(before))

    near = give_back(found)
    shares = along_ring(shares)
    mine, partner = lax.fori_loop(1, rounds, collect_in, collect(sent, found, near, ()))
    (target_rows,) = vmem_call(
        target_kernel,
        [struct((4, ROW, ROW), BF16)],
        where + (pair_tgt, shares),
        scalars=3,
        scratch=[pltpu.VMEM((4, ROW, ROW), F32)],
    )
    flat = target_rows.reshape(4, targets.shape[1])
    slots = jnp.arange(targets.shape[0], dtype=jnp.int32)[:, None]
    summed = jnp.zeros(targets.shape, BF16)
    for p in range(4):
        summed = jnp.where(slots == ids[p], flat[p][None, :], summed)
    partner, summed = lax.optimization_barrier((across(partner), summed))
    owned = (mine + partner.astype(F32)).astype(BF16).reshape(sources.shape)
    return summed, owned


def solution(mesh):
    return jax.shard_map(
        per_device,
        mesh=mesh,
        in_specs=(P("band", "dom"), P(None, "band", "dom"), P(None, "band"), P()),
        out_specs=(P("band", "dom"), P(None, "band", "dom")),
        check_vma=False,
    )
```

```python
import numpy as np
import jax
import jax.numpy as jnp
from jax import lax
from jax.experimental import pallas as pl
from jax.experimental.pallas import tpu as pltpu
from jax.sharding import PartitionSpec as P

SIDE = 64
SWEEPS = 8
RING = 16
CAP = 6
LANES = 3
ROW = 128
HALF = 64
VMEM_LIMIT = 48 * 1024 * 1024
F32 = jnp.float32
BF16 = jnp.bfloat16


def eigen_system():
    line = np.zeros((SIDE, SIDE))
    for delta, weight in ((0, 30.0), (1, -16.0), (2, 1.0)):
        for i in range(SIDE - delta):
            line[i, i + delta] = weight / 12.0
            line[i + delta, i] = weight / 12.0
    values, vectors = np.linalg.eigh(line)
    return values, vectors * np.where(vectors[0] < 0, -1.0, 1.0)[None, :]


def halves(matrix):
    high = np.asarray(matrix, np.float32).astype(jnp.bfloat16)
    low = (np.asarray(matrix, np.float64) - high.astype(np.float64)).astype(jnp.bfloat16)
    return np.stack([high, low])


def tables():
    values, v = eigen_system()
    along_z = np.kron(np.eye(2), v)
    even, odd = v[0::2], v[1::2]
    fwd = np.zeros((2, 32, 4, 2, 4, 32))
    bwd = np.zeros((2, 4, 32, 2, 32, 4))
    for x in range(4):
        fwd[0, :, x, 0, x, :] = even[:, 0::2].T
        fwd[0, :, x, 1, x, :] = odd[:, 0::2].T
        fwd[1, :, x, 0, x, :] = odd[:, 1::2].T
        fwd[1, :, x, 1, x, :] = even[:, 1::2].T
        bwd[0, x, :, 0, :, x] = even[:, 0::2]
        bwd[0, x, :, 1, :, x] = even[:, 1::2]
        bwd[1, x, :, 0, :, x] = odd[:, 1::2]
        bwd[1, x, :, 1, :, x] = odd[:, 0::2]
    along_x = np.zeros((2, SIDE, RING, 2, 4))
    for pick in range(2):
        along_x[pick, :, :, pick, :] = v.T.reshape(SIDE, RING, 4)
    rows = np.arange(SIDE).reshape(16, 2, 1, 2, 1)
    spectrum = values[rows] + values.reshape(1, 1, SIDE, 1, 1) + values.reshape(1, 1, 1, 1, SIDE)
    return dict(
        z_fwd=halves(along_z),
        z_bwd=halves(along_z.T),
        y_fwd=halves(fwd.reshape(256, 256)),
        y_bwd=halves(bwd.reshape(256, 256)),
        x_fwd=halves(along_x.reshape(ROW, ROW)),
        x_bwd=halves(along_x.reshape(ROW, ROW).T),
        spectrum=spectrum.reshape(8, 256, ROW).astype(np.float32),
    )


def split(value):
    high = value.astype(BF16)
    return high, (value - high.astype(F32)).astype(BF16)


def mm(left, right):
    return jnp.dot(left, right, preferred_element_type=F32)


def left_mul(table, value):
    high, low = split(value)
    return mm(table[0], high) + mm(table[0], low) + mm(table[1], high)


def right_mul(value, table):
    high, low = split(value)
    return mm(high, table[0]) + mm(low, table[0]) + mm(high, table[1])


def swap_halves(value):
    return jnp.concatenate([value[:, HALF:], value[:, :HALF]], axis=1)


def by_half(both):
    lane = lax.broadcasted_iota(jnp.int32, (ROW, ROW), 1)
    return jnp.where(lane < HALF, both[:ROW], both[ROW:])


def vmem_call(kernel, outs, operands, scalars=0, scratch=()):
    whole = pl.BlockSpec(memory_space=pltpu.VMEM)
    smem = pl.BlockSpec(memory_space=pltpu.SMEM)
    return pl.pallas_call(
        kernel,
        out_shape=outs,
        in_specs=[smem] * scalars + [whole] * (len(operands) - scalars),
        out_specs=[whole] * len(outs),
        scratch_shapes=list(scratch),
        compiler_params=pltpu.CompilerParams(vmem_limit_bytes=VMEM_LIMIT),
    )(*operands)


def smem_call(kernel, size, *operands):
    smem = pl.BlockSpec(memory_space=pltpu.SMEM)
    return pl.pallas_call(
        kernel,
        out_shape=struct((size,), jnp.int32),
        in_specs=[smem] * len(operands),
        out_specs=smem,
    )(*operands)


def struct(shape, dtype):
    return jax.ShapeDtypeStruct(shape, dtype)


def ring(value):
    return lax.bitwise_and(value, RING - 1)


def far_step(z):
    return 2 - 4 * lax.bitwise_and(z, 1)


def steps_of(z):
    return 1, -1, far_step(z)


def want_of(pair_src, z, x, want):
    quad, slot = lax.shift_right_logical(want, 2), lax.bitwise_and(want, 3)
    block = lax.shift_right_logical(slot, 1)
    band = 2 * (4 * quad + lax.bitwise_and(z, 3)) + x
    source = pair_src[block, 2 * band + lax.bitwise_and(slot, 1)]
    z_own = lax.shift_right_logical(source, 3)
    other = lax.bitwise_xor(lax.bitwise_and(lax.shift_right_logical(source, 2), 1), x)
    return z_own, 8 * other + 4 * block + lax.bitwise_and(source, 3)


def wants_of(pair_src, z, x):
    for want in range(16):
        yield (want,) + want_of(pair_src, z, x, jnp.int32(want))


def in_round(hit, count):
    return jnp.logical_and(hit, jnp.logical_and(count >= 0, count < CAP))


def sent_kernel(place, pair_src, sent):
    z, x = place[0], place[1]
    for lane, step in enumerate(steps_of(z)):
        for n in range(CAP):
            sent[lane * CAP + n] = -1
        count = -CAP * place[2]
        for _, z_own, row in wants_of(pair_src, z + step, x):
            hit = z_own == z

            @pl.when(in_round(hit, count))
            def _():
                sent[lane * CAP + count] = row

            count = count + hit.astype(jnp.int32)


def found_kernel(place, pair_src, found):
    z, x, turn = place[0], place[1], place[2]
    counts = [-CAP * turn] * LANES
    for want, z_own, row in wants_of(pair_src, z, x):
        at = jnp.where(jnp.logical_and(z_own == z, turn == 0), row, -1)
        for lane, step in enumerate(steps_of(z)):
            hit = z_own == ring(z - step)
            at = jnp.where(in_round(hit, counts[lane]), 16 + lane * CAP + counts[lane], at)
            counts[lane] = counts[lane] + hit.astype(jnp.int32)
        found[want] = at


def pack_rows_kernel(sent, own, other, *outs):
    for lane, out in enumerate(outs):
        for n in range(CAP):
            row = sent[lane * CAP + n]

            @pl.when(row >= 0)
            def _():
                @pl.when(row < 8)
                def _():
                    out[n] = own[row]

                @pl.when(row >= 8)
                def _():
                    out[n] = other[row - 8]


def place_rows_kernel(found, own, other, *refs):
    out = refs[-1]
    for before in refs[3:-1]:
        out[...] = before[...]
    spans = [(own, 0, 8), (other, 8, 16)]
    spans += [(near, 16 + lane * CAP, 16 + lane * CAP + CAP) for lane, near in enumerate(refs[:3])]
    for want in range(16):
        at = found[want]

        @pl.when(at >= 0)
        def _():
            for rows, first, last in spans:

                @pl.when(jnp.logical_and(at >= first, at < last))
                def _():
                    out[want] = rows[at - first]


def for_each_solved(place, pair_src, queue, body):
    z, x = place[0], place[1]

    def note(want, count):
        z_own, _ = want_of(pair_src, z, x, want)
        near = jnp.logical_or(ring(z - z_own + 1) <= 2, ring(z - z_own) == ring(far_step(z)))

        @pl.when(near)
        def _():
            queue[count] = want

        return count + near.astype(jnp.int32)

    count = lax.fori_loop(0, 16, note, jnp.int32(0))

    def step(turn, carry):
        body((queue[2 * turn], queue[jnp.minimum(2 * turn + 1, count - 1)]))
        return carry

    lax.fori_loop(0, lax.shift_right_logical(count + 1, 1), step, 0)


def density_kernel(place, pair_src, sources, wanted, z_fwd, y_fwd, spectra, queue):
    def body(wants):
        pairs = [sources[want].astype(F32) * wanted[want].astype(F32) for want in wants]
        pairs = [right_mul(pair, z_fwd) for pair in pairs]
        pairs = [jnp.concatenate([pair, swap_halves(pair)], axis=0) for pair in pairs]
        pairs = [by_half(left_mul(y_fwd, pair)).astype(BF16) for pair in pairs]
        for want, pair in zip(wants, pairs):
            spectra[want] = pair

    for_each_solved(place, pair_src, queue, body)


def solve_kernel(slabs, spectrum, x_fwd, x_bwd, out, residual, directions):
    def dot_of(value):
        return jnp.sum(value.reshape(32, 8, ROW), axis=0)

    zero = jnp.zeros((8, ROW), F32)

    def start(j, carry):
        norm, power = carry
        part = slabs[:, pl.ds(pl.multiple_of(16 * j, 16), 16), :].astype(F32)
        part = [part[:, :8].reshape(ROW, ROW), part[:, 8:].reshape(ROW, ROW)]
        part = jnp.concatenate(part, axis=1).astype(BF16)
        value = mm(x_fwd[0], part) + mm(x_fwd[1], part)
        value = jnp.concatenate([value[:, :ROW], value[:, ROW:]], axis=0)
        directions[0, j] = value
        square = value * value
        return norm + dot_of(square), power + dot_of(square * spectrum[j])

    norm, power = lax.fori_loop(0, 8, start, (zero, zero), unroll=4)
    norm, power = jnp.sum(norm), jnp.sum(power)
    steps, ratio = [norm / power], jnp.float32(0.0)
    for sweep in range(SWEEPS - 1):
        step = steps[-1]

        def advance(j, carry, sweep=sweep, step=step, ratio=ratio):
            new, power = carry
            lam = spectrum[j]
            if sweep == 0:
                r = d = directions[0, j]
            else:
                r = residual[j]
                d = r + ratio * directions[sweep - 1, j]
                directions[sweep, j] = d
            r = r - step * (lam * d)
            residual[j] = r
            square = r * r
            return new + dot_of(square), power + dot_of(square * lam)

        new, power = lax.fori_loop(0, 8, advance, (zero, zero), unroll=4)
        new, power = jnp.sum(new), jnp.sum(power)
        ratio = new / norm
        steps.append(new / (power - ratio * new / step))
        norm = new

    def finish(j, carry):
        value = steps[-1] * (residual[j] + ratio * directions[SWEEPS - 2, j])
        for sweep in range(SWEEPS - 1):
            value = value + steps[sweep] * directions[sweep, j]
        part = left_mul(x_bwd, jnp.concatenate([value[:ROW], value[ROW:]], axis=1))
        part = [part[:, :ROW].reshape(RING, 8, ROW), part[:, ROW:].reshape(RING, 8, ROW)]
        part = jnp.concatenate(part, axis=1)
        out[:, pl.ds(pl.multiple_of(16 * j, 16), 16), :] = part.astype(out.dtype)
        return carry

    lax.fori_loop(0, 8, finish, 0, unroll=4)


def term_kernel(place, pair_src, spectra, sources, wanted, z_bwd, y_bwd, terms, shares, queue):
    def body(wants):
        pairs = [spectra[want] for want in wants]
        pairs = [jnp.concatenate([pair, swap_halves(pair)], axis=0) for pair in pairs]
        pairs = [by_half(mm(y_bwd[0], pair) + mm(y_bwd[1], pair)) for pair in pairs]
        pairs = [-right_mul(pair, z_bwd) for pair in pairs]
        for want, pair in zip(wants, pairs):
            terms[want] = (pair * wanted[want].astype(F32)).astype(BF16)
            shares[want] = (pair * sources[want].astype(F32)).astype(BF16)

    for_each_solved(place, pair_src, queue, body)


def pack_terms_kernel(found, terms, *outs):
    for want in range(16):
        at = found[want] - 16

        @pl.when(at >= 0)
        def _():
            for lane, out in enumerate(outs):

                @pl.when(jnp.logical_and(at >= lane * CAP, at < lane * CAP + CAP))
                def _():
                    out[at - lane * CAP] = terms[want]


def add_terms_kernel(sent, found, terms, *refs):
    near, before, (mine, partner, held) = refs[:3], refs[3:-3], refs[-3:]
    mine[...] = before[0][...] if before else jnp.zeros((8, ROW, ROW), F32)
    held[...] = before[1][...].astype(F32) if before else jnp.zeros((8, ROW, ROW), F32)

    def add(row, term):
        @pl.when(row < 8)
        def _():
            mine[row] = mine[row] + term[...].astype(F32)

        @pl.when(row >= 8)
        def _():
            held[row - 8] = held[row - 8] + term[...].astype(F32)

    for want in range(16):
        at = found[want]

        @pl.when(jnp.logical_and(at >= 0, at < 16))
        def _():
            add(at, terms.at[want])

    for lane in range(3):
        for n in range(CAP):
            row = sent[lane * CAP + n]

            @pl.when(row >= 0)
            def _():
                add(row, near[lane].at[n])

    partner[...] = held[...].astype(BF16)


def target_kernel(place, pair_src, pair_tgt, shares, rows, held):
    z, x = place[0], place[1]
    quad = lax.shift_right_logical(z, 2)
    for p in range(4):
        z_own, _ = want_of(pair_src, z, x, 4 * quad + p)
        ahead = lax.bitwise_and(z - z_own, 3)
        relay = ring(z_own + jnp.where(ahead == 3, -1, jnp.where(ahead == 2, far_step(z_own), ahead)))
        held[p] = shares[4 * lax.shift_right_logical(relay, 2) + p].astype(F32)
    for p in range(4):
        same = jnp.zeros((ROW, ROW), F32)
        for other in range(4):
            hit = pair_tgt[p // 2, p % 2] == pair_tgt[other // 2, other % 2]
            same = same + jnp.where(hit, held[other], 0.0)
        rows[p] = same.astype(BF16)


def hand_over(packets, sign):
    moves = (lambda z: 1, lambda z: -1, far_step_of)
    return tuple(
        lax.ppermute(
            packet,
            "band",
            [(2 * z + x, 2 * ((z + sign * move(z)) % RING) + x) for z in range(RING) for x in range(2)],
        )
        for packet, move in zip(packets, moves)
    )


def far_step_of(z):
    return -2 if z % 2 else 2


def across(value):
    return lax.ppermute(value, "band", [(i, i ^ 1) for i in range(32)])


def along_ring(value):
    groups = [[8 * quad + member for quad in range(4)] for member in range(8)]
    return lax.all_to_all(value, "band", 0, 0, axis_index_groups=groups, tiled=True)


def rounds_of(pair_src):
    band = jnp.arange(pair_src.shape[1], dtype=jnp.int32) // 2
    z, x = band // 2, band % 2
    z_own = pair_src // 8
    key = (z_own * 8 + (z % 4) * 2 + x).reshape(-1)
    moves = ((z_own - z) % 4 != 0).astype(jnp.int32).reshape(-1)
    shared = moves * jnp.sum((key[:, None] == key[None, :]).astype(jnp.int32), axis=1)
    return jnp.maximum(1, (jnp.max(shared) + CAP - 1) // CAP)


def per_device(targets, sources, pair_tgt, pair_src):
    table = {name: jnp.asarray(value) for name, value in tables().items()}
    band = lax.axis_index("band")
    sixteen = struct((16, ROW, ROW), BF16)
    packets = [struct((CAP, ROW, ROW), BF16)] * 3

    def place_in(turn):
        turn = jnp.asarray(turn, jnp.int32)
        return jnp.stack([band // 2, band % 2, turn]).astype(jnp.int32)

    def sent_in(turn):
        return smem_call(sent_kernel, 3 * CAP, place_in(turn), pair_src)

    def found_in(turn):
        return smem_call(found_kernel, 16, place_in(turn), pair_src)

    own, ids = lax.optimization_barrier((sources.reshape(8, ROW, ROW), pair_tgt.reshape(4)))
    other = across(own)
    wanted = targets[ids].reshape(4, ROW, ROW)
    wanted = along_ring(jnp.concatenate([wanted] * 4, axis=0))

    def pack_rows_in(sent):
        return vmem_call(pack_rows_kernel, packets, (sent, own, other), scalars=1)

    def deliver(near, found, before):
        operands = (found, own, other) + near + before
        return vmem_call(place_rows_kernel, [sixteen], operands, scalars=1)[0]

    def deliver_in(turn, before):
        return deliver(hand_over(pack_rows_in(sent_in(turn)), 1), found_in(turn), (before,))

    sent, found = sent_in(0), found_in(0)
    near = hand_over(pack_rows_in(sent), 1)
    first, wants = lax.optimization_barrier((near[0], pair_src))
    rounds = rounds_of(wants)
    rows = lax.fori_loop(1, rounds, deliver_in, deliver((first,) + near[1:], found, ()))
    where = (place_in(0), pair_src)
    (spectra,) = vmem_call(
        density_kernel,
        [sixteen],
        where + (rows, wanted, table["z_fwd"], table["y_fwd"]),
        scalars=2,
        scratch=[pltpu.SMEM((16,), jnp.int32)],
    )
    slabs = lax.all_to_all(spectra, "dom", 0, 0, tiled=True)
    (solved,) = vmem_call(
        solve_kernel,
        [sixteen],
        (slabs, table["spectrum"], table["x_fwd"], table["x_bwd"]),
        scratch=[pltpu.VMEM((8, 256, ROW), F32), pltpu.VMEM((SWEEPS - 1, 8, 256, ROW), F32)],
    )
    back = lax.all_to_all(solved, "dom", 0, 0, tiled=True)
    terms, shares = vmem_call(
        term_kernel,
        [sixteen, sixteen],
        where + (back, rows, wanted, table["z_bwd"], table["y_bwd"]),
        scalars=2,
        scratch=[pltpu.SMEM((16,), jnp.int32)],
    )

    def pack_terms_in(found):
        return vmem_call(pack_terms_kernel, packets, (found, terms), scalars=1)

    def collect(sent, found, near, before):
        outs = [struct((8, ROW, ROW), F32), struct((8, ROW, ROW), BF16)]
        operands = (sent, found, terms) + near + before
        scratch = [pltpu.VMEM((8, ROW, ROW), F32)]
        return vmem_call(add_terms_kernel, outs, operands, scalars=2, scratch=scratch)

    def collect_in(turn, before):
        found = found_in(turn)
        return collect(sent_in(turn), found, hand_over(pack_terms_in(found), -1), tuple(before))

    packed, shares = lax.optimization_barrier((pack_terms_in(found), shares))
    near = hand_over(packed, -1)
    shares = along_ring(shares)
    mine, partner = lax.fori_loop(1, rounds, collect_in, collect(sent, found, near, ()))
    (target_rows,) = vmem_call(
        target_kernel,
        [struct((4, ROW, ROW), BF16)],
        where + (pair_tgt, shares),
        scalars=3,
        scratch=[pltpu.VMEM((4, ROW, ROW), F32)],
    )
    flat = target_rows.reshape(4, targets.shape[1])
    slots = jnp.arange(targets.shape[0], dtype=jnp.int32)[:, None]
    summed = jnp.zeros(targets.shape, BF16)
    for p in range(4):
        summed = jnp.where(slots == ids[p], flat[p][None, :], summed)
    partner, summed = lax.optimization_barrier((across(partner), summed))
    owned = (mine + partner.astype(F32)).astype(BF16).reshape(sources.shape)
    return summed, owned


def solution(mesh):
    return jax.shard_map(
        per_device,
        mesh=mesh,
        in_specs=(P("band", "dom"), P(None, "band", "dom"), P(None, "band"), P()),
        out_specs=(P("band", "dom"), P(None, "band", "dom")),
        check_vma=False,
    )
```
